32 devices in a mesh: groups: 2 (over y), dp: 4 (over z), mp: 2 (over x), section: 2 (over core).
Axes of the slice: x: 2, y: 2, z: 4, core: 2. Of those that a mesh axis runs over, the one named last changes fastest.
Arguments:
- online_obs: bfloat16 [64, 192, 2048], P('dp', 'groups', 'mp'), parts along dimension 1, may hold values from -6 to 6
- offline_obs: bfloat16 [64, 64, 2048], P(('groups', 'dp'), None, 'mp'), parts along dimension 0, may hold values from -6 to 6
- online_rewards: float32 [64, 192], P('dp', 'groups'), parts along dimension 1, may hold values from -6 to 6
- offline_rewards: float32 [64, 64], P(('groups', 'dp')), parts along dimension 0, may hold values from -6 to 6
- online_behaviour: float32 [64, 192], P('dp', 'groups'), parts along dimension 1, may hold values from -4.5 to -1.5
- offline_behaviour: float32 [64, 64], P(('groups', 'dp')), parts along dimension 0, may hold values from -4.5 to -1.5
- online_actions: int32 [64, 192], P('dp', 'groups'), parts along dimension 1, may hold values from 0 to 17
- offline_actions: int32 [64, 64], P(('groups', 'dp')), parts along dimension 0, may hold values from 0 to 17
- online_done: int32 [64, 192], P('dp', 'groups'), parts along dimension 1, may hold values 0 or 1
- offline_done: int32 [64, 64], P(('groups', 'dp')), parts along dimension 0, may hold values 0 or 1
- online_lengths: int32 [192], P(('groups', 'dp')), parts along dimension 0, may hold values from 16 to 64, as said below
- offline_lengths: int32 [64], P(('groups', 'dp')), parts along dimension 0, may hold values from 16 to 64, as said below
- torso_weights: bfloat16 [2, 2048, 2048], P('section', None, 'mp'), may hold values from -0.125 to 0.125
- value_head: bfloat16 [2048], P('mp'), may hold values from -0.125 to 0.125
- policy_head: bfloat16 [2048, 18], P('mp'), may hold values from -0.125 to 0.125
Outputs:
- torso_grads: float32 [4, 2048, 2048], P(('groups', 'section'), None, 'mp'), parts along dimension 0
The draws below stay inside these ranges and needn't reach their ends.
There are 2 independent parts, one for each index of `groups`. The reference program is written for one: setup_inputs(seed, part) draws one part's arguments, and reference() takes and returns one part's arrays. A program takes and returns all parts, laid end to end along the dimension named above; an argument that names none is the same for every part. Nothing has to cross between parts.
Inputs may be any that keep to these rules, and one draw needn't show every extreme that they name: `online_lengths`: each array has a trajectory of full length 64. `offline_lengths`: each array has a trajectory of full length 64.
All inputs are finite; a program needn't handle non-finite values. No bound on the sum of `online_done` or of `offline_done` on one device may be relied on, other than what follows from the above.
Results may differ from the reference program's by a relative error of at most 0.003.
Values may be sent and summed in bfloat16 or wider, within the bound.
No kernel may reach another device: no remote copies, remote signals or barrier semaphores. Data moves between devices by JAX's collectives and lax.ppermute only.
A program may use at most 128 MiB of HBM per device.

```python
import math
import jax
import jax.numpy as jnp
from jax import lax

D = 2048
H = 2048
A = 18
L = 64
S_ON = 96
S_OFF = 32


def draw_online_lengths(key, part):
    key = jax.random.fold_in(key, 11)
    sequence_length = jax.random.randint(key, (S_ON,), L // 4, L + 1)
    return sequence_length.at[0].set(L).astype(jnp.int32)


def draw_offline_lengths(key, part):
    key = jax.random.fold_in(key, 12)
    sequence_length = jax.random.randint(key, (S_OFF,), L // 4, L + 1)
    return sequence_length.at[0].set(L).astype(jnp.int32)


def place_ends(result, rng, low, high):
    longest = result.shape.index(max(result.shape))
    spots = []
    for shift in (0, 1):
        where = [jax.random.randint(jax.random.fold_in(rng, axis), (), 0, length) for axis, length in enumerate(result.shape)]
        where[longest] = (where[longest] + shift) % result.shape[longest]
        spots.append(tuple(where))
    return result.at[spots[0]].set(low).at[spots[1]].set(high)


def shard_levels(stream_key, extent, shards, smallest, high):
    level, own = 1.0, jax.random.fold_in(stream_key, 6)
    for axis_at, shards_of in shards:
        heights = jnp.exp(jax.random.uniform(jax.random.fold_in(own, axis_at), (shards_of,), jnp.float32, smallest / len(shards), high / len(shards)))
        level = level * jnp.repeat(heights, extent[axis_at] // shards_of).reshape([-1 if axis == axis_at else 1 for axis in range(len(extent))])
    return level


def scatter_about(rng, dims, spread, reach, shards=(), kind=jnp.bfloat16):
    result = jax.random.normal(rng, dims, jnp.float32) * spread
    if len(shards) > 0:
        result = shard_levels(rng, dims, shards, -0.22, 0.18) * result
    return jnp.clip(result, min=-reach, max=reach).astype(kind)


def setup_inputs(seed: int = 0, part: int = 0) -> dict:
    keys = jax.random.split(jax.random.key(seed), 16)
    part_splits = jax.random.split(jax.random.fold_in(keys[15], part), 16)
    online_obs = scatter_about(part_splits[0], (L, S_ON, D), 1.0, 6.0, ((0, 4), (2, 2)))
    offline_obs = scatter_about(part_splits[1], (S_OFF, L, D), 1.0, 6.0, ((0, 4), (2, 2)))
    online_rewards = scatter_about(part_splits[2], (L, S_ON), 1.0, 6.0, ((0, 4),), jnp.float32)
    offline_rewards = scatter_about(part_splits[3], (S_OFF, L), 1.0, 6.0, ((0, 4),), jnp.float32)
    online_behaviour = jnp.clip(-4.5 + 3.0 * jax.random.uniform(part_splits[4], (L, S_ON), jnp.float32) ** shard_levels(part_splits[4], (L, S_ON), ((0, 4),), -0.2, 0.2), -4.5, -1.5)
    offline_behaviour = jnp.clip(-4.5 + 3.0 * jax.random.uniform(part_splits[5], (S_OFF, L), jnp.float32) ** shard_levels(part_splits[5], (S_OFF, L), ((0, 4),), -0.2, 0.2), -4.5, -1.5)
    online_actions = place_ends(jax.random.randint(part_splits[6], (L, S_ON), 0, A), jax.random.fold_in(part_splits[6], 1), 0, A - 1).astype(jnp.int32)
    offline_actions = place_ends(jax.random.randint(part_splits[7], (S_OFF, L), 0, A), jax.random.fold_in(part_splits[7], 1), 0, A - 1).astype(jnp.int32)
    online_done = place_ends((jax.random.randint(part_splits[8], (L, S_ON), 0, 32) < 1).astype(jnp.int32), jax.random.fold_in(part_splits[8], 1), 0, 1)
    offline_done = place_ends((jax.random.randint(part_splits[9], (S_OFF, L), 0, 32) < 1).astype(jnp.int32), jax.random.fold_in(part_splits[9], 1), 0, 1)
    online_lengths = draw_online_lengths(jax.random.fold_in(jax.random.fold_in(keys[15], part), 71), part)
    offline_lengths = draw_offline_lengths(jax.random.fold_in(jax.random.fold_in(keys[15], part), 71), part)
    torso_weights = scatter_about(keys[12], (2, D, H), D ** -0.5, 0.125, ((0, 2), (2, 2)))
    value_head = scatter_about(keys[13], (H,), H ** -0.5, 0.125, ((0, 2),))
    policy_head = scatter_about(keys[14], (H, A), H ** -0.5, 0.125, ((0, 2),))
    return dict(online_obs=online_obs, offline_obs=offline_obs, online_rewards=online_rewards, offline_rewards=offline_rewards, online_behaviour=online_behaviour, offline_behaviour=offline_behaviour, online_actions=online_actions, offline_actions=offline_actions, online_done=online_done, offline_done=offline_done, online_lengths=online_lengths, offline_lengths=offline_lengths, torso_weights=torso_weights, value_head=value_head, policy_head=policy_head)


DISCOUNT_RATE = 0.99
TRACE_LAMBDA = 0.95

def silu_slope(pre):
    sigma = jax.nn.sigmoid(pre)
    return sigma * (1.0 + pre * (1.0 - sigma))

def importance_trace_terms(value_estimates, policy_logits, reward_rows, behaviour_probs, taken_actions, episode_finished, sequence_length, objective_scale):
    seq_count, step_count = value_estimates.shape
    action_count = policy_logits.shape[0]
    positions = jnp.arange(step_count, dtype=jnp.int32)
    valid_mask = (positions[None, :] < sequence_length[:, None]).astype(jnp.float32)
    zero_column = jnp.zeros((seq_count, 1), jnp.float32)
    valid_next = jnp.concatenate([valid_mask[:, 1:], zero_column], axis=1)
    log_probs = jax.nn.log_softmax(policy_logits, axis=0)
    one_hot = (jnp.arange(action_count, dtype=jnp.int32)[:, None, None] == taken_actions[None]).astype(jnp.float32)
    chosen = lax.optimization_barrier(jnp.sum(one_hot * log_probs, axis=0))
    clip_ratio = jnp.exp(jnp.minimum(chosen - behaviour_probs, 0.0))
    discount = DISCOUNT_RATE * (1.0 - episode_finished.astype(jnp.float32))
    next_value = jnp.concatenate([value_estimates[:, 1:], zero_column], axis=1) * valid_next
    td_error = valid_mask * clip_ratio * (reward_rows + discount * next_value - value_estimates)
    trace_coef = discount * TRACE_LAMBDA * clip_ratio * valid_next

    def backward_step(carried, inputs):
        error_now, coef_now = inputs
        updated = error_now + coef_now * carried
        return (updated, updated)
    final_state, stacked = lax.scan(backward_step, jnp.zeros((seq_count,), jnp.float32), (td_error.T, trace_coef.T), reverse=True)
    correction = stacked.T
    targets = value_estimates + correction
    next_target = jnp.concatenate([targets[:, 1:], zero_column], axis=1) * valid_next
    policy_adv = clip_ratio * (reward_rows + discount * next_target - value_estimates)
    value_gradient = -objective_scale * valid_mask * correction
    logits_gradient = objective_scale * (valid_mask * policy_adv)[None] * (jnp.exp(log_probs) - one_hot)
    return (value_gradient, logits_gradient)

def reference(online_obs, offline_obs, online_rewards, offline_rewards, online_behaviour, offline_behaviour, online_actions, offline_actions, online_done, offline_done, online_lengths, offline_lengths, torso_weights, value_head, policy_head):
    x_online = online_obs.reshape(L * S_ON, D)
    x_offline = offline_obs.reshape(S_OFF * L, D)
    pre_c_on = jnp.dot(x_online, torso_weights[0], preferred_element_type=jnp.float32)
    pre_c_off = jnp.dot(x_offline, torso_weights[0], preferred_element_type=jnp.float32)
    pre_p_on = jnp.dot(x_online, torso_weights[1], preferred_element_type=jnp.float32)
    pre_p_off = jnp.dot(x_offline, torso_weights[1], preferred_element_type=jnp.float32)
    value_on = jnp.dot(jax.nn.silu(pre_c_on).astype(jnp.bfloat16), value_head, preferred_element_type=jnp.float32)
    value_off = jnp.dot(jax.nn.silu(pre_c_off).astype(jnp.bfloat16), value_head, preferred_element_type=jnp.float32)
    logit_on = jnp.dot(jax.nn.silu(pre_p_on).astype(jnp.bfloat16), policy_head, preferred_element_type=jnp.float32)
    logit_off = jnp.dot(jax.nn.silu(pre_p_off).astype(jnp.bfloat16), policy_head, preferred_element_type=jnp.float32)
    value_estimates = jnp.concatenate([value_on.reshape(L, S_ON).T, value_off.reshape(S_OFF, L)], axis=0)
    policy_logits = jnp.concatenate([logit_on.reshape(L, S_ON, A).transpose(2, 1, 0), logit_off.reshape(S_OFF, L, A).transpose(2, 0, 1)], axis=1)
    reward_rows = jnp.concatenate([online_rewards.T, offline_rewards], axis=0)
    behaviour_probs = jnp.concatenate([online_behaviour.T, offline_behaviour], axis=0)
    taken_actions = jnp.concatenate([online_actions.T, offline_actions], axis=0).astype(jnp.int32)
    episode_finished = jnp.concatenate([online_done.T, offline_done], axis=0).astype(jnp.int32)
    sequence_length = jnp.concatenate([online_lengths, offline_lengths], axis=0).astype(jnp.int32)
    objective_scale = math.sqrt(H / ((S_ON + S_OFF) * L))
    value_gradient, logits_gradient = importance_trace_terms(value_estimates, policy_logits, reward_rows, behaviour_probs, taken_actions, episode_finished, sequence_length, objective_scale)
    dv_on = value_gradient[:S_ON].T.reshape(L * S_ON)
    dv_off = value_gradient[S_ON:].reshape(S_OFF * L)
    dl_on = logits_gradient[:, :S_ON].transpose(2, 1, 0).reshape(L * S_ON, A)
    dl_off = logits_gradient[:, S_ON:].transpose(1, 2, 0).reshape(S_OFF * L, A)
    value_w = value_head.astype(jnp.float32)
    policy_w = policy_head.astype(jnp.float32)
    dz_c_on = (dv_on[:, None] * value_w[None, :] * silu_slope(pre_c_on)).astype(jnp.bfloat16)
    dz_c_off = (dv_off[:, None] * value_w[None, :] * silu_slope(pre_c_off)).astype(jnp.bfloat16)
    dz_p_on = (jnp.dot(dl_on, policy_w.T, precision=lax.Precision.HIGHEST) * silu_slope(pre_p_on)).astype(jnp.bfloat16)
    dz_p_off = (jnp.dot(dl_off, policy_w.T, precision=lax.Precision.HIGHEST) * silu_slope(pre_p_off)).astype(jnp.bfloat16)
    grad_critic = jnp.dot(x_online.T, dz_c_on, preferred_element_type=jnp.float32) + jnp.dot(x_offline.T, dz_c_off, preferred_element_type=jnp.float32)
    grad_policy = jnp.dot(x_online.T, dz_p_on, preferred_element_type=jnp.float32) + jnp.dot(x_offline.T, dz_p_off, preferred_element_type=jnp.float32)
    return jnp.stack([grad_critic, grad_policy])
```

```python
import functools
import math

import jax
import jax.numpy as jnp
from jax import lax
from jax.experimental import pallas as pl
from jax.experimental.pallas import tpu as pltpu
from jax.sharding import PartitionSpec as P

DISCOUNT_RATE = 0.99
TRACE_LAMBDA = 0.95


def silu_slope(pre):
    sigma = jax.nn.sigmoid(pre)
    return sigma * (1.0 + pre * (1.0 - sigma))


def importance_trace_terms(
    value_estimates,
    policy_logits,
    reward_rows,
    behaviour_probs,
    taken_actions,
    episode_finished,
    sequence_length,
    objective_scale,
):
    seq_count, step_count = value_estimates.shape
    action_count = policy_logits.shape[0]
    positions = jnp.arange(step_count, dtype=jnp.int32)
    valid_mask = (positions[None, :] < sequence_length[:, None]).astype(jnp.float32)
    zero_column = jnp.zeros((seq_count, 1), jnp.float32)
    valid_next = jnp.concatenate([valid_mask[:, 1:], zero_column], axis=1)
    log_probs = jax.nn.log_softmax(policy_logits, axis=0)
    one_hot = (
        jnp.arange(action_count, dtype=jnp.int32)[:, None, None] == taken_actions[None]
    ).astype(jnp.float32)
    chosen = jnp.sum(one_hot * log_probs, axis=0)
    clip_ratio = jnp.exp(jnp.minimum(chosen - behaviour_probs, 0.0))
    discount = DISCOUNT_RATE * (1.0 - episode_finished.astype(jnp.float32))
    next_value = jnp.concatenate([value_estimates[:, 1:], zero_column], axis=1) * valid_next
    td_error = valid_mask * clip_ratio * (reward_rows + discount * next_value - value_estimates)
    trace_coef = discount * TRACE_LAMBDA * clip_ratio * valid_next

    def backward_step(carried, inputs):
        error_now, coef_now = inputs
        updated = error_now + coef_now * carried
        return (updated, updated)

    final_state, stacked = lax.scan(
        backward_step,
        jnp.zeros((seq_count,), jnp.float32),
        (td_error.T, trace_coef.T),
        reverse=True,
    )
    correction = stacked.T
    targets = value_estimates + correction
    next_target = jnp.concatenate([targets[:, 1:], zero_column], axis=1) * valid_next
    policy_adv = clip_ratio * (reward_rows + discount * next_target - value_estimates)
    value_gradient = -objective_scale * valid_mask * correction
    logits_gradient = (
        objective_scale * (valid_mask * policy_adv)[None] * (jnp.exp(log_probs) - one_hot)
    )
    return (value_gradient, logits_gradient)


def head_terms(hidden, value_w, policy_w):
    logit_part = jnp.einsum("rh,ha->ar", hidden, policy_w, preferred_element_type=jnp.float32)
    value_part = jnp.dot(hidden, value_w, preferred_element_type=jnp.float32)
    return jnp.concatenate([logit_part, value_part[None]], axis=0)


def full_rows(online_part, offline_part):
    return (
        lax.all_gather(online_part, "mp", axis=2, tiled=True),
        lax.all_gather(offline_part, "mp", axis=2, tiled=True),
    )


def general_plan(
    online_obs,
    offline_obs,
    online_rewards,
    offline_rewards,
    online_behaviour,
    offline_behaviour,
    online_actions,
    offline_actions,
    online_done,
    offline_done,
    online_lengths,
    offline_lengths,
    torso_weights,
    value_head,
    policy_head,
):
    owned_online = online_lengths.shape[0]
    owned_offline = offline_obs.shape[0]
    step_count = offline_obs.shape[1]
    action_count = policy_head.shape[1]
    record_stack = jnp.stack(
        [
            online_rewards,
            online_behaviour,
            online_actions.astype(jnp.float32),
            online_done.astype(jnp.float32),
        ]
    )
    records = lax.all_to_all(record_stack, "dp", split_axis=2, concat_axis=1, tiled=True)
    slabs = lax.all_to_all(online_obs, "dp", split_axis=1, concat_axis=0, tiled=True)
    x_online, x_offline = full_rows(slabs, offline_obs)
    feature_count = x_online.shape[2]
    x_online = x_online.reshape(step_count * owned_online, feature_count)
    x_offline = x_offline.reshape(owned_offline * step_count, feature_count)
    weight = torso_weights[0]
    pre_online = jnp.dot(x_online, weight, preferred_element_type=jnp.float32)
    pre_offline = jnp.dot(x_offline, weight, preferred_element_type=jnp.float32)
    hidden_online = jax.nn.silu(pre_online).astype(jnp.bfloat16)
    hidden_offline = jax.nn.silu(pre_offline).astype(jnp.bfloat16)
    is_critic = (lax.axis_index("section") == 0).astype(jnp.float32)
    is_policy = 1.0 - is_critic
    row_keep = jnp.where(jnp.arange(action_count + 1) == action_count, is_critic, is_policy)
    partial_value = jnp.concatenate(
        [
            head_terms(hidden_online, value_head, policy_head),
            head_terms(hidden_offline, value_head, policy_head),
        ],
        axis=1,
    )
    partial_value = partial_value * row_keep[:, None]
    heads = lax.psum(partial_value, ("mp", "section"))
    online_count = step_count * owned_online
    logits_on = (
        heads[:action_count, :online_count]
        .reshape(action_count, step_count, owned_online)
        .transpose(0, 2, 1)
    )
    logits_off = heads[:action_count, online_count:].reshape(
        action_count, owned_offline, step_count
    )
    values_on = heads[action_count, :online_count].reshape(step_count, owned_online).T
    values_off = heads[action_count, online_count:].reshape(owned_offline, step_count)
    record_seq = records.transpose(0, 2, 1)
    value_estimates = jnp.concatenate([values_on, values_off], axis=0)
    policy_logits = jnp.concatenate([logits_on, logits_off], axis=1)
    reward_rows = jnp.concatenate([record_seq[0], offline_rewards], axis=0)
    behaviour_probs = jnp.concatenate([record_seq[1], offline_behaviour], axis=0)
    taken_actions = jnp.concatenate([record_seq[2].astype(jnp.int32), offline_actions], axis=0)
    episode_finished = jnp.concatenate([record_seq[3].astype(jnp.int32), offline_done], axis=0)
    sequence_length = jnp.concatenate([online_lengths, offline_lengths], axis=0)
    total_seqs = online_obs.shape[1] + owned_offline * lax.axis_size("dp")
    hidden_total = value_head.shape[0] * lax.axis_size("mp")
    objective_scale = math.sqrt(hidden_total / (total_seqs * step_count))
    value_gradient, logits_gradient = importance_trace_terms(
        value_estimates,
        policy_logits,
        reward_rows,
        behaviour_probs,
        taken_actions,
        episode_finished,
        sequence_length,
        objective_scale,
    )
    value_gradient = value_gradient * is_critic
    logits_gradient = logits_gradient * is_policy
    dv_on = value_gradient[:owned_online].T.reshape(online_count)
    dv_off = value_gradient[owned_online:].reshape(owned_offline * step_count)
    dl_on = logits_gradient[:, :owned_online].transpose(0, 2, 1).reshape(action_count, online_count)
    dl_off = logits_gradient[:, owned_online:].reshape(action_count, owned_offline * step_count)
    value_w = value_head.astype(jnp.float32)
    policy_w = policy_head.astype(jnp.float32)
    dh_on = dv_on[:, None] * value_w[None, :] + jnp.einsum(
        "ar,ha->rh", dl_on, policy_w, precision=lax.Precision.HIGHEST
    )
    dh_off = dv_off[:, None] * value_w[None, :] + jnp.einsum(
        "ar,ha->rh", dl_off, policy_w, precision=lax.Precision.HIGHEST
    )
    dz_online = (dh_on * silu_slope(pre_online)).astype(jnp.bfloat16)
    dz_offline = (dh_off * silu_slope(pre_offline)).astype(jnp.bfloat16)
    local_grad = jnp.einsum("rd,rh->dh", x_online, dz_online, preferred_element_type=jnp.float32)
    local_grad = local_grad + jnp.einsum(
        "rd,rh->dh", x_offline, dz_offline, preferred_element_type=jnp.float32
    )
    summed = lax.psum(local_grad, "dp")
    return summed[None]


HEAD_ROWS = 24
SPLIT_ROWS = 4 * HEAD_ROWS
COLUMN_BLOCK = 256
GRAD_CHUNKS = 8
LANES = 128
CODE_LIMIT = 32512.0
CODE_TAIL = 16
LOG_TWO = math.log(2.0)
GRAD_LEAD = 3
ONLINE_CHUNKS = 2
VMEM_BYTES = 56 * 1024 * 1024
SWAP = ((0, 1), (1, 0))
TO_CENTER = ((0, 1), (3, 2))
CENTER = ((1, 2), (2, 1))
FROM_CENTER = ((1, 0), (2, 3))


def params():
    return pltpu.CompilerParams(vmem_limit_bytes=VMEM_BYTES)


def cost(flops, nbytes, transcendentals=0):
    return pl.CostEstimate(
        flops=int(flops), bytes_accessed=int(nbytes), transcendentals=int(transcendentals)
    )


def whole(array):
    rank = len(array.shape)
    return pl.BlockSpec(array.shape, lambda *_: (0,) * rank)


def untouched(arrays):
    return [pl.BlockSpec(memory_space=pl.ANY) for _ in arrays]


def forward_body(place, own_ref, other_ref, weight_ref, head_ref, slope_ref, heads_ref):
    groups, width, features = own_ref.shape
    m = place[0]
    own_at = pl.multiple_of(m * features, features)
    other_at = pl.multiple_of((1 - m) * features, features)
    rows = groups * width
    pre = jnp.dot(
        own_ref[...].reshape(rows, features),
        weight_ref[pl.ds(own_at, features), :],
        preferred_element_type=jnp.float32,
    )
    pre = pre + jnp.dot(
        other_ref[...].reshape(rows, features),
        weight_ref[pl.ds(other_at, features), :],
        preferred_element_type=jnp.float32,
    )
    sigma = 1.0 / (1.0 + jnp.exp(-pre))
    slope_ref[...] = sigma * (1.0 + pre * (1.0 - sigma))
    hidden = (pre * sigma).astype(jnp.bfloat16)

    @pl.when(pl.program_id(0) == 0)
    def _():
        heads_ref[...] = jnp.zeros_like(heads_ref)

    for g in range(groups):
        part = lax.dot_general(
            head_ref[...],
            hidden[g * width : (g + 1) * width],
            (((1,), (1,)), ((), ())),
            preferred_element_type=jnp.float32,
        )
        heads_ref[g] += part[:HEAD_ROWS]


def forward(place, own, first_group, other, weight, head):
    groups, width, features = other.shape
    hidden_count = weight.shape[1]
    rows = groups * width
    block = min(COLUMN_BLOCK, hidden_count)
    at = first_group // groups
    return pl.pallas_call(
        forward_body,
        grid_spec=pltpu.PrefetchScalarGridSpec(
            num_scalar_prefetch=1,
            grid=(hidden_count // block,),
            in_specs=[
                pl.BlockSpec((groups, width, features), lambda h, p: (at, 0, 0)),
                pl.BlockSpec((groups, width, features), lambda h, p: (0, 0, 0)),
                pl.BlockSpec((weight.shape[0], block), lambda h, p: (0, h)),
                pl.BlockSpec((head.shape[0], block), lambda h, p: (0, h)),
            ],
            out_specs=[
                pl.BlockSpec((rows, block), lambda h, p: (0, h)),
                pl.BlockSpec((groups, HEAD_ROWS, width), lambda h, p: (0, 0, 0)),
            ],
        ),
        out_shape=[
            jax.ShapeDtypeStruct((rows, hidden_count), jnp.float32),
            jax.ShapeDtypeStruct((groups, HEAD_ROWS, width), jnp.float32),
        ],
        compiler_params=params(),
        cost_estimate=cost(
            4 * rows * features * hidden_count,
            8 * rows * hidden_count,
            rows * hidden_count,
        ),
        name="forward_rows",
    )(place, own, other, weight, head)


def action_terms(parts, actions, behaviour, action_count):
    heads = parts[0] + parts[1] + (parts[2] + parts[3])
    row = lax.broadcasted_iota(jnp.int32, heads.shape, 0)
    is_logit = row < action_count
    logits = jnp.where(is_logit, heads, -1e30)
    shifted = logits - jnp.max(logits, axis=0, keepdims=True)
    log_sum = jnp.log(jnp.sum(jnp.exp(shifted), axis=0, keepdims=True))
    log_probs = shifted - log_sum
    taken = row == actions
    chosen = jnp.sum(jnp.where(taken, log_probs, 0.0), axis=0, keepdims=True)
    rho = jnp.exp(jnp.minimum(chosen - behaviour, 0.0))
    spread = jnp.where(is_logit, jnp.exp(log_probs) - taken.astype(jnp.float32), 0.0)
    return heads[action_count : action_count + 1], rho, spread


def trace_terms(value, rho, reward, discount, length, position, axis, reach, scale):
    size = value.shape[axis]
    valid = (position < length).astype(jnp.float32)
    valid_next = (position + 1 < length).astype(jnp.float32)
    next_value = pltpu.roll(value, size - 1, axis) * valid_next
    correction = valid * rho * (reward + discount * next_value - value)
    coef = discount * TRACE_LAMBDA * rho * valid_next
    shift = 1
    while shift < reach:
        correction = correction + coef * pltpu.roll(correction, size - shift, axis)
        coef = coef * pltpu.roll(coef, size - shift, axis)
        shift *= 2
    targets = value + correction
    next_target = pltpu.roll(targets, size - 1, axis) * valid_next
    advantage = rho * (reward + discount * next_target - value)
    return -scale * valid * correction, scale * (valid * advantage)


def split_terms(logit_weight, value_weight, spread, action_count):
    row = lax.broadcasted_iota(jnp.int32, spread.shape, 0)
    full = jnp.where(row == action_count, value_weight, logit_weight * spread)
    high = full.astype(jnp.bfloat16).astype(jnp.float32)
    rest = full - high
    middle = rest.astype(jnp.bfloat16).astype(jnp.float32)
    low = rest - middle
    return jnp.concatenate([high, middle, low, jnp.zeros_like(full)], axis=0).astype(jnp.bfloat16)


def online_heads_body(action_count, *refs):
    chunks = refs[: 4 * ONLINE_CHUNKS]
    actions, behaviour, reward, done, pack_ref, spread_ref = refs[4 * ONLINE_CHUNKS :]
    steps = actions.shape[0]
    per_chunk = steps // ONLINE_CHUNKS
    for t in range(steps):
        c, g = divmod(t, per_chunk)
        value, rho, spread = action_terms(
            [chunks[4 * c + i][g] for i in range(4)],
            actions[t : t + 1, :],
            behaviour[t : t + 1, :],
            action_count,
        )
        pack_ref[t : t + 1, :] = value
        pack_ref[steps + t : steps + t + 1, :] = rho
        spread_ref[t] = spread
    pack_ref[2 * steps : 3 * steps, :] = reward[...]
    pack_ref[3 * steps : 4 * steps, :] = DISCOUNT_RATE * (1.0 - done[...].astype(jnp.float32))


def online_trace_body(action_count, scale, place, own, one, two, three, length, spread, terms_ref):
    steps = spread.shape[0]
    blocks = (own, one, two, three)

    def field(i):
        return jnp.concatenate([b[i * steps : (i + 1) * steps, :] for b in blocks], axis=0)

    value = field(0)
    position = lax.broadcasted_iota(jnp.int32, value.shape, 0) + place[2] * steps
    value_weight, logit_weight = trace_terms(
        value, field(1), field(2), field(3), length[...], position, 0, value.shape[0], scale
    )
    for t in range(steps):
        terms_ref[t] = split_terms(
            logit_weight[t : t + 1, :], value_weight[t : t + 1, :], spread[t], action_count
        )


def offline_trace_body(
    action_count, step_count, scale, p0, p1, p2, p3, actions, behaviour, reward, done, length, terms_ref
):
    groups = terms_ref.shape[0]
    values, rhos, spreads = [], [], []
    for g in range(groups):
        value, rho, spread = action_terms(
            [p0[g], p1[g], p2[g], p3[g]],
            actions[g : g + 1, :],
            behaviour[g : g + 1, :],
            action_count,
        )
        values.append(value)
        rhos.append(rho)
        spreads.append(spread)
    value = jnp.concatenate(values, axis=0)
    rho = jnp.concatenate(rhos, axis=0)
    position = lax.rem(lax.broadcasted_iota(jnp.int32, value.shape, 1), step_count)
    discount = DISCOUNT_RATE * (1.0 - done[...].astype(jnp.float32))
    value_weight, logit_weight = trace_terms(
        value, rho, reward[...], discount, length[...], position, 1, step_count, scale
    )
    for g in range(groups):
        terms_ref[g] = split_terms(
            logit_weight[g : g + 1, :], value_weight[g : g + 1, :], spreads[g], action_count
        )


def back_body(terms_ref, head_ref, slope_ref, dz_ref):
    groups, _, width = terms_ref.shape
    for g in range(groups):
        rows = slice(g * width, (g + 1) * width)
        dh = lax.dot_general(
            terms_ref[g],
            head_ref[...],
            (((0,), (0,)), ((), ())),
            preferred_element_type=jnp.float32,
        )
        dz_ref[rows, :] = (dh * slope_ref[rows, :]).astype(jnp.bfloat16)


def back(terms, first_group, head, slope):
    rows, hidden_count = slope.shape
    width = terms.shape[2]
    groups = rows // width
    block = min(COLUMN_BLOCK, hidden_count)
    at = first_group // groups
    return pl.pallas_call(
        back_body,
        grid=(hidden_count // block,),
        in_specs=[
            pl.BlockSpec((groups, SPLIT_ROWS, width), lambda h: (at, 0, 0)),
            pl.BlockSpec((SPLIT_ROWS, block), lambda h: (0, h)),
            pl.BlockSpec((rows, block), lambda h: (0, h)),
        ],
        out_specs=pl.BlockSpec((rows, block), lambda h: (0, h)),
        out_shape=jax.ShapeDtypeStruct((rows, hidden_count), jnp.bfloat16),
        compiler_params=params(),
        cost_estimate=cost(2 * rows * SPLIT_ROWS * hidden_count, 6 * rows * hidden_count),
        name="back_rows",
    )(terms, head, slope)


def encode(blocks, message_ref):
    rows = blocks[0].shape[0]
    largest = functools.reduce(jnp.maximum, [jnp.abs(v) for v in blocks])
    largest = jnp.max(jnp.max(largest, axis=0, keepdims=True), axis=1, keepdims=True)
    exponent = jnp.ceil(jnp.log(jnp.maximum(largest, 1e-30)) * (1.0 / LOG_TWO) + 0.01)
    scale = jnp.exp(exponent * -LOG_TWO) * CODE_LIMIT
    for c, v in enumerate(blocks):
        code = jnp.clip(jnp.floor(v * scale + 0.5), -CODE_LIMIT, CODE_LIMIT)
        message_ref[c * rows : (c + 1) * rows, :] = code.astype(jnp.int32).astype(jnp.int16)
    tail = jnp.broadcast_to(exponent, (CODE_TAIL, LANES)).astype(jnp.int32)
    message_ref[len(blocks) * rows :, :] = tail.astype(jnp.int16)


def decode(message_ref, count):
    rows = (message_ref.shape[0] - CODE_TAIL) // count
    exponent = message_ref[count * rows :, :].astype(jnp.int32).astype(jnp.float32)[:1, :]
    step = jnp.exp(exponent * LOG_TWO) * (1.0 / CODE_LIMIT)
    return [
        message_ref[c * rows : (c + 1) * rows, :].astype(jnp.int32).astype(jnp.float32) * step
        for c in range(count)
    ]


def message_shape(rows, columns):
    return jax.ShapeDtypeStruct((rows * (columns // LANES) + CODE_TAIL, LANES), jnp.int16)


def grad_body(count, deps, *refs):
    xs, dzs = refs[:count], refs[count : 2 * count]
    message_ref, sums_ref = refs[2 * count + deps :]
    h = pl.program_id(0)
    total = None
    for x, dz in zip(xs, dzs):
        part = lax.dot_general(
            x[...], dz[...], (((0,), (0,)), ((), ())), preferred_element_type=jnp.float32
        )
        total = part if total is None else total + part
    sums_ref[h] = total

    @pl.when(h == pl.num_programs(0) - 1)
    def _():
        blocks = []
        for i in range(sums_ref.shape[0]):
            for c in range(sums_ref.shape[2] // LANES):
                blocks.append(sums_ref[i, :, c * LANES : (c + 1) * LANES])
        encode(blocks, message_ref)


def grad_chunk(pieces, column, columns, deps):
    hidden_count = pieces[0][2].shape[1]
    block = min(COLUMN_BLOCK, hidden_count)
    rows = sum(dz.shape[0] for _, _, dz in pieces)
    message = message_shape(columns, hidden_count)

    def x_spec(at, dz):
        return pl.BlockSpec((dz.shape[0], columns), lambda h: (at, column))

    return pl.pallas_call(
        functools.partial(grad_body, len(pieces), len(deps)),
        grid=(hidden_count // block,),
        in_specs=[x_spec(at, dz) for _, at, dz in pieces]
        + [pl.BlockSpec((dz.shape[0], block), lambda h: (0, h)) for _, _, dz in pieces]
        + untouched(deps),
        out_specs=whole(message),
        out_shape=message,
        scratch_shapes=[pltpu.VMEM((hidden_count // block, columns, block), jnp.float32)],
        compiler_params=params(),
        cost_estimate=cost(2 * rows * columns * hidden_count, 2 * rows * hidden_count),
        name="grad_chunk",
    )(*[x for x, _, _ in pieces], *[dz for _, _, dz in pieces], *deps)


def add_body(count, a, b, *refs):
    encode([u + v for u, v in zip(decode(a, count), decode(b, count))], refs[-1])


def add_chunk(a, b, count, deps):
    return pl.pallas_call(
        functools.partial(add_body, count),
        grid=(1,),
        in_specs=[whole(a), whole(b)] + untouched(deps),
        out_specs=whole(a),
        out_shape=jax.ShapeDtypeStruct(a.shape, a.dtype),
        compiler_params=params(),
        cost_estimate=cost(a.size, 6 * a.size),
        name="add_chunk",
    )(a, b, *deps)


def place_body(count, place, total, received, *refs):
    out = refs[-1]
    at_end = place[1] == 1

    def write(message):
        for c, v in enumerate(decode(message, count)):
            out[:, c * LANES : (c + 1) * LANES] = v

    @pl.when(at_end)
    def _():
        write(received)

    @pl.when(jnp.logical_not(at_end))
    def _():
        write(total)


def place_chunk(place, total, received, result, of_own, index, rows, shape, deps):
    row_count, hidden_count = shape
    per_half = row_count // (2 * rows)

    def at(i, p):
        half = p[0] if of_own else 1 - p[0]
        return (half * per_half + index, 0)

    earlier = [] if result is None else [result]
    return pl.pallas_call(
        functools.partial(place_body, hidden_count // LANES),
        grid_spec=pltpu.PrefetchScalarGridSpec(
            num_scalar_prefetch=1,
            grid=(1,),
            in_specs=[
                pl.BlockSpec(total.shape, lambda i, p: (0, 0)),
                pl.BlockSpec(total.shape, lambda i, p: (0, 0)),
            ]
            + untouched(earlier + deps),
            out_specs=pl.BlockSpec((rows, hidden_count), at),
        ),
        out_shape=jax.ShapeDtypeStruct(shape, jnp.float32),
        input_output_aliases={3: 0} if earlier else {},
        compiler_params=params(),
        cost_estimate=cost(total.size, 8 * total.size),
        name="place_chunk",
    )(place, total, received, *earlier, *deps)


def other_half(obs, first, count, section):
    half = count // 2
    mine = lax.dynamic_slice_in_dim(obs, first + section * half, half, axis=0)
    got = lax.ppermute(mine, "mp", SWAP)
    rest = lax.ppermute(got, "section", SWAP)
    return jnp.where(
        section == 0,
        jnp.concatenate([got, rest], axis=0),
        jnp.concatenate([rest, got], axis=0),
    )


def from_chip_pair(part):
    received = [part]
    for flip in (1, 2, 3):
        pairs = [(i, i ^ flip) for i in range(4)]
        received.append(lax.ppermute(part, ("mp", "section"), pairs))
    return received


def line_plan(
    online_obs,
    offline_obs,
    online_rewards,
    offline_rewards,
    online_behaviour,
    offline_behaviour,
    online_actions,
    offline_actions,
    online_done,
    offline_done,
    online_lengths,
    offline_lengths,
    torso_weights,
    value_head,
    policy_head,
):
    section = lax.axis_index("section")
    m = lax.axis_index("mp")
    z = lax.axis_index("dp")
    dp = lax.axis_size("dp")
    steps, online_count, features = online_obs.shape
    offline_count, step_count, _ = offline_obs.shape
    action_count = policy_head.shape[1]
    hidden_count = value_head.shape[0]
    place = jnp.stack([m, ((z == 0) | (z == dp - 1)).astype(jnp.int32), z]).astype(jnp.int32)
    weight = torso_weights[0]
    scale = math.sqrt(
        hidden_count
        * lax.axis_size("mp")
        / ((online_count + offline_count * dp) * step_count)
    )

    offline_groups = offline_count // 2
    offline_rows = offline_obs.reshape(offline_groups, 2 * step_count, features)
    per_chunk = steps // ONLINE_CHUNKS
    others = [
        other_half(online_obs, c * per_chunk, per_chunk, section) for c in range(ONLINE_CHUNKS)
    ]
    other_offline = other_half(offline_rows, 0, offline_groups, section)

    policy_rows = jnp.where(section == 1, policy_head.T, 0)
    value_row = jnp.where(section == 0, value_head[None], 0)
    head = jnp.concatenate([policy_rows, value_row], axis=0).astype(jnp.bfloat16)
    head = jnp.pad(head, ((0, HEAD_ROWS - action_count - 1), (0, 0)))
    forward_head = jnp.pad(head, ((0, 32 - HEAD_ROWS), (0, 0)))
    back_head = jnp.concatenate([head, head, head, jnp.zeros_like(head)], axis=0)

    owned = online_lengths.shape[0]
    length_row = lax.dynamic_update_slice(
        jnp.zeros((online_count,), jnp.float32), online_lengths.astype(jnp.float32), (z * owned,)
    )
    for flip in (1, 2):
        length_row = length_row + lax.ppermute(
            length_row, "dp", [(i, i ^ flip) for i in range(dp)]
        )
    length_row = length_row.astype(jnp.int32)[None]
    lanes = (offline_groups, 2 * step_count)
    offline_length = jnp.broadcast_to(
        offline_lengths[:, None], (offline_count, step_count)
    ).reshape(lanes)

    slopes, online_parts = [], []
    for c in range(ONLINE_CHUNKS):
        slope, part = forward(
            place, online_obs, c * per_chunk, others[c], weight, forward_head
        )
        slopes.append(slope)
        online_parts += from_chip_pair(part)
    offline_slope, offline_part = forward(
        place, offline_rows, 0, other_offline, weight, forward_head
    )
    offline_parts = from_chip_pair(offline_part)

    pack, spread = pl.pallas_call(
        functools.partial(online_heads_body, action_count),
        out_shape=[
            jax.ShapeDtypeStruct((4 * steps, online_count), jnp.float32),
            jax.ShapeDtypeStruct((steps, HEAD_ROWS, online_count), jnp.float32),
        ],
        compiler_params=params(),
        name="online_heads",
    )(*online_parts, online_actions, online_behaviour, online_rewards, online_done)
    later = [
        lax.ppermute(pack, "dp", [(i, i - hop) for i in range(hop, dp)]) for hop in range(1, dp)
    ]
    smem = pl.BlockSpec(memory_space=pltpu.SMEM)
    vmem = pl.BlockSpec(memory_space=pltpu.VMEM)
    online_terms = pl.pallas_call(
        functools.partial(online_trace_body, action_count, scale),
        in_specs=[smem] + [vmem] * 6,
        out_specs=vmem,
        out_shape=jax.ShapeDtypeStruct((steps, SPLIT_ROWS, online_count), jnp.bfloat16),
        compiler_params=params(),
        name="online_trace",
    )(place, pack, *later, length_row, spread)
    pieces = []
    for c in range(ONLINE_CHUNKS):
        pieces.append(back(online_terms, c * per_chunk, back_head, slopes[c]))

    offline_terms = pl.pallas_call(
        functools.partial(offline_trace_body, action_count, step_count, scale),
        out_shape=jax.ShapeDtypeStruct(
            (offline_groups, SPLIT_ROWS, 2 * step_count), jnp.bfloat16
        ),
        compiler_params=params(),
        name="offline_trace",
    )(
        *offline_parts,
        offline_actions.reshape(lanes),
        offline_behaviour.reshape(lanes),
        offline_rewards.reshape(lanes),
        offline_done.reshape(lanes),
        offline_length,
    )
    pieces.append(back(offline_terms, 0, back_head, offline_slope))

    own_rows = online_obs.reshape(steps * online_count, features)
    own_offline = offline_rows.reshape(-1, features)
    own_x = [(own_rows, c) for c in range(ONLINE_CHUNKS)] + [(own_offline, 0)]
    other_x = [(o.reshape(-1, features), 0) for o in others + [other_offline]]
    columns = 2 * features // GRAD_CHUNKS
    per_half = GRAD_CHUNKS // 2
    lane_blocks = hidden_count // LANES

    def local_grad(k, deps):
        source = own_x if k < per_half else other_x
        return grad_chunk(
            [(x, at, dz) for (x, at), dz in zip(source, pieces)], k % per_half, columns, deps
        )

    inward, partial, across, total, outward = {}, {}, {}, {}, {}
    own_grad = {}
    result = None
    for k in range(GRAD_LEAD):
        own_grad[k] = local_grad(k, [])
        inward[k] = lax.ppermute(own_grad[k], "dp", TO_CENTER)
    for k in range(GRAD_CHUNKS + 2):
        if k < GRAD_CHUNKS:
            partial[k] = add_chunk(own_grad[k], inward[k], lane_blocks, [])
            across[k] = lax.ppermute(partial[k], "dp", CENTER)
        j = k - 1
        if 0 <= j < GRAD_CHUNKS:
            deps = [partial[k]] if k < GRAD_CHUNKS else []
            total[j] = add_chunk(partial[j], across[j], lane_blocks, deps)
            outward[j] = lax.ppermute(total[j], "dp", FROM_CENTER)
            ahead = j + GRAD_LEAD
            if ahead < GRAD_CHUNKS:
                own_grad[ahead] = local_grad(ahead, [total[j]])
                inward[ahead] = lax.ppermute(own_grad[ahead], "dp", TO_CENTER)
        j = k - 2
        if 0 <= j < GRAD_CHUNKS:
            deps = [total[j + 1]] if j + 1 < GRAD_CHUNKS else []
            result = place_chunk(
                place,
                total[j],
                outward[j],
                result,
                j < per_half,
                j % per_half,
                columns,
                (2 * features, hidden_count),
                deps,
            )
    return result[None]


def solution(mesh):
    on_line = mesh.shape["dp"] == 4 and mesh.shape["mp"] == 2 and mesh.shape["section"] == 2
    in_specs = (
        P("dp", "groups", "mp"),
        P(("groups", "dp"), None, "mp"),
        P("dp", "groups"),
        P(("groups", "dp"), None),
        P("dp", "groups"),
        P(("groups", "dp"), None),
        P("dp", "groups"),
        P(("groups", "dp"), None),
        P("dp", "groups"),
        P(("groups", "dp"), None),
        P(("groups", "dp")),
        P(("groups", "dp")),
        P("section", None, "mp"),
        P("mp"),
        P("mp", None),
    )
    out_specs = P(("groups", "section"), None, "mp")
    per_device = line_plan if on_line else general_plan
    return jax.shard_map(
        per_device, mesh=mesh, in_specs=in_specs, out_specs=out_specs, check_vma=False
    )
```

```python
import functools
import math

import jax
import jax.numpy as jnp
from jax import lax
from jax.experimental import pallas as pl
from jax.experimental.pallas import tpu as pltpu
from jax.sharding import PartitionSpec as P

DISCOUNT_RATE = 0.99
TRACE_LAMBDA = 0.95


def silu_slope(pre):
    sigma = jax.nn.sigmoid(pre)
    return sigma * (1.0 + pre * (1.0 - sigma))


def importance_trace_terms(
    value_estimates,
    policy_logits,
    reward_rows,
    behaviour_probs,
    taken_actions,
    episode_finished,
    sequence_length,
    objective_scale,
):
    seq_count, step_count = value_estimates.shape
    action_count = policy_logits.shape[0]
    positions = jnp.arange(step_count, dtype=jnp.int32)
    valid_mask = (positions[None, :] < sequence_length[:, None]).astype(jnp.float32)
    zero_column = jnp.zeros((seq_count, 1), jnp.float32)
    valid_next = jnp.concatenate([valid_mask[:, 1:], zero_column], axis=1)
    log_probs = jax.nn.log_softmax(policy_logits, axis=0)
    one_hot = (
        jnp.arange(action_count, dtype=jnp.int32)[:, None, None] == taken_actions[None]
    ).astype(jnp.float32)
    chosen = jnp.sum(one_hot * log_probs, axis=0)
    clip_ratio = jnp.exp(jnp.minimum(chosen - behaviour_probs, 0.0))
    discount = DISCOUNT_RATE * (1.0 - episode_finished.astype(jnp.float32))
    next_value = jnp.concatenate([value_estimates[:, 1:], zero_column], axis=1) * valid_next
    td_error = valid_mask * clip_ratio * (reward_rows + discount * next_value - value_estimates)
    trace_coef = discount * TRACE_LAMBDA * clip_ratio * valid_next

    def backward_step(carried, inputs):
        error_now, coef_now = inputs
        updated = error_now + coef_now * carried
        return (updated, updated)

    final_state, stacked = lax.scan(
        backward_step,
        jnp.zeros((seq_count,), jnp.float32),
        (td_error.T, trace_coef.T),
        reverse=True,
    )
    correction = stacked.T
    targets = value_estimates + correction
    next_target = jnp.concatenate([targets[:, 1:], zero_column], axis=1) * valid_next
    policy_adv = clip_ratio * (reward_rows + discount * next_target - value_estimates)
    value_gradient = -objective_scale * valid_mask * correction
    logits_gradient = (
        objective_scale * (valid_mask * policy_adv)[None] * (jnp.exp(log_probs) - one_hot)
    )
    return (value_gradient, logits_gradient)


def head_terms(hidden, value_w, policy_w):
    logit_part = jnp.einsum("rh,ha->ar", hidden, policy_w, preferred_element_type=jnp.float32)
    value_part = jnp.dot(hidden, value_w, preferred_element_type=jnp.float32)
    return jnp.concatenate([logit_part, value_part[None]], axis=0)


def full_rows(online_part, offline_part):
    return (
        lax.all_gather(online_part, "mp", axis=2, tiled=True),
        lax.all_gather(offline_part, "mp", axis=2, tiled=True),
    )


def general_plan(
    online_obs,
    offline_obs,
    online_rewards,
    offline_rewards,
    online_behaviour,
    offline_behaviour,
    online_actions,
    offline_actions,
    online_done,
    offline_done,
    online_lengths,
    offline_lengths,
    torso_weights,
    value_head,
    policy_head,
):
    owned_online = online_lengths.shape[0]
    owned_offline = offline_obs.shape[0]
    step_count = offline_obs.shape[1]
    action_count = policy_head.shape[1]
    record_stack = jnp.stack(
        [
            online_rewards,
            online_behaviour,
            online_actions.astype(jnp.float32),
            online_done.astype(jnp.float32),
        ]
    )
    records = lax.all_to_all(record_stack, "dp", split_axis=2, concat_axis=1, tiled=True)
    slabs = lax.all_to_all(online_obs, "dp", split_axis=1, concat_axis=0, tiled=True)
    x_online, x_offline = full_rows(slabs, offline_obs)
    feature_count = x_online.shape[2]
    x_online = x_online.reshape(step_count * owned_online, feature_count)
    x_offline = x_offline.reshape(owned_offline * step_count, feature_count)
    weight = torso_weights[0]
    pre_online = jnp.dot(x_online, weight, preferred_element_type=jnp.float32)
    pre_offline = jnp.dot(x_offline, weight, preferred_element_type=jnp.float32)
    hidden_online = jax.nn.silu(pre_online).astype(jnp.bfloat16)
    hidden_offline = jax.nn.silu(pre_offline).astype(jnp.bfloat16)
    is_critic = (lax.axis_index("section") == 0).astype(jnp.float32)
    is_policy = 1.0 - is_critic
    row_keep = jnp.where(jnp.arange(action_count + 1) == action_count, is_critic, is_policy)
    partial_value = jnp.concatenate(
        [
            head_terms(hidden_online, value_head, policy_head),
            head_terms(hidden_offline, value_head, policy_head),
        ],
        axis=1,
    )
    partial_value = partial_value * row_keep[:, None]
    heads = lax.psum(partial_value, ("mp", "section"))
    online_count = step_count * owned_online
    logits_on = (
        heads[:action_count, :online_count]
        .reshape(action_count, step_count, owned_online)
        .transpose(0, 2, 1)
    )
    logits_off = heads[:action_count, online_count:].reshape(
        action_count, owned_offline, step_count
    )
    values_on = heads[action_count, :online_count].reshape(step_count, owned_online).T
    values_off = heads[action_count, online_count:].reshape(owned_offline, step_count)
    record_seq = records.transpose(0, 2, 1)
    value_estimates = jnp.concatenate([values_on, values_off], axis=0)
    policy_logits = jnp.concatenate([logits_on, logits_off], axis=1)
    reward_rows = jnp.concatenate([record_seq[0], offline_rewards], axis=0)
    behaviour_probs = jnp.concatenate([record_seq[1], offline_behaviour], axis=0)
    taken_actions = jnp.concatenate([record_seq[2].astype(jnp.int32), offline_actions], axis=0)
    episode_finished = jnp.concatenate([record_seq[3].astype(jnp.int32), offline_done], axis=0)
    sequence_length = jnp.concatenate([online_lengths, offline_lengths], axis=0)
    total_seqs = online_obs.shape[1] + owned_offline * lax.axis_size("dp")
    hidden_total = value_head.shape[0] * lax.axis_size("mp")
    objective_scale = math.sqrt(hidden_total / (total_seqs * step_count))
    value_gradient, logits_gradient = importance_trace_terms(
        value_estimates,
        policy_logits,
        reward_rows,
        behaviour_probs,
        taken_actions,
        episode_finished,
        sequence_length,
        objective_scale,
    )
    value_gradient = value_gradient * is_critic
    logits_gradient = logits_gradient * is_policy
    dv_on = value_gradient[:owned_online].T.reshape(online_count)
    dv_off = value_gradient[owned_online:].reshape(owned_offline * step_count)
    dl_on = logits_gradient[:, :owned_online].transpose(0, 2, 1).reshape(action_count, online_count)
    dl_off = logits_gradient[:, owned_online:].reshape(action_count, owned_offline * step_count)
    value_w = value_head.astype(jnp.float32)
    policy_w = policy_head.astype(jnp.float32)
    dh_on = dv_on[:, None] * value_w[None, :] + jnp.einsum(
        "ar,ha->rh", dl_on, policy_w, precision=lax.Precision.HIGHEST
    )
    dh_off = dv_off[:, None] * value_w[None, :] + jnp.einsum(
        "ar,ha->rh", dl_off, policy_w, precision=lax.Precision.HIGHEST
    )
    dz_online = (dh_on * silu_slope(pre_online)).astype(jnp.bfloat16)
    dz_offline = (dh_off * silu_slope(pre_offline)).astype(jnp.bfloat16)
    local_grad = jnp.einsum("rd,rh->dh", x_online, dz_online, preferred_element_type=jnp.float32)
    local_grad = local_grad + jnp.einsum(
        "rd,rh->dh", x_offline, dz_offline, preferred_element_type=jnp.float32
    )
    summed = lax.psum(local_grad, "dp")
    return summed[None]


HEAD_ROWS = 24
SPLIT_ROWS = 4 * HEAD_ROWS
COLUMN_BLOCK = 256
GRAD_CHUNKS = 8
GRAD_LEAD = 4
ONLINE_CHUNKS = 4
OFFLINE_CHUNKS = 2
LANES = 128
CODE_LIMIT = 32512.0
CODE_TAIL = 16
LOG_TWO = math.log(2.0)
SCRATCH_BYTES = 12 * 1024 * 1024
SWAP = ((0, 1), (1, 0))
TO_CENTER = ((0, 1), (3, 2))
CENTER = ((1, 2), (2, 1))
FROM_CENTER = ((1, 0), (2, 3))
VMEM = pl.BlockSpec(memory_space=pltpu.VMEM)
SMEM = pl.BlockSpec(memory_space=pltpu.SMEM)


SHORT = pl.CostEstimate(flops=1, bytes_accessed=1, transcendentals=0)


def params():
    return pltpu.CompilerParams(vmem_limit_bytes=SCRATCH_BYTES)


def resident(array):
    return pltpu.with_memory_space_constraint(array, pltpu.VMEM)


def vmem_call(body, place, arrays, outs, name, deps=()):
    operands = list(arrays) + list(deps)

    def run(place_ref, *refs):
        body(place_ref, *refs[: len(arrays)], *refs[len(operands) :])

    return pl.pallas_call(
        run,
        in_specs=[SMEM] + [VMEM] * len(operands),
        out_specs=[VMEM] * len(outs),
        out_shape=[pltpu.VMEM(shape, dtype) for shape, dtype in outs],
        compiler_params=params(),
        cost_estimate=SHORT,
        name=name,
    )(place, *[resident(x) for x in operands])


def stage_body(copies, count, place, *refs):
    sources, outs, sems = refs[:count], refs[count:-1], refs[-1]
    started = []
    for i, (which, first, rows) in enumerate(copies):
        source = sources[which]
        if rows is not None:
            source = source.at[pl.ds(first + place[3] * rows, rows)]
        copy = pltpu.make_async_copy(source, outs[i], sems.at[i])
        copy.start()
        started.append(copy)
    for copy in started:
        copy.wait()


def stage(place, sources, copies, deps=()):
    sources = list(sources)
    operands = sources + list(deps)
    outs = []
    for which, _, rows in copies:
        shape = sources[which].shape
        outs.append(shape if rows is None else (rows,) + shape[1:])

    def run(place_ref, *refs):
        stage_body(copies, len(sources), place_ref, *refs[: len(sources)], *refs[len(operands) :])

    return pl.pallas_call(
        run,
        in_specs=[SMEM]
        + [pl.BlockSpec(memory_space=pltpu.HBM)] * len(sources)
        + [VMEM] * len(deps),
        out_specs=[VMEM] * len(outs),
        out_shape=[
            pltpu.VMEM(shape, sources[which].dtype) for shape, (which, _, _) in zip(outs, copies)
        ],
        scratch_shapes=[pltpu.SemaphoreType.DMA((len(copies),))],
        compiler_params=params(),
        cost_estimate=SHORT,
        name="stage_rows",
    )(place, *sources, *[resident(x) for x in deps])


def forward_body(first, earlier_count, place, *refs):
    own_ref, got_ref, rest_ref, weight_ref, head_ref = refs[:5]
    earlier = refs[5 : 5 + earlier_count]
    slope_ref, heads_ref, other_ref = refs[5 + earlier_count :]
    groups, width, features = other_ref.shape
    half = groups // 2
    rows = groups * width
    m, section = place[0], place[3]
    own_at = pl.multiple_of(m * features, features)
    other_at = pl.multiple_of((1 - m) * features, features)
    other_ref[pl.ds(section * half, half)] = got_ref[...]
    other_ref[pl.ds((1 - section) * half, half)] = rest_ref[...]
    own = own_ref[first : first + groups].reshape(rows, features)
    other = other_ref[...].reshape(rows, features)
    hidden_count = weight_ref.shape[1]
    before = heads_ref.shape[0] - groups
    if earlier:
        heads_ref[:before] = earlier[0][...]
    sums = [jnp.zeros((HEAD_ROWS, width), jnp.float32)] * groups
    for h in range(0, hidden_count, COLUMN_BLOCK):
        block = slice(h, h + COLUMN_BLOCK)
        pre = jnp.dot(
            own, weight_ref[pl.ds(own_at, features), block], preferred_element_type=jnp.float32
        )
        pre = pre + jnp.dot(
            other, weight_ref[pl.ds(other_at, features), block], preferred_element_type=jnp.float32
        )
        sigma = 0.5 * jnp.tanh(0.5 * pre) + 0.5
        hidden = pre * sigma
        slope = sigma + hidden * (1.0 - sigma)
        hidden = hidden.astype(jnp.bfloat16)
        for g in range(groups):
            part = slice(g * width, (g + 1) * width)
            slope_ref[g, :, block] = slope[part]
            heads = lax.dot_general(
                head_ref[:, block],
                hidden[part],
                (((1,), (1,)), ((), ())),
                preferred_element_type=jnp.float32,
            )
            sums[g] = sums[g] + heads[:HEAD_ROWS]
    for g in range(groups):
        heads_ref[before + g] = sums[g]


def forward(place, own, first, pieces, weight, head, earlier, deps):
    got, rest = pieces
    half, width, features = got.shape
    groups = 2 * half
    hidden_count = weight.shape[1]
    before = sum(x.shape[0] for x in earlier)
    return vmem_call(
        functools.partial(forward_body, first, len(earlier)),
        place,
        [own, got, rest, weight, head] + earlier,
        [
            ((groups, width, hidden_count), jnp.float32),
            ((before + groups, HEAD_ROWS, width), jnp.float32),
            ((groups, width, features), jnp.bfloat16),
        ],
        "forward_rows",
        deps,
    )


def action_terms(parts, actions, behaviour, action_count):
    heads = parts[0] + parts[1] + (parts[2] + parts[3])
    row = lax.broadcasted_iota(jnp.int32, heads.shape, 0)
    is_logit = row < action_count
    logits = jnp.where(is_logit, heads, -1e30)
    shifted = logits - jnp.max(logits, axis=0, keepdims=True)
    log_sum = jnp.log(jnp.sum(jnp.exp(shifted), axis=0, keepdims=True))
    log_probs = shifted - log_sum
    taken = row == actions
    chosen = jnp.sum(jnp.where(taken, log_probs, 0.0), axis=0, keepdims=True)
    rho = jnp.exp(jnp.minimum(chosen - behaviour, 0.0))
    spread = jnp.where(is_logit, jnp.exp(log_probs) - taken.astype(jnp.float32), 0.0)
    return heads[action_count : action_count + 1], rho, spread


def trace_terms(value, rho, reward, discount, length, position, axis, reach, scale):
    size = value.shape[axis]
    valid = (position < length).astype(jnp.float32)
    valid_next = (position + 1 < length).astype(jnp.float32)
    next_value = pltpu.roll(value, size - 1, axis) * valid_next
    correction = valid * rho * (reward + discount * next_value - value)
    coef = discount * TRACE_LAMBDA * rho * valid_next
    shift = 1
    while shift < reach:
        correction = correction + coef * pltpu.roll(correction, size - shift, axis)
        coef = coef * pltpu.roll(coef, size - shift, axis)
        shift *= 2
    targets = value + correction
    next_target = pltpu.roll(targets, size - 1, axis) * valid_next
    advantage = rho * (reward + discount * next_target - value)
    return -scale * valid * correction, scale * (valid * advantage)


def split_terms(logit_weight, value_weight, spread, action_count):
    row = lax.broadcasted_iota(jnp.int32, spread.shape, 0)
    full = jnp.where(row == action_count, value_weight, logit_weight * spread)
    high = full.astype(jnp.bfloat16).astype(jnp.float32)
    rest = full - high
    middle = rest.astype(jnp.bfloat16).astype(jnp.float32)
    low = rest - middle
    return jnp.concatenate([high, middle, low, jnp.zeros_like(full)], axis=0).astype(jnp.bfloat16)


def write_back(terms, head_ref, slope, dz_ref, g):
    dh = lax.dot_general(
        terms, head_ref[...], (((0,), (0,)), ((), ())), preferred_element_type=jnp.float32
    )
    dz_ref[g] = (dh * slope).astype(jnp.bfloat16)


def online_heads_body(action_count, place, *refs):
    first, second = refs[:4], refs[4:8]
    actions, behaviour, reward, done, pack_ref, spread_ref = refs[8:]
    steps = actions.shape[0]
    half = steps // 2
    for t in range(steps):
        parts = first if t < half else second
        value, rho, spread = action_terms(
            [p[t % half] for p in parts],
            actions[t : t + 1, :],
            behaviour[t : t + 1, :],
            action_count,
        )
        pack_ref[t : t + 1, :] = value
        pack_ref[steps + t : steps + t + 1, :] = rho
        spread_ref[t] = spread
    pack_ref[2 * steps : 3 * steps, :] = reward[...]
    pack_ref[3 * steps : 4 * steps, :] = DISCOUNT_RATE * (1.0 - done[...].astype(jnp.float32))


def online_back_body(action_count, scale, place, *refs):
    blocks, length, spread, head_ref = refs[:4], refs[4], refs[5], refs[6]
    slopes, dz_ref = refs[7:-1], refs[-1]
    steps = spread.shape[0]
    per_slope = steps // len(slopes)

    def field(i):
        return jnp.concatenate([b[i * steps : (i + 1) * steps, :] for b in blocks], axis=0)

    value = field(0)
    position = lax.broadcasted_iota(jnp.int32, value.shape, 0) + place[2] * steps
    value_weight, logit_weight = trace_terms(
        value,
        field(1),
        field(2),
        field(3),
        length[...],
        position,
        0,
        value.shape[0],
        scale,
    )
    for t in range(steps):
        terms = split_terms(
            logit_weight[t : t + 1, :], value_weight[t : t + 1, :], spread[t], action_count
        )
        write_back(terms, head_ref, slopes[t // per_slope][t % per_slope], dz_ref, t)


def offline_back_body(action_count, step_count, scale, place, *refs):
    parts = refs[:4]
    actions, behaviour, reward, done, length, head_ref = refs[4:10]
    slopes, dz_ref = refs[10:-1], refs[-1]
    groups = dz_ref.shape[0]
    per_slope = groups // len(slopes)
    values, rhos, spreads = [], [], []
    for g in range(groups):
        value, rho, spread = action_terms(
            [p[g] for p in parts],
            actions[g : g + 1, :],
            behaviour[g : g + 1, :],
            action_count,
        )
        values.append(value)
        rhos.append(rho)
        spreads.append(spread)
    value = jnp.concatenate(values, axis=0)
    rho = jnp.concatenate(rhos, axis=0)
    position = lax.rem(lax.broadcasted_iota(jnp.int32, value.shape, 1), step_count)
    discount = DISCOUNT_RATE * (1.0 - done[...].astype(jnp.float32))
    value_weight, logit_weight = trace_terms(
        value, rho, reward[...], discount, length[...], position, 1, step_count, scale
    )
    for g in range(groups):
        terms = split_terms(
            logit_weight[g : g + 1, :], value_weight[g : g + 1, :], spreads[g], action_count
        )
        write_back(terms, head_ref, slopes[g // per_slope][g % per_slope], dz_ref, g)


def encode(v, c, message_ref):
    rows = v.shape[0]
    largest = jnp.max(jnp.abs(v), axis=0, keepdims=True)
    exponent = jnp.ceil(jnp.log(jnp.maximum(largest, 1e-30)) * (1.0 / LOG_TWO) + 0.01)
    scale = jnp.exp(exponent * -LOG_TWO) * CODE_LIMIT
    code = jnp.clip(jnp.floor(v * scale + 0.5), -CODE_LIMIT, CODE_LIMIT)
    message_ref[c * rows : (c + 1) * rows, :] = code.astype(jnp.int32).astype(jnp.int16)
    return exponent


def encode_tail(exponents, message_ref):
    fill = [jnp.zeros_like(exponents[0])] * (CODE_TAIL - len(exponents))
    tail = jnp.concatenate(exponents + fill, axis=0).astype(jnp.int32)
    message_ref[message_ref.shape[0] - CODE_TAIL :, :] = tail.astype(jnp.int16)


def decoder(message_ref, count):
    rows = (message_ref.shape[0] - CODE_TAIL) // count
    exponents = message_ref[count * rows :, :].astype(jnp.int32).astype(jnp.float32)
    steps = jnp.exp(exponents * LOG_TWO) * (1.0 / CODE_LIMIT)

    def block(c):
        code = message_ref[c * rows : (c + 1) * rows, :].astype(jnp.int32).astype(jnp.float32)
        return code * steps[c : c + 1, :]

    return block


def message_of(rows, columns):
    return ((rows * (columns // LANES) + CODE_TAIL, LANES), jnp.int16)


def grad_body(pieces, column, columns, place, *refs):
    xs, dzs = refs[: len(pieces)], refs[len(pieces) : len(pieces) + 2]
    message_ref = refs[-1]
    hidden_count = dzs[0].shape[2]
    exponents = []
    at = slice(column * columns, (column + 1) * columns)
    for h in range(0, hidden_count, COLUMN_BLOCK):
        total = None
        for x, (which, first) in zip(xs, pieces):
            groups, width, _ = x.shape
            part = lax.dot_general(
                x[:, :, at].reshape(groups * width, columns),
                dzs[which][first : first + groups, :, h : h + COLUMN_BLOCK].reshape(
                    groups * width, COLUMN_BLOCK
                ),
                (((0,), (0,)), ((), ())),
                preferred_element_type=jnp.float32,
            )
            total = part if total is None else total + part
        for c in range(COLUMN_BLOCK // LANES):
            block = total[:, c * LANES : (c + 1) * LANES]
            exponents.append(encode(block, h // LANES + c, message_ref))
    encode_tail(exponents, message_ref)


def grad_chunk(place, pieces, dzs, column, columns, deps):
    hidden_count = dzs[0].shape[2]
    return vmem_call(
        functools.partial(grad_body, [p[1:] for p in pieces], column, columns),
        place,
        [x for x, _, _ in pieces] + dzs,
        [message_of(columns, hidden_count)],
        "grad_chunk",
        deps,
    )[0]


def add_body(count, place, *refs):
    first, second = decoder(refs[0], count), decoder(refs[1], count)
    out = refs[-1]
    encode_tail([encode(first(c) + second(c), c, out) for c in range(count)], out)


def add_chunk(place, a, b, count, deps):
    return vmem_call(
        functools.partial(add_body, count),
        place,
        [a, b],
        [(a.shape, a.dtype)],
        "add_chunk",
        deps,
    )[0]


def place_body(count, place, total, received, *refs):
    out, token = refs[-2:]
    token[...] = jnp.zeros_like(token)
    at_end = place[1] == 1

    def write(message):
        block = decoder(message, count)
        for c in range(count):
            out[:, c * LANES : (c + 1) * LANES] = block(c)

    @pl.when(at_end)
    def _():
        write(received)

    @pl.when(jnp.logical_not(at_end))
    def _():
        write(total)


def place_chunk(place, total, received, result, of_own, index, rows, shape, deps):
    row_count, hidden_count = shape
    per_half = row_count // (2 * rows)

    def at(i, p):
        half = p[0] if of_own else 1 - p[0]
        return (half * per_half + index, 0)

    earlier = [] if result is None else [result]
    return pl.pallas_call(
        functools.partial(place_body, hidden_count // LANES),
        grid_spec=pltpu.PrefetchScalarGridSpec(
            num_scalar_prefetch=1,
            grid=(1,),
            in_specs=[VMEM, VMEM]
            + [pl.BlockSpec(memory_space=pl.ANY) for _ in earlier]
            + [VMEM for _ in deps],
            out_specs=[pl.BlockSpec((rows, hidden_count), at), VMEM],
        ),
        out_shape=[jax.ShapeDtypeStruct(shape, jnp.float32), pltpu.VMEM((8, LANES), jnp.float32)],
        input_output_aliases={3: 0} if earlier else {},
        compiler_params=params(),
        cost_estimate=SHORT,
        name="place_chunk",
    )(place, resident(total), resident(received), *earlier, *[resident(d) for d in deps])


def pipeline_order(count, lead):
    order = [("grad", k) for k in range(min(lead, count))]
    for k in range(count + 3):
        if k < count:
            order.append(("partial", k))
        if 0 <= k - 1 < count:
            order.append(("total", k - 1))
            if k - 1 + lead < count:
                order.append(("grad", k - 1 + lead))
        if 0 <= k - 3 < count:
            order.append(("place", k - 3))
    return order


def after(array, *others):
    return lax.optimization_barrier((array,) + others)[0]


def chip_pair(part, gate=()):
    across = lax.ppermute(part, "mp", SWAP)
    return [
        part,
        lax.ppermute(part, "section", SWAP),
        across,
        lax.ppermute(after(across, *gate), "section", SWAP),
    ]


def line_plan(
    online_obs,
    offline_obs,
    online_rewards,
    offline_rewards,
    online_behaviour,
    offline_behaviour,
    online_actions,
    offline_actions,
    online_done,
    offline_done,
    online_lengths,
    offline_lengths,
    torso_weights,
    value_head,
    policy_head,
):
    section = lax.axis_index("section")
    m = lax.axis_index("mp")
    z = lax.axis_index("dp")
    dp = lax.axis_size("dp")
    steps, online_count, features = online_obs.shape
    offline_count, step_count, _ = offline_obs.shape
    action_count = policy_head.shape[1]
    hidden_count = value_head.shape[0]
    at_end = ((z == 0) | (z == dp - 1)).astype(jnp.int32)
    place = jnp.stack([m, at_end, z, section]).astype(jnp.int32)
    weight = torso_weights[0]
    scale = math.sqrt(
        hidden_count
        * lax.axis_size("mp")
        / ((online_count + offline_count * dp) * step_count)
    )

    offline_groups = offline_count // 2
    offline_rows = offline_obs.reshape(offline_groups, 2 * step_count, features)
    chunks, copies = [], []
    for which, (obs, count) in enumerate(
        ((online_obs, ONLINE_CHUNKS), (offline_rows, OFFLINE_CHUNKS))
    ):
        groups = obs.shape[0] // count
        for c in range(count):
            chunks.append((which, c * groups))
            copies.append((which, c * groups, groups // 2))
    sources = [online_obs, offline_rows, weight]
    halves = list(stage(place, sources[:1], copies[:1]))
    *staged, own_online, own_offline, weight = stage(
        place,
        sources,
        copies[1:] + [(0, 0, None), (1, 0, None), (2, 0, None)],
        halves,
    )
    halves += staged
    own = (own_online, own_offline)

    policy_rows = jnp.where(section == 1, policy_head.T, 0)
    value_row = jnp.where(section == 0, value_head[None], 0)
    head = jnp.concatenate([policy_rows, value_row], axis=0).astype(jnp.bfloat16)
    head = jnp.pad(head, ((0, HEAD_ROWS - action_count - 1), (0, 0)))
    forward_head = jnp.pad(head, ((0, 32 - HEAD_ROWS), (0, 0)))
    back_head = jnp.concatenate([head, head, head, jnp.zeros_like(head)], axis=0)

    owned = online_lengths.shape[0]
    length_row = lax.dynamic_update_slice(
        jnp.zeros((online_count,), jnp.float32), online_lengths.astype(jnp.float32), (z * owned,)
    )
    for flip in (1, 2):
        length_row = length_row + lax.ppermute(
            length_row, "dp", [(i, i ^ flip) for i in range(dp)]
        )
    length_row = length_row.astype(jnp.int32)[None]
    lanes = (offline_groups, 2 * step_count)
    offline_length = jnp.broadcast_to(
        offline_lengths[:, None], (offline_count, step_count)
    ).reshape(lanes)

    slopes, parts, others = [], [], []
    got = [lax.ppermute(half, "mp", SWAP) for half in halves]
    for k, (which, first) in enumerate(chunks):
        mine = after(got[k], parts[k - 1]) if k else got[k]
        rest = lax.ppermute(mine, "section", SWAP)
        earlier = [parts[k - 1]] if k % 2 else []
        if k == 0:
            deps = [back_head, offline_length]
        else:
            deps = [parts[k - 1]] + ([length_row] if k == 1 else [])
        slope, part, other = forward(
            place, own[which], first, (got[k], rest), weight, forward_head, earlier, deps
        )
        slopes.append(slope)
        parts.append(part)
        others.append(other)
    last = parts[-1]

    pack, spread = vmem_call(
        functools.partial(online_heads_body, action_count),
        place,
        chip_pair(parts[1], [last])
        + chip_pair(parts[3], [last])
        + [online_actions, online_behaviour, online_rewards, online_done],
        [
            ((4 * steps, online_count), jnp.float32),
            ((steps, HEAD_ROWS, online_count), jnp.float32),
        ],
        "online_heads",
        [last],
    )
    later = [
        lax.ppermute(pack, "dp", [(i, i - hop) for i in range(hop, dp)]) for hop in range(1, dp)
    ]

    (dz_offline,) = vmem_call(
        functools.partial(offline_back_body, action_count, step_count, scale),
        place,
        chip_pair(parts[5])
        + [
            offline_actions.reshape(lanes),
            offline_behaviour.reshape(lanes),
            offline_rewards.reshape(lanes),
            offline_done.reshape(lanes),
            offline_length,
            back_head,
        ]
        + slopes[ONLINE_CHUNKS:],
        [((offline_groups, 2 * step_count, hidden_count), jnp.bfloat16)],
        "offline_back",
        [pack],
    )

    (dz_online,) = vmem_call(
        functools.partial(online_back_body, action_count, scale),
        place,
        [pack, *later, length_row, spread, back_head] + slopes[:ONLINE_CHUNKS],
        [((steps, online_count, hidden_count), jnp.bfloat16)],
        "online_back",
        [dz_offline],
    )

    own_x = [(own_online, 0, 0), (own_offline, 1, 0)]
    other_x = [(others[k], int(k >= ONLINE_CHUNKS), chunks[k][1]) for k in range(len(chunks))]
    columns = 2 * features // GRAD_CHUNKS
    per_half = GRAD_CHUNKS // 2
    lane_blocks = hidden_count // LANES

    messages, inward, partial, across, total, outward = {}, {}, {}, {}, {}, {}
    result, last = None, dz_online
    for kind, k in pipeline_order(GRAD_CHUNKS, GRAD_LEAD):
        if kind == "grad":
            last = messages[k] = grad_chunk(
                place,
                own_x if k < per_half else other_x,
                [dz_online, dz_offline],
                k % per_half,
                columns,
                [last],
            )
            inward[k] = lax.ppermute(last, "dp", TO_CENTER)
        elif kind == "partial":
            last = partial[k] = add_chunk(place, messages[k], inward[k], lane_blocks, [last])
            across[k] = lax.ppermute(last, "dp", CENTER)
        elif kind == "total":
            last = total[k] = add_chunk(place, partial[k], across[k], lane_blocks, [last])
            outward[k] = lax.ppermute(last, "dp", FROM_CENTER)
        else:
            result, last = place_chunk(
                place,
                total[k],
                outward[k],
                result,
                k < per_half,
                k % per_half,
                columns,
                (2 * features, hidden_count),
                [last],
            )
    return result[None]


def solution(mesh):
    on_line = mesh.shape["dp"] == 4 and mesh.shape["mp"] == 2 and mesh.shape["section"] == 2
    in_specs = (
        P("dp", "groups", "mp"),
        P(("groups", "dp"), None, "mp"),
        P("dp", "groups"),
        P(("groups", "dp"), None),
        P("dp", "groups"),
        P(("groups", "dp"), None),
        P("dp", "groups"),
        P(("groups", "dp"), None),
        P("dp", "groups"),
        P(("groups", "dp"), None),
        P(("groups", "dp")),
        P(("groups", "dp")),
        P("section", None, "mp"),
        P("mp"),
        P("mp", None),
    )
    out_specs = P(("groups", "section"), None, "mp")
    per_device = line_plan if on_line else general_plan
    return jax.shard_map(
        per_device, mesh=mesh, in_specs=in_specs, out_specs=out_specs, check_vma=False
    )
```

```python
import functools
import math

import jax
import jax.numpy as jnp
from jax import lax
from jax.experimental import pallas as pl
from jax.experimental.pallas import tpu as pltpu
from jax.sharding import PartitionSpec as P

DISCOUNT_RATE = 0.99
TRACE_LAMBDA = 0.95


def silu_slope(pre):
    sigma = jax.nn.sigmoid(pre)
    return sigma * (1.0 + pre * (1.0 - sigma))


def importance_trace_terms(
    value_estimates,
    policy_logits,
    reward_rows,
    behaviour_probs,
    taken_actions,
    episode_finished,
    sequence_length,
    objective_scale,
):
    seq_count, step_count = value_estimates.shape
    action_count = policy_logits.shape[0]
    positions = jnp.arange(step_count, dtype=jnp.int32)
    valid_mask = (positions[None, :] < sequence_length[:, None]).astype(jnp.float32)
    zero_column = jnp.zeros((seq_count, 1), jnp.float32)
    valid_next = jnp.concatenate([valid_mask[:, 1:], zero_column], axis=1)
    log_probs = jax.nn.log_softmax(policy_logits, axis=0)
    one_hot = (
        jnp.arange(action_count, dtype=jnp.int32)[:, None, None] == taken_actions[None]
    ).astype(jnp.float32)
    chosen = jnp.sum(one_hot * log_probs, axis=0)
    clip_ratio = jnp.exp(jnp.minimum(chosen - behaviour_probs, 0.0))
    discount = DISCOUNT_RATE * (1.0 - episode_finished.astype(jnp.float32))
    next_value = jnp.concatenate([value_estimates[:, 1:], zero_column], axis=1) * valid_next
    td_error = valid_mask * clip_ratio * (reward_rows + discount * next_value - value_estimates)
    trace_coef = discount * TRACE_LAMBDA * clip_ratio * valid_next

    def backward_step(carried, inputs):
        error_now, coef_now = inputs
        updated = error_now + coef_now * carried
        return (updated, updated)

    final_state, stacked = lax.scan(
        backward_step,
        jnp.zeros((seq_count,), jnp.float32),
        (td_error.T, trace_coef.T),
        reverse=True,
    )
    correction = stacked.T
    targets = value_estimates + correction
    next_target = jnp.concatenate([targets[:, 1:], zero_column], axis=1) * valid_next
    policy_adv = clip_ratio * (reward_rows + discount * next_target - value_estimates)
    value_gradient = -objective_scale * valid_mask * correction
    logits_gradient = (
        objective_scale * (valid_mask * policy_adv)[None] * (jnp.exp(log_probs) - one_hot)
    )
    return (value_gradient, logits_gradient)


def head_terms(hidden, value_w, policy_w):
    logit_part = jnp.einsum("rh,ha->ar", hidden, policy_w, preferred_element_type=jnp.float32)
    value_part = jnp.dot(hidden, value_w, preferred_element_type=jnp.float32)
    return jnp.concatenate([logit_part, value_part[None]], axis=0)


def full_rows(online_part, offline_part):
    return (
        lax.all_gather(online_part, "mp", axis=2, tiled=True),
        lax.all_gather(offline_part, "mp", axis=2, tiled=True),
    )


def general_plan(
    online_obs,
    offline_obs,
    online_rewards,
    offline_rewards,
    online_behaviour,
    offline_behaviour,
    online_actions,
    offline_actions,
    online_done,
    offline_done,
    online_lengths,
    offline_lengths,
    torso_weights,
    value_head,
    policy_head,
):
    owned_online = online_lengths.shape[0]
    owned_offline = offline_obs.shape[0]
    step_count = offline_obs.shape[1]
    action_count = policy_head.shape[1]
    record_stack = jnp.stack(
        [
            online_rewards,
            online_behaviour,
            online_actions.astype(jnp.float32),
            online_done.astype(jnp.float32),
        ]
    )
    records = lax.all_to_all(record_stack, "dp", split_axis=2, concat_axis=1, tiled=True)
    slabs = lax.all_to_all(online_obs, "dp", split_axis=1, concat_axis=0, tiled=True)
    x_online, x_offline = full_rows(slabs, offline_obs)
    feature_count = x_online.shape[2]
    x_online = x_online.reshape(step_count * owned_online, feature_count)
    x_offline = x_offline.reshape(owned_offline * step_count, feature_count)
    weight = torso_weights[0]
    pre_online = jnp.dot(x_online, weight, preferred_element_type=jnp.float32)
    pre_offline = jnp.dot(x_offline, weight, preferred_element_type=jnp.float32)
    hidden_online = jax.nn.silu(pre_online).astype(jnp.bfloat16)
    hidden_offline = jax.nn.silu(pre_offline).astype(jnp.bfloat16)
    is_critic = (lax.axis_index("section") == 0).astype(jnp.float32)
    is_policy = 1.0 - is_critic
    row_keep = jnp.where(jnp.arange(action_count + 1) == action_count, is_critic, is_policy)
    partial_value = jnp.concatenate(
        [
            head_terms(hidden_online, value_head, policy_head),
            head_terms(hidden_offline, value_head, policy_head),
        ],
        axis=1,
    )
    partial_value = partial_value * row_keep[:, None]
    heads = lax.psum(partial_value, ("mp", "section"))
    online_count = step_count * owned_online
    logits_on = (
        heads[:action_count, :online_count]
        .reshape(action_count, step_count, owned_online)
        .transpose(0, 2, 1)
    )
    logits_off = heads[:action_count, online_count:].reshape(
        action_count, owned_offline, step_count
    )
    values_on = heads[action_count, :online_count].reshape(step_count, owned_online).T
    values_off = heads[action_count, online_count:].reshape(owned_offline, step_count)
    record_seq = records.transpose(0, 2, 1)
    value_estimates = jnp.concatenate([values_on, values_off], axis=0)
    policy_logits = jnp.concatenate([logits_on, logits_off], axis=1)
    reward_rows = jnp.concatenate([record_seq[0], offline_rewards], axis=0)
    behaviour_probs = jnp.concatenate([record_seq[1], offline_behaviour], axis=0)
    taken_actions = jnp.concatenate([record_seq[2].astype(jnp.int32), offline_actions], axis=0)
    episode_finished = jnp.concatenate([record_seq[3].astype(jnp.int32), offline_done], axis=0)
    sequence_length = jnp.concatenate([online_lengths, offline_lengths], axis=0)
    total_seqs = online_obs.shape[1] + owned_offline * lax.axis_size("dp")
    hidden_total = value_head.shape[0] * lax.axis_size("mp")
    objective_scale = math.sqrt(hidden_total / (total_seqs * step_count))
    value_gradient, logits_gradient = importance_trace_terms(
        value_estimates,
        policy_logits,
        reward_rows,
        behaviour_probs,
        taken_actions,
        episode_finished,
        sequence_length,
        objective_scale,
    )
    value_gradient = value_gradient * is_critic
    logits_gradient = logits_gradient * is_policy
    dv_on = value_gradient[:owned_online].T.reshape(online_count)
    dv_off = value_gradient[owned_online:].reshape(owned_offline * step_count)
    dl_on = logits_gradient[:, :owned_online].transpose(0, 2, 1).reshape(action_count, online_count)
    dl_off = logits_gradient[:, owned_online:].reshape(action_count, owned_offline * step_count)
    value_w = value_head.astype(jnp.float32)
    policy_w = policy_head.astype(jnp.float32)
    dh_on = dv_on[:, None] * value_w[None, :] + jnp.einsum(
        "ar,ha->rh", dl_on, policy_w, precision=lax.Precision.HIGHEST
    )
    dh_off = dv_off[:, None] * value_w[None, :] + jnp.einsum(
        "ar,ha->rh", dl_off, policy_w, precision=lax.Precision.HIGHEST
    )
    dz_online = (dh_on * silu_slope(pre_online)).astype(jnp.bfloat16)
    dz_offline = (dh_off * silu_slope(pre_offline)).astype(jnp.bfloat16)
    local_grad = jnp.einsum("rd,rh->dh", x_online, dz_online, preferred_element_type=jnp.float32)
    local_grad = local_grad + jnp.einsum(
        "rd,rh->dh", x_offline, dz_offline, preferred_element_type=jnp.float32
    )
    summed = lax.psum(local_grad, "dp")
    return summed[None]


HEAD_ROWS = 24
SPLIT_ROWS = 4 * HEAD_ROWS
COLUMN_BLOCK = 256
ROW_GROUPS = 4
PLACE_PARTS = 4
GRAD_CHUNKS = 8
GRAD_LEAD = 5
LANES = 128
CODE_LIMIT = 32512.0
CODE_TAIL = 16
LOG_TWO = math.log(2.0)
SCRATCH_BYTES = 6 * 1024 * 1024
SWAP = ((0, 1), (1, 0))
TO_CENTER = ((0, 1), (3, 2))
CENTER = ((1, 2), (2, 1))
FROM_CENTER = ((1, 0), (2, 3))
VMEM = pl.BlockSpec(memory_space=pltpu.VMEM)
SMEM = pl.BlockSpec(memory_space=pltpu.SMEM)


SHORT = pl.CostEstimate(flops=1, bytes_accessed=1, transcendentals=0)


def params():
    return pltpu.CompilerParams(vmem_limit_bytes=SCRATCH_BYTES)


def resident(array):
    return pltpu.with_memory_space_constraint(array, pltpu.VMEM)


def vmem_call(body, place, arrays, outs, name, deps=()):
    operands = list(arrays) + list(deps)

    def run(place_ref, *refs):
        body(place_ref, *refs[: len(arrays)], *refs[len(operands) :])

    return pl.pallas_call(
        run,
        in_specs=[SMEM] + [VMEM] * len(operands),
        out_specs=[VMEM] * len(outs),
        out_shape=[pltpu.VMEM(shape, dtype) for shape, dtype in outs],
        compiler_params=params(),
        cost_estimate=SHORT,
        name=name,
    )(place, *[resident(x) for x in operands])


def own_half_body(place, own_ref, weight_ref, out_ref):
    groups, width, features = own_ref.shape
    at = pl.multiple_of(place[0] * features, features)
    for first in range(0, groups, ROW_GROUPS):
        part = slice(first, first + ROW_GROUPS)
        own = own_ref[part].reshape(-1, features)
        for h in range(0, weight_ref.shape[1], COLUMN_BLOCK):
            block = slice(h, h + COLUMN_BLOCK)
            pre = jnp.dot(
                own, weight_ref[pl.ds(at, features), block], preferred_element_type=jnp.float32
            )
            out_ref[part, :, block] = pre.reshape(-1, width, COLUMN_BLOCK)


def own_half(place, own, weight, deps):
    groups, width, _ = own.shape
    return vmem_call(
        own_half_body,
        place,
        [own, weight],
        [((groups, width, weight.shape[1]), jnp.float32)],
        "own_half",
        deps,
    )[0]


def forward_body(place, pre_ref, got_ref, rest_ref, weight_ref, head_ref, *refs):
    slope_ref, heads_ref, hidden_ref = refs[-3:]
    half, width, features = got_ref.shape
    hidden_count = weight_ref.shape[1]
    m, section = place[0], place[3]
    other_at = pl.multiple_of((1 - m) * features, features)
    count = min(half, ROW_GROUPS)
    for x_ref, start in ((got_ref, section * half), (rest_ref, (1 - section) * half)):
        for first in range(0, half, count):
            at = pl.ds(start + first, count)
            other = x_ref[first : first + count].reshape(-1, features)
            for h in range(0, hidden_count, COLUMN_BLOCK):
                block = slice(h, h + COLUMN_BLOCK)
                pre = jnp.dot(
                    other,
                    weight_ref[pl.ds(other_at, features), block],
                    preferred_element_type=jnp.float32,
                )
                pre = pre + pre_ref[at, :, block].reshape(-1, COLUMN_BLOCK)
                sigma = 0.5 * jnp.tanh(0.5 * pre) + 0.5
                hidden = pre * sigma
                slope = sigma + hidden * (1.0 - sigma)
                slope_ref[at, :, block] = slope.reshape(-1, width, COLUMN_BLOCK)
                hidden_ref[:, block] = hidden.astype(jnp.bfloat16)
            for g in range(count):
                heads = lax.dot_general(
                    head_ref[...],
                    hidden_ref[g * width : (g + 1) * width],
                    (((1,), (1,)), ((), ())),
                    preferred_element_type=jnp.float32,
                )
                heads_ref[start + first + g] = heads[:HEAD_ROWS]


def forward(place, pre, got, rest, weight, head, deps):
    groups, width, hidden_count = pre.shape
    operands = [pre, got, rest, weight, head] + deps
    return pl.pallas_call(
        forward_body,
        in_specs=[SMEM] + [VMEM] * len(operands),
        out_specs=[VMEM, VMEM],
        out_shape=[
            pltpu.VMEM(pre.shape, jnp.float32),
            pltpu.VMEM((groups, HEAD_ROWS, width), jnp.float32),
        ],
        scratch_shapes=[
            pltpu.VMEM((min(groups // 2, ROW_GROUPS) * width, hidden_count), jnp.bfloat16)
        ],
        input_output_aliases={1: 0},
        compiler_params=params(),
        cost_estimate=SHORT,
        name="forward_rows",
    )(place, *[resident(x) for x in operands])


def action_terms(parts, actions, behaviour, action_count):
    heads = parts[0] + parts[1] + (parts[2] + parts[3])
    row = lax.broadcasted_iota(jnp.int32, heads.shape, 0)
    is_logit = row < action_count
    logits = jnp.where(is_logit, heads, -1e30)
    shifted = logits - jnp.max(logits, axis=0, keepdims=True)
    log_sum = jnp.log(jnp.sum(jnp.exp(shifted), axis=0, keepdims=True))
    log_probs = shifted - log_sum
    taken = row == actions
    chosen = jnp.sum(jnp.where(taken, log_probs, 0.0), axis=0, keepdims=True)
    rho = jnp.exp(jnp.minimum(chosen - behaviour, 0.0))
    spread = jnp.where(is_logit, jnp.exp(log_probs) - taken.astype(jnp.float32), 0.0)
    return heads[action_count : action_count + 1], rho, spread


def trace_terms(value, rho, reward, discount, length, position, axis, reach, scale):
    size = value.shape[axis]
    valid = (position < length).astype(jnp.float32)
    valid_next = (position + 1 < length).astype(jnp.float32)
    next_value = pltpu.roll(value, size - 1, axis) * valid_next
    correction = valid * rho * (reward + discount * next_value - value)
    coef = discount * TRACE_LAMBDA * rho * valid_next
    shift = 1
    while shift < reach:
        correction = correction + coef * pltpu.roll(correction, size - shift, axis)
        coef = coef * pltpu.roll(coef, size - shift, axis)
        shift *= 2
    targets = value + correction
    next_target = pltpu.roll(targets, size - 1, axis) * valid_next
    advantage = rho * (reward + discount * next_target - value)
    return -scale * valid * correction, scale * (valid * advantage)


def split_terms(logit_weight, value_weight, spread, action_count):
    row = lax.broadcasted_iota(jnp.int32, spread.shape, 0)
    full = jnp.where(row == action_count, value_weight, logit_weight * spread)
    high = full.astype(jnp.bfloat16).astype(jnp.float32)
    rest = full - high
    middle = rest.astype(jnp.bfloat16).astype(jnp.float32)
    low = rest - middle
    return jnp.concatenate([high, middle, low, jnp.zeros_like(full)], axis=0).astype(jnp.bfloat16)


def write_back(terms, head_ref, slope, dz_ref, g):
    dh = lax.dot_general(
        terms, head_ref[...], (((0,), (0,)), ((), ())), preferred_element_type=jnp.float32
    )
    dz_ref[g] = (dh * slope).astype(jnp.bfloat16)


def online_heads_body(action_count, place, *refs):
    parts = refs[:4]
    actions, behaviour, reward, done, lengths, pack_ref, spread_ref = refs[4:]
    steps = actions.shape[0]
    for t in range(steps):
        value, rho, spread = action_terms(
            [p[t] for p in parts],
            actions[t : t + 1, :],
            behaviour[t : t + 1, :],
            action_count,
        )
        pack_ref[t : t + 1, :] = value
        pack_ref[steps + t : steps + t + 1, :] = rho
        spread_ref[t] = spread
    pack_ref[2 * steps : 3 * steps, :] = reward[...]
    pack_ref[3 * steps : 4 * steps, :] = DISCOUNT_RATE * (1.0 - done[...].astype(jnp.float32))
    pack_ref[4 * steps :, :] = jnp.broadcast_to(lengths[...], (8, lengths.shape[1]))


def online_back_body(action_count, scale, place, *refs):
    blocks, spread, head_ref, slope_ref, dz_ref = refs[:4], *refs[4:]
    steps = spread.shape[0]
    z = place[2]

    def field(i):
        parts = []
        for hop, b in enumerate(blocks):
            part = b[i * steps : (i + 1) * steps, :]
            parts.append(jnp.where(z + hop < len(blocks), part, 0.0) if hop else part)
        return jnp.concatenate(parts, axis=0)

    length = sum(b[4 * steps : 4 * steps + 1, :] for b in blocks).astype(jnp.int32)
    value = field(0)
    position = lax.broadcasted_iota(jnp.int32, value.shape, 0) + z * steps
    value_weight, logit_weight = trace_terms(
        value,
        field(1),
        field(2),
        field(3),
        length,
        position,
        0,
        value.shape[0],
        scale,
    )
    for t in range(steps):
        terms = split_terms(
            logit_weight[t : t + 1, :], value_weight[t : t + 1, :], spread[t], action_count
        )
        write_back(terms, head_ref, slope_ref[t], dz_ref, t)


def offline_back_body(action_count, step_count, scale, place, *refs):
    parts = refs[:4]
    actions, behaviour, reward, done, length, head_ref, slope_ref, dz_ref = refs[4:]
    groups = dz_ref.shape[0]
    values, rhos, spreads = [], [], []
    for g in range(groups):
        value, rho, spread = action_terms(
            [p[g] for p in parts],
            actions[g : g + 1, :],
            behaviour[g : g + 1, :],
            action_count,
        )
        values.append(value)
        rhos.append(rho)
        spreads.append(spread)
    value = jnp.concatenate(values, axis=0)
    rho = jnp.concatenate(rhos, axis=0)
    position = lax.rem(lax.broadcasted_iota(jnp.int32, value.shape, 1), step_count)
    discount = DISCOUNT_RATE * (1.0 - done[...].astype(jnp.float32))
    value_weight, logit_weight = trace_terms(
        value, rho, reward[...], discount, length[...], position, 1, step_count, scale
    )
    for g in range(groups):
        terms = split_terms(
            logit_weight[g : g + 1, :], value_weight[g : g + 1, :], spreads[g], action_count
        )
        write_back(terms, head_ref, slope_ref[g], dz_ref, g)


def encode(v, c, message_ref):
    rows = v.shape[0]
    largest = jnp.max(jnp.abs(v), axis=0, keepdims=True)
    exponent = jnp.ceil(jnp.log(jnp.maximum(largest, 1e-30)) * (1.0 / LOG_TWO) + 0.01)
    scale = jnp.exp(exponent * -LOG_TWO) * CODE_LIMIT
    code = jnp.floor(v * scale + 0.5)
    message_ref[c * rows : (c + 1) * rows, :] = code.astype(jnp.int32).astype(jnp.int16)
    return exponent


def encode_tail(exponents, message_ref):
    fill = [jnp.zeros_like(exponents[0])] * (CODE_TAIL - len(exponents))
    tail = jnp.concatenate(exponents + fill, axis=0).astype(jnp.int32)
    message_ref[message_ref.shape[0] - CODE_TAIL :, :] = tail.astype(jnp.int16)


def decoder(message_ref, count):
    rows = (message_ref.shape[0] - CODE_TAIL) // count
    exponents = message_ref[count * rows :, :].astype(jnp.int32).astype(jnp.float32)
    steps = jnp.exp(exponents * LOG_TWO) * (1.0 / CODE_LIMIT)

    def block(c, first=0, size=rows):
        at = slice(c * rows + first, c * rows + first + size)
        code = message_ref[at, :].astype(jnp.int32).astype(jnp.float32)
        return code * steps[c : c + 1, :]

    return block


def message_of(rows, columns):
    return ((rows * (columns // LANES) + CODE_TAIL, LANES), jnp.int16)


def grad_body(pieces, column, columns, place, *refs):
    xs, dzs = refs[: len(pieces)], refs[len(pieces) : len(pieces) + 2]
    message_ref = refs[-1]
    hidden_count = dzs[0].shape[2]
    section = place[3]
    exponents = []
    at = slice(column * columns, (column + 1) * columns)
    for h in range(0, hidden_count, COLUMN_BLOCK):
        total = None
        for x, (which, swapped) in zip(xs, pieces):
            groups, width, _ = x.shape
            first = 0
            if swapped is not None:
                first = (1 - section if swapped else section) * groups
            part = lax.dot_general(
                x[:, :, at].reshape(groups * width, columns),
                dzs[which][pl.ds(first, groups), :, h : h + COLUMN_BLOCK].reshape(
                    groups * width, COLUMN_BLOCK
                ),
                (((0,), (0,)), ((), ())),
                preferred_element_type=jnp.float32,
            )
            total = part if total is None else total + part
        for c in range(COLUMN_BLOCK // LANES):
            block = total[:, c * LANES : (c + 1) * LANES]
            exponents.append(encode(block, h // LANES + c, message_ref))
    encode_tail(exponents, message_ref)


def grad_chunk(place, pieces, dzs, column, columns, deps):
    hidden_count = dzs[0].shape[2]
    return vmem_call(
        functools.partial(grad_body, [p[1:] for p in pieces], column, columns),
        place,
        [x for x, _, _ in pieces] + dzs,
        [message_of(columns, hidden_count)],
        "grad_chunk",
        deps,
    )[0]


def add_body(count, place, *refs):
    first, second = decoder(refs[0], count), decoder(refs[1], count)
    out = refs[-1]
    encode_tail([encode(first(c) + second(c), c, out) for c in range(count)], out)


def add_chunk(place, a, b, count, deps):
    return vmem_call(
        functools.partial(add_body, count),
        place,
        [a, b],
        [(a.shape, a.dtype)],
        "add_chunk",
        deps,
    )[0]


def place_body(count, rows, of_own, index, place, total, received, *refs):
    out, token, held, sems = refs[-4:]
    token[...] = jnp.zeros_like(token)
    half = place[0] if of_own else 1 - place[0]
    first = pl.multiple_of(half * (out.shape[0] // 2) + index * rows, rows)
    at_end = place[1] == 1
    part = rows // PLACE_PARTS

    def copies(i):
        here = slice(i * part, (i + 1) * part)
        return pltpu.make_async_copy(
            held.at[here], out.at[pl.ds(first + i * part, part)], sems.at[i]
        )

    def write(message):
        block = decoder(message, count)
        for i in range(PLACE_PARTS):
            here = slice(i * part, (i + 1) * part)
            for c in range(count):
                held[here, c * LANES : (c + 1) * LANES] = block(c, i * part, part)
            copies(i).start()

    @pl.when(at_end)
    def _():
        write(received)

    @pl.when(jnp.logical_not(at_end))
    def _():
        write(total)

    for i in range(PLACE_PARTS):
        copies(i).wait()


def place_chunk(place, total, received, result, of_own, index, rows, shape, deps):
    hidden_count = shape[1]
    earlier = [] if result is None else [result]
    operands = [total, received] + deps
    return pl.pallas_call(
        functools.partial(place_body, hidden_count // LANES, rows, of_own, index),
        in_specs=[SMEM]
        + [VMEM] * len(operands)
        + [pl.BlockSpec(memory_space=pl.ANY) for _ in earlier],
        out_specs=[pl.BlockSpec(memory_space=pl.ANY), VMEM],
        out_shape=[
            jax.ShapeDtypeStruct(shape, jnp.float32),
            pltpu.VMEM((8, LANES), jnp.float32),
        ],
        scratch_shapes=[
            pltpu.VMEM((rows, hidden_count), jnp.float32),
            pltpu.SemaphoreType.DMA((PLACE_PARTS,)),
        ],
        input_output_aliases={1 + len(operands): 0} if earlier else {},
        compiler_params=params(),
        cost_estimate=SHORT,
        name="place_chunk",
    )(place, *[resident(x) for x in operands], *earlier)


def pipeline_order(count, lead):
    order = [("grad", k) for k in range(min(lead, count))]
    ahead = len(order)
    for k in range(count + 3):
        if k < count:
            order.append(("partial", k))
            while ahead < min(count, lead + 2 * (k + 1)):
                order.append(("grad", ahead))
                ahead += 1
        if 0 <= k - 3 < count:
            order.append(("place", k - 3))
        if 0 <= k - 1 < count:
            order.append(("total", k - 1))
    return order


def after(array, *others):
    return lax.optimization_barrier((array,) + others)[0]


def chip_pair(part, gate=()):
    across = lax.ppermute(part, "mp", SWAP)
    return [
        part,
        lax.ppermute(part, "section", SWAP),
        across,
        lax.ppermute(after(across, *gate), "section", SWAP),
    ]


def line_plan(
    online_obs,
    offline_obs,
    online_rewards,
    offline_rewards,
    online_behaviour,
    offline_behaviour,
    online_actions,
    offline_actions,
    online_done,
    offline_done,
    online_lengths,
    offline_lengths,
    torso_weights,
    value_head,
    policy_head,
):
    section = lax.axis_index("section")
    m = lax.axis_index("mp")
    z = lax.axis_index("dp")
    dp = lax.axis_size("dp")
    steps, online_count, features = online_obs.shape
    offline_count, step_count, _ = offline_obs.shape
    action_count = policy_head.shape[1]
    hidden_count = value_head.shape[0]
    at_end = ((z == 0) | (z == dp - 1)).astype(jnp.int32)
    place = jnp.stack([m, at_end, z, section]).astype(jnp.int32)
    weight = torso_weights[0]
    scale = math.sqrt(
        hidden_count
        * lax.axis_size("mp")
        / ((online_count + offline_count * dp) * step_count)
    )

    offline_groups = offline_count // 2
    offline_rows = offline_obs.reshape(offline_groups, 2 * step_count, features)
    own = [online_obs, offline_rows]
    halves = [
        lax.dynamic_slice_in_dim(x, section * (x.shape[0] // 2), x.shape[0] // 2, axis=0)
        for x in own
    ]

    policy_rows = jnp.where(section == 1, policy_head.T, 0)
    value_row = jnp.where(section == 0, value_head[None], 0)
    head = jnp.concatenate([policy_rows, value_row], axis=0).astype(jnp.bfloat16)
    head = jnp.pad(head, ((0, HEAD_ROWS - action_count - 1), (0, 0)))
    forward_head = jnp.pad(head, ((0, 32 - HEAD_ROWS), (0, 0)))
    back_head = jnp.concatenate([head, head, head, jnp.zeros_like(head)], axis=0)

    owned = online_lengths.shape[0]
    length_row = lax.dynamic_update_slice(
        jnp.zeros((online_count,), jnp.float32), online_lengths.astype(jnp.float32), (z * owned,)
    )
    length_row = length_row[None]
    lanes = (offline_groups, 2 * step_count)
    offline_length = jnp.broadcast_to(offline_lengths[:, None], (offline_count, step_count))
    offline_terms = [
        x.reshape(lanes)
        for x in (
            offline_actions,
            offline_behaviour,
            offline_rewards,
            offline_done,
            offline_length,
        )
    ]

    got = [lax.ppermute(half, "mp", SWAP) for half in halves]
    early = halves + [back_head, forward_head, length_row] + offline_terms
    pre_online = own_half(place, online_obs, weight, early)
    pre_offline = own_half(place, offline_rows, weight, [pre_online])
    rests = [lax.ppermute(after(got[0], pre_offline), "section", SWAP)]
    online_slope, online_part = forward(
        place, pre_online, got[0], rests[0], weight, forward_head, []
    )
    rests.append(lax.ppermute(after(got[1], online_part), "section", SWAP))
    offline_slope, offline_part = forward(
        place, pre_offline, got[1], rests[1], weight, forward_head, [online_part]
    )
    offline_parts = chip_pair(offline_part, [])
    pack, spread = vmem_call(
        functools.partial(online_heads_body, action_count),
        place,
        chip_pair(online_part, [offline_part, offline_parts[2]])
        + [online_actions, online_behaviour, online_rewards, online_done, length_row],
        [
            ((4 * steps + 8, online_count), jnp.float32),
            ((steps, HEAD_ROWS, online_count), jnp.float32),
        ],
        "online_heads",
        [offline_part],
    )

    (dz_offline,) = vmem_call(
        functools.partial(offline_back_body, action_count, step_count, scale),
        place,
        offline_parts + offline_terms + [back_head, offline_slope],
        [(offline_slope.shape, jnp.bfloat16)],
        "offline_back",
        [pack],
    )

    blocks = [pack]
    for hop in range(1, dp):
        pairs = [(i, (i - hop) % dp) for i in range(dp)]
        blocks.append(lax.ppermute(pack, "dp", pairs))
    (dz_online,) = vmem_call(
        functools.partial(online_back_body, action_count, scale),
        place,
        blocks + [spread, back_head, online_slope],
        [(online_slope.shape, jnp.bfloat16)],
        "online_back",
        [dz_offline],
    )

    own_x = [(online_obs, 0, None), (offline_rows, 1, None)]
    other_x = []
    for which in range(2):
        other_x += [(got[which], which, 0), (rests[which], which, 1)]
    columns = 2 * features // GRAD_CHUNKS
    per_half = GRAD_CHUNKS // 2
    lane_blocks = hidden_count // LANES

    messages, inward, partial, across, total, outward = {}, {}, {}, {}, {}, {}
    result, last = None, dz_online
    for kind, k in pipeline_order(GRAD_CHUNKS, GRAD_LEAD):
        if kind == "grad":
            last = messages[k] = grad_chunk(
                place,
                own_x if k < per_half else other_x,
                [dz_online, dz_offline],
                k % per_half,
                columns,
                [last],
            )
            inward[k] = lax.ppermute(last, "dp", TO_CENTER)
        elif kind == "partial":
            last = partial[k] = add_chunk(place, messages[k], inward[k], lane_blocks, [last])
            across[k] = lax.ppermute(last, "dp", CENTER)
        elif kind == "total":
            last = total[k] = add_chunk(place, partial[k], across[k], lane_blocks, [last])
            outward[k] = lax.ppermute(last, "dp", FROM_CENTER)
        else:
            result, last = place_chunk(
                place,
                total[k],
                outward[k],
                result,
                k < per_half,
                k % per_half,
                columns,
                (2 * features, hidden_count),
                [last],
            )
    return result[None]


def solution(mesh):
    on_line = mesh.shape["dp"] == 4 and mesh.shape["mp"] == 2 and mesh.shape["section"] == 2
    in_specs = (
        P("dp", "groups", "mp"),
        P(("groups", "dp"), None, "mp"),
        P("dp", "groups"),
        P(("groups", "dp"), None),
        P("dp", "groups"),
        P(("groups", "dp"), None),
        P("dp", "groups"),
        P(("groups", "dp"), None),
        P("dp", "groups"),
        P(("groups", "dp"), None),
        P(("groups", "dp")),
        P(("groups", "dp")),
        P("section", None, "mp"),
        P("mp"),
        P("mp", None),
    )
    out_specs = P(("groups", "section"), None, "mp")
    per_device = line_plan if on_line else general_plan
    return jax.shard_map(
        per_device, mesh=mesh, in_specs=in_specs, out_specs=out_specs, check_vma=False
    )
```

```python
import functools
import math

import jax
import jax.numpy as jnp
from jax import lax
from jax.experimental import pallas as pl
from jax.experimental.pallas import tpu as pltpu
from jax.sharding import PartitionSpec as P

DISCOUNT_RATE = 0.99
TRACE_LAMBDA = 0.95


def silu_slope(pre):
    sigma = jax.nn.sigmoid(pre)
    return sigma * (1.0 + pre * (1.0 - sigma))


def importance_trace_terms(
    value_estimates,
    policy_logits,
    reward_rows,
    behaviour_probs,
    taken_actions,
    episode_finished,
    sequence_length,
    objective_scale,
):
    seq_count, step_count = value_estimates.shape
    action_count = policy_logits.shape[0]
    positions = jnp.arange(step_count, dtype=jnp.int32)
    valid_mask = (positions[None, :] < sequence_length[:, None]).astype(jnp.float32)
    zero_column = jnp.zeros((seq_count, 1), jnp.float32)
    valid_next = jnp.concatenate([valid_mask[:, 1:], zero_column], axis=1)
    log_probs = jax.nn.log_softmax(policy_logits, axis=0)
    one_hot = (
        jnp.arange(action_count, dtype=jnp.int32)[:, None, None] == taken_actions[None]
    ).astype(jnp.float32)
    chosen = jnp.sum(one_hot * log_probs, axis=0)
    clip_ratio = jnp.exp(jnp.minimum(chosen - behaviour_probs, 0.0))
    discount = DISCOUNT_RATE * (1.0 - episode_finished.astype(jnp.float32))
    next_value = jnp.concatenate([value_estimates[:, 1:], zero_column], axis=1) * valid_next
    td_error = valid_mask * clip_ratio * (reward_rows + discount * next_value - value_estimates)
    trace_coef = discount * TRACE_LAMBDA * clip_ratio * valid_next

    def backward_step(carried, inputs):
        error_now, coef_now = inputs
        updated = error_now + coef_now * carried
        return (updated, updated)

    final_state, stacked = lax.scan(
        backward_step,
        jnp.zeros((seq_count,), jnp.float32),
        (td_error.T, trace_coef.T),
        reverse=True,
    )
    correction = stacked.T
    targets = value_estimates + correction
    next_target = jnp.concatenate([targets[:, 1:], zero_column], axis=1) * valid_next
    policy_adv = clip_ratio * (reward_rows + discount * next_target - value_estimates)
    value_gradient = -objective_scale * valid_mask * correction
    logits_gradient = (
        objective_scale * (valid_mask * policy_adv)[None] * (jnp.exp(log_probs) - one_hot)
    )
    return (value_gradient, logits_gradient)


def head_terms(hidden, value_w, policy_w):
    logit_part = jnp.einsum("rh,ha->ar", hidden, policy_w, preferred_element_type=jnp.float32)
    value_part = jnp.dot(hidden, value_w, preferred_element_type=jnp.float32)
    return jnp.concatenate([logit_part, value_part[None]], axis=0)


def full_rows(online_part, offline_part):
    return (
        lax.all_gather(online_part, "mp", axis=2, tiled=True),
        lax.all_gather(offline_part, "mp", axis=2, tiled=True),
    )


def general_plan(
    online_obs,
    offline_obs,
    online_rewards,
    offline_rewards,
    online_behaviour,
    offline_behaviour,
    online_actions,
    offline_actions,
    online_done,
    offline_done,
    online_lengths,
    offline_lengths,
    torso_weights,
    value_head,
    policy_head,
):
    owned_online = online_lengths.shape[0]
    owned_offline = offline_obs.shape[0]
    step_count = offline_obs.shape[1]
    action_count = policy_head.shape[1]
    record_stack = jnp.stack(
        [
            online_rewards,
            online_behaviour,
            online_actions.astype(jnp.float32),
            online_done.astype(jnp.float32),
        ]
    )
    records = lax.all_to_all(record_stack, "dp", split_axis=2, concat_axis=1, tiled=True)
    slabs = lax.all_to_all(online_obs, "dp", split_axis=1, concat_axis=0, tiled=True)
    x_online, x_offline = full_rows(slabs, offline_obs)
    feature_count = x_online.shape[2]
    x_online = x_online.reshape(step_count * owned_online, feature_count)
    x_offline = x_offline.reshape(owned_offline * step_count, feature_count)
    weight = torso_weights[0]
    pre_online = jnp.dot(x_online, weight, preferred_element_type=jnp.float32)
    pre_offline = jnp.dot(x_offline, weight, preferred_element_type=jnp.float32)
    hidden_online = jax.nn.silu(pre_online).astype(jnp.bfloat16)
    hidden_offline = jax.nn.silu(pre_offline).astype(jnp.bfloat16)
    is_critic = (lax.axis_index("section") == 0).astype(jnp.float32)
    is_policy = 1.0 - is_critic
    row_keep = jnp.where(jnp.arange(action_count + 1) == action_count, is_critic, is_policy)
    partial_value = jnp.concatenate(
        [
            head_terms(hidden_online, value_head, policy_head),
            head_terms(hidden_offline, value_head, policy_head),
        ],
        axis=1,
    )
    partial_value = partial_value * row_keep[:, None]
    heads = lax.psum(partial_value, ("mp", "section"))
    online_count = step_count * owned_online
    logits_on = (
        heads[:action_count, :online_count]
        .reshape(action_count, step_count, owned_online)
        .transpose(0, 2, 1)
    )
    logits_off = heads[:action_count, online_count:].reshape(
        action_count, owned_offline, step_count
    )
    values_on = heads[action_count, :online_count].reshape(step_count, owned_online).T
    values_off = heads[action_count, online_count:].reshape(owned_offline, step_count)
    record_seq = records.transpose(0, 2, 1)
    value_estimates = jnp.concatenate([values_on, values_off], axis=0)
    policy_logits = jnp.concatenate([logits_on, logits_off], axis=1)
    reward_rows = jnp.concatenate([record_seq[0], offline_rewards], axis=0)
    behaviour_probs = jnp.concatenate([record_seq[1], offline_behaviour], axis=0)
    taken_actions = jnp.concatenate([record_seq[2].astype(jnp.int32), offline_actions], axis=0)
    episode_finished = jnp.concatenate([record_seq[3].astype(jnp.int32), offline_done], axis=0)
    sequence_length = jnp.concatenate([online_lengths, offline_lengths], axis=0)
    total_seqs = online_obs.shape[1] + owned_offline * lax.axis_size("dp")
    hidden_total = value_head.shape[0] * lax.axis_size("mp")
    objective_scale = math.sqrt(hidden_total / (total_seqs * step_count))
    value_gradient, logits_gradient = importance_trace_terms(
        value_estimates,
        policy_logits,
        reward_rows,
        behaviour_probs,
        taken_actions,
        episode_finished,
        sequence_length,
        objective_scale,
    )
    value_gradient = value_gradient * is_critic
    logits_gradient = logits_gradient * is_policy
    dv_on = value_gradient[:owned_online].T.reshape(online_count)
    dv_off = value_gradient[owned_online:].reshape(owned_offline * step_count)
    dl_on = logits_gradient[:, :owned_online].transpose(0, 2, 1).reshape(action_count, online_count)
    dl_off = logits_gradient[:, owned_online:].reshape(action_count, owned_offline * step_count)
    value_w = value_head.astype(jnp.float32)
    policy_w = policy_head.astype(jnp.float32)
    dh_on = dv_on[:, None] * value_w[None, :] + jnp.einsum(
        "ar,ha->rh", dl_on, policy_w, precision=lax.Precision.HIGHEST
    )
    dh_off = dv_off[:, None] * value_w[None, :] + jnp.einsum(
        "ar,ha->rh", dl_off, policy_w, precision=lax.Precision.HIGHEST
    )
    dz_online = (dh_on * silu_slope(pre_online)).astype(jnp.bfloat16)
    dz_offline = (dh_off * silu_slope(pre_offline)).astype(jnp.bfloat16)
    local_grad = jnp.einsum("rd,rh->dh", x_online, dz_online, preferred_element_type=jnp.float32)
    local_grad = local_grad + jnp.einsum(
        "rd,rh->dh", x_offline, dz_offline, preferred_element_type=jnp.float32
    )
    summed = lax.psum(local_grad, "dp")
    return summed[None]


HEAD_ROWS = 24
SPLIT_ROWS = 4 * HEAD_ROWS
COLUMN_BLOCK = 256
GRAD_BLOCK = 512
ADD_BLOCKS = 2
ROW_GROUPS = 4
GRAD_CHUNKS = 8
GRAD_LEAD = 5
LANES = 128
CODE_LIMIT = 32512.0
CODE_TAIL = 16
LOG_TWO = math.log(2.0)
SCRATCH_BYTES = 6 * 1024 * 1024
SWAP = ((0, 1), (1, 0))
TO_CENTER = ((0, 1), (3, 2))
CENTER = ((1, 2), (2, 1))
FROM_CENTER = ((1, 0), (2, 3))
VMEM = pl.BlockSpec(memory_space=pltpu.VMEM)
SMEM = pl.BlockSpec(memory_space=pltpu.SMEM)
EXPONENTS = pltpu.VMEM((CODE_TAIL, LANES), jnp.float32)


SHORT = pl.CostEstimate(flops=1, bytes_accessed=1, transcendentals=0)


def params():
    return pltpu.CompilerParams(vmem_limit_bytes=SCRATCH_BYTES)


def resident(array):
    return pltpu.with_memory_space_constraint(array, pltpu.VMEM)


def vmem_call(body, place, arrays, outs, name, deps=(), scratch=()):
    operands = list(arrays) + list(deps)

    def run(place_ref, *refs):
        body(place_ref, *refs[: len(arrays)], *refs[len(operands) :])

    return pl.pallas_call(
        run,
        in_specs=[SMEM] + [VMEM] * len(operands),
        out_specs=[VMEM] * len(outs),
        out_shape=[pltpu.VMEM(shape, dtype) for shape, dtype in outs],
        scratch_shapes=list(scratch),
        compiler_params=params(),
        cost_estimate=SHORT,
        name=name,
    )(place, *[resident(x) for x in operands])


def own_half_body(place, own_ref, weight_ref, out_ref):
    groups, width, features = own_ref.shape
    at = pl.multiple_of(place[0] * features, features)
    for first in range(0, groups, ROW_GROUPS):
        part = slice(first, first + ROW_GROUPS)
        own = own_ref[part].reshape(-1, features)
        for h in range(0, weight_ref.shape[1], COLUMN_BLOCK):
            block = slice(h, h + COLUMN_BLOCK)
            pre = jnp.dot(
                own, weight_ref[pl.ds(at, features), block], preferred_element_type=jnp.float32
            )
            out_ref[part, :, block] = pre.reshape(-1, width, COLUMN_BLOCK)


def own_half(place, own, weight, deps):
    groups, width, _ = own.shape
    return vmem_call(
        own_half_body,
        place,
        [own, weight],
        [((groups, width, weight.shape[1]), jnp.float32)],
        "own_half",
        deps,
    )[0]


def forward_body(place, pre_ref, got_ref, rest_ref, weight_ref, head_ref, *refs):
    slope_ref, heads_ref, hidden_ref = refs[-3:]
    half, width, features = got_ref.shape
    hidden_count = weight_ref.shape[1]
    m, section = place[0], place[3]
    other_at = pl.multiple_of((1 - m) * features, features)
    count = min(half, ROW_GROUPS)
    for x_ref, start in ((got_ref, section * half), (rest_ref, (1 - section) * half)):
        for first in range(0, half, count):
            at = pl.ds(start + first, count)
            other = x_ref[first : first + count].reshape(-1, features)
            for h in range(0, hidden_count, COLUMN_BLOCK):
                block = slice(h, h + COLUMN_BLOCK)
                pre = jnp.dot(
                    other,
                    weight_ref[pl.ds(other_at, features), block],
                    preferred_element_type=jnp.float32,
                )
                pre = pre + pre_ref[at, :, block].reshape(-1, COLUMN_BLOCK)
                sigma = 0.5 * jnp.tanh(0.5 * pre) + 0.5
                hidden = pre * sigma
                slope = sigma + hidden * (1.0 - sigma)
                slope_ref[at, :, block] = slope.reshape(-1, width, COLUMN_BLOCK)
                hidden_ref[:, block] = hidden.astype(jnp.bfloat16)
            for g in range(count):
                heads = lax.dot_general(
                    head_ref[...],
                    hidden_ref[g * width : (g + 1) * width],
                    (((1,), (1,)), ((), ())),
                    preferred_element_type=jnp.float32,
                )
                heads_ref[start + first + g] = heads[:HEAD_ROWS]


def forward(place, pre, got, rest, weight, head, deps):
    groups, width, hidden_count = pre.shape
    operands = [pre, got, rest, weight, head] + deps
    return pl.pallas_call(
        forward_body,
        in_specs=[SMEM] + [VMEM] * len(operands),
        out_specs=[VMEM, VMEM],
        out_shape=[
            pltpu.VMEM(pre.shape, jnp.float32),
            pltpu.VMEM((groups, HEAD_ROWS, width), jnp.float32),
        ],
        scratch_shapes=[
            pltpu.VMEM((min(groups // 2, ROW_GROUPS) * width, hidden_count), jnp.bfloat16)
        ],
        input_output_aliases={1: 0},
        compiler_params=params(),
        cost_estimate=SHORT,
        name="forward_rows",
    )(place, *[resident(x) for x in operands])


def action_terms(parts, actions, behaviour, action_count):
    heads = parts[0] + parts[1] + (parts[2] + parts[3])
    row = lax.broadcasted_iota(jnp.int32, heads.shape, 0)
    is_logit = row < action_count
    logits = jnp.where(is_logit, heads, -1e30)
    shifted = logits - jnp.max(logits, axis=0, keepdims=True)
    log_sum = jnp.log(jnp.sum(jnp.exp(shifted), axis=0, keepdims=True))
    log_probs = shifted - log_sum
    taken = row == actions
    chosen = jnp.sum(jnp.where(taken, log_probs, 0.0), axis=0, keepdims=True)
    rho = jnp.exp(jnp.minimum(chosen - behaviour, 0.0))
    spread = jnp.where(is_logit, jnp.exp(log_probs) - taken.astype(jnp.float32), 0.0)
    return heads[action_count : action_count + 1], rho, spread


def trace_terms(value, rho, reward, discount, length, position, axis, reach, scale):
    size = value.shape[axis]
    valid = (position < length).astype(jnp.float32)
    valid_next = (position + 1 < length).astype(jnp.float32)
    next_value = pltpu.roll(value, size - 1, axis) * valid_next
    correction = valid * rho * (reward + discount * next_value - value)
    coef = discount * TRACE_LAMBDA * rho * valid_next
    shift = 1
    while shift < reach:
        correction = correction + coef * pltpu.roll(correction, size - shift, axis)
        coef = coef * pltpu.roll(coef, size - shift, axis)
        shift *= 2
    targets = value + correction
    next_target = pltpu.roll(targets, size - 1, axis) * valid_next
    advantage = rho * (reward + discount * next_target - value)
    return -scale * valid * correction, scale * (valid * advantage)


def split_terms(logit_weight, value_weight, spread, action_count):
    row = lax.broadcasted_iota(jnp.int32, spread.shape, 0)
    full = jnp.where(row == action_count, value_weight, logit_weight * spread)
    high = full.astype(jnp.bfloat16).astype(jnp.float32)
    rest = full - high
    middle = rest.astype(jnp.bfloat16).astype(jnp.float32)
    low = rest - middle
    return jnp.concatenate([high, middle, low, jnp.zeros_like(full)], axis=0).astype(jnp.bfloat16)


def write_back(terms, head_ref, slope, dz_ref, g):
    dh = lax.dot_general(
        terms, head_ref[...], (((0,), (0,)), ((), ())), preferred_element_type=jnp.float32
    )
    dz_ref[g] = (dh * slope).astype(jnp.bfloat16)


def online_heads_body(action_count, place, *refs):
    parts = refs[:4]
    actions, behaviour, reward, done, lengths, pack_ref, spread_ref = refs[4:]
    steps = actions.shape[0]
    for t in range(steps):
        value, rho, spread = action_terms(
            [p[t] for p in parts],
            actions[t : t + 1, :],
            behaviour[t : t + 1, :],
            action_count,
        )
        pack_ref[t : t + 1, :] = value
        pack_ref[steps + t : steps + t + 1, :] = rho
        spread_ref[t] = spread
    pack_ref[2 * steps : 3 * steps, :] = reward[...]
    pack_ref[3 * steps : 4 * steps, :] = DISCOUNT_RATE * (1.0 - done[...].astype(jnp.float32))
    pack_ref[4 * steps :, :] = jnp.broadcast_to(lengths[...], (8, lengths.shape[1]))


def online_back_body(action_count, scale, place, *refs):
    blocks, spread, head_ref, slope_ref, dz_ref = refs[:4], *refs[4:]
    steps = spread.shape[0]
    z = place[2]

    def field(i):
        parts = []
        for hop, b in enumerate(blocks):
            part = b[i * steps : (i + 1) * steps, :]
            parts.append(jnp.where(z + hop < len(blocks), part, 0.0) if hop else part)
        return jnp.concatenate(parts, axis=0)

    length = sum(b[4 * steps : 4 * steps + 1, :] for b in blocks).astype(jnp.int32)
    value = field(0)
    position = lax.broadcasted_iota(jnp.int32, value.shape, 0) + z * steps
    value_weight, logit_weight = trace_terms(
        value,
        field(1),
        field(2),
        field(3),
        length,
        position,
        0,
        value.shape[0],
        scale,
    )
    for t in range(steps):
        terms = split_terms(
            logit_weight[t : t + 1, :], value_weight[t : t + 1, :], spread[t], action_count
        )
        write_back(terms, head_ref, slope_ref[t], dz_ref, t)


def offline_back_body(action_count, step_count, scale, place, *refs):
    parts = refs[:4]
    actions, behaviour, reward, done, length, head_ref, slope_ref, dz_ref = refs[4:]
    groups = dz_ref.shape[0]
    values, rhos, spreads = [], [], []
    for g in range(groups):
        value, rho, spread = action_terms(
            [p[g] for p in parts],
            actions[g : g + 1, :],
            behaviour[g : g + 1, :],
            action_count,
        )
        values.append(value)
        rhos.append(rho)
        spreads.append(spread)
    value = jnp.concatenate(values, axis=0)
    rho = jnp.concatenate(rhos, axis=0)
    position = lax.rem(lax.broadcasted_iota(jnp.int32, value.shape, 1), step_count)
    discount = DISCOUNT_RATE * (1.0 - done[...].astype(jnp.float32))
    value_weight, logit_weight = trace_terms(
        value, rho, reward[...], discount, length[...], position, 1, step_count, scale
    )
    for g in range(groups):
        terms = split_terms(
            logit_weight[g : g + 1, :], value_weight[g : g + 1, :], spreads[g], action_count
        )
        write_back(terms, head_ref, slope_ref[g], dz_ref, g)


def encode(v, c, message_ref, exponents_ref):
    rows = v.shape[0]
    largest = jnp.max(jnp.abs(v), axis=0, keepdims=True)
    exponent = jnp.ceil(jnp.log(jnp.maximum(largest, 1e-30)) * (1.0 / LOG_TWO) + 0.01)
    scale = jnp.exp(exponent * -LOG_TWO) * CODE_LIMIT
    code = jnp.floor(v * scale + 0.5)
    at = pl.ds(pl.multiple_of(c * rows, rows), rows)
    message_ref[at, :] = code.astype(jnp.int32).astype(jnp.int16)
    exponents_ref[pl.ds(c, 1), :] = exponent


def encode_tail(message_ref, exponents_ref):
    tail = exponents_ref[...].astype(jnp.int32)
    message_ref[message_ref.shape[0] - CODE_TAIL :, :] = tail.astype(jnp.int16)


def decode_steps(message_ref, steps_ref):
    exponents = message_ref[message_ref.shape[0] - CODE_TAIL :, :]
    exponents = exponents.astype(jnp.int32).astype(jnp.float32)
    steps_ref[...] = jnp.exp(exponents * LOG_TWO) * (1.0 / CODE_LIMIT)


def decode(message_ref, steps_ref, c, rows):
    at = pl.ds(pl.multiple_of(c * rows, rows), rows)
    code = message_ref[at, :].astype(jnp.int32).astype(jnp.float32)
    return code * steps_ref[pl.ds(c, 1), :]


def message_of(rows, columns):
    return ((rows * (columns // LANES) + CODE_TAIL, LANES), jnp.int16)


def grad_body(pieces, column, columns, place, *refs):
    xs, dzs = refs[: len(pieces)], refs[len(pieces) : len(pieces) + 2]
    message_ref, exponents_ref = refs[-2:]
    hidden_count = dzs[0].shape[2]
    section = place[3]
    at = slice(column * columns, (column + 1) * columns)
    exponents_ref[...] = jnp.zeros_like(exponents_ref)

    def step(h, carry):
        block = pl.ds(pl.multiple_of(h * GRAD_BLOCK, GRAD_BLOCK), GRAD_BLOCK)
        total = None
        for x, (which, swapped) in zip(xs, pieces):
            groups, width, _ = x.shape
            first = 0
            if swapped is not None:
                first = (1 - section if swapped else section) * groups
            part = lax.dot_general(
                x[:, :, at].reshape(groups * width, columns),
                dzs[which][pl.ds(first, groups), :, block].reshape(groups * width, GRAD_BLOCK),
                (((0,), (0,)), ((), ())),
                preferred_element_type=jnp.float32,
            )
            total = part if total is None else total + part
        per_block = GRAD_BLOCK // LANES
        for c in range(per_block):
            lanes = total[:, c * LANES : (c + 1) * LANES]
            encode(lanes, h * per_block + c, message_ref, exponents_ref)
        return carry

    lax.fori_loop(0, hidden_count // GRAD_BLOCK, step, 0)
    encode_tail(message_ref, exponents_ref)


def grad_chunk(place, pieces, dzs, column, columns, deps):
    hidden_count = dzs[0].shape[2]
    return vmem_call(
        functools.partial(grad_body, [p[1:] for p in pieces], column, columns),
        place,
        [x for x, _, _ in pieces] + dzs,
        [message_of(columns, hidden_count)],
        "grad_chunk",
        deps,
        [EXPONENTS],
    )[0]


def add_body(count, place, a_ref, b_ref, out_ref, exponents_ref, a_steps, b_steps):
    rows = (out_ref.shape[0] - CODE_TAIL) // count
    decode_steps(a_ref, a_steps)
    decode_steps(b_ref, b_steps)
    exponents_ref[...] = jnp.zeros_like(exponents_ref)

    def step(i, carry):
        for j in range(ADD_BLOCKS):
            c = i * ADD_BLOCKS + j
            v = decode(a_ref, a_steps, c, rows) + decode(b_ref, b_steps, c, rows)
            encode(v, c, out_ref, exponents_ref)
        return carry

    lax.fori_loop(0, count // ADD_BLOCKS, step, 0)
    encode_tail(out_ref, exponents_ref)


def add_chunk(place, a, b, count, deps):
    return vmem_call(
        functools.partial(add_body, count),
        place,
        [a, b],
        [(a.shape, a.dtype)],
        "add_chunk",
        deps,
        [EXPONENTS] * 3,
    )[0]


def place_body(count, rows, of_own, index, place, total, received, *refs):
    out, token, held, steps, sem = refs[-5:]
    token[...] = jnp.zeros_like(token)
    half = place[0] if of_own else 1 - place[0]
    first = pl.multiple_of(half * (out.shape[0] // 2) + index * rows, rows)
    at_end = place[1] == 1

    def write(message):
        decode_steps(message, steps)
        for c in range(count):
            held[:, c * LANES : (c + 1) * LANES] = decode(message, steps, c, rows)

    @pl.when(at_end)
    def _():
        write(received)

    @pl.when(jnp.logical_not(at_end))
    def _():
        write(total)

    copy = pltpu.make_async_copy(held, out.at[pl.ds(first, rows)], sem)
    copy.start()
    copy.wait()


def place_chunk(place, total, received, result, of_own, index, rows, shape, deps):
    hidden_count = shape[1]
    earlier = [] if result is None else [result]
    operands = [total, received] + deps
    return pl.pallas_call(
        functools.partial(place_body, hidden_count // LANES, rows, of_own, index),
        in_specs=[SMEM]
        + [VMEM] * len(operands)
        + [pl.BlockSpec(memory_space=pl.ANY) for _ in earlier],
        out_specs=[pl.BlockSpec(memory_space=pl.ANY), VMEM],
        out_shape=[
            jax.ShapeDtypeStruct(shape, jnp.float32),
            pltpu.VMEM((8, LANES), jnp.float32),
        ],
        scratch_shapes=[
            pltpu.VMEM((rows, hidden_count), jnp.float32),
            EXPONENTS,
            pltpu.SemaphoreType.DMA(()),
        ],
        input_output_aliases={1 + len(operands): 0} if earlier else {},
        compiler_params=params(),
        cost_estimate=SHORT,
        name="place_chunk",
    )(place, *[resident(x) for x in operands], *earlier)


def pipeline_order(count, lead):
    order = [("grad", k) for k in range(min(lead, count))]
    ahead = len(order)
    for k in range(count + 3):
        if k < count:
            order.append(("partial", k))
            while ahead < min(count, lead + 2 * (k + 1)):
                order.append(("grad", ahead))
                ahead += 1
        if 0 <= k - 3 < count:
            order.append(("place", k - 3))
        if 0 <= k - 1 < count:
            order.append(("total", k - 1))
    return order


def after(array, *others):
    return lax.optimization_barrier((array,) + others)[0]


def chip_pair(part, gate=()):
    across = lax.ppermute(part, "mp", SWAP)
    return [
        part,
        lax.ppermute(part, "section", SWAP),
        across,
        lax.ppermute(after(across, *gate), "section", SWAP),
    ]


def line_plan(
    online_obs,
    offline_obs,
    online_rewards,
    offline_rewards,
    online_behaviour,
    offline_behaviour,
    online_actions,
    offline_actions,
    online_done,
    offline_done,
    online_lengths,
    offline_lengths,
    torso_weights,
    value_head,
    policy_head,
):
    section = lax.axis_index("section")
    m = lax.axis_index("mp")
    z = lax.axis_index("dp")
    dp = lax.axis_size("dp")
    steps, online_count, features = online_obs.shape
    offline_count, step_count, _ = offline_obs.shape
    action_count = policy_head.shape[1]
    hidden_count = value_head.shape[0]
    at_end = ((z == 0) | (z == dp - 1)).astype(jnp.int32)
    place = jnp.stack([m, at_end, z, section]).astype(jnp.int32)
    weight = torso_weights[0]
    scale = math.sqrt(
        hidden_count
        * lax.axis_size("mp")
        / ((online_count + offline_count * dp) * step_count)
    )

    offline_groups = offline_count // 2
    offline_rows = offline_obs.reshape(offline_groups, 2 * step_count, features)
    own = [online_obs, offline_rows]
    halves = [
        lax.dynamic_slice_in_dim(x, section * (x.shape[0] // 2), x.shape[0] // 2, axis=0)
        for x in own
    ]

    policy_rows = jnp.where(section == 1, policy_head.T, 0)
    value_row = jnp.where(section == 0, value_head[None], 0)
    head = jnp.concatenate([policy_rows, value_row], axis=0).astype(jnp.bfloat16)
    head = jnp.pad(head, ((0, HEAD_ROWS - action_count - 1), (0, 0)))
    forward_head = jnp.pad(head, ((0, 32 - HEAD_ROWS), (0, 0)))
    back_head = jnp.concatenate([head, head, head, jnp.zeros_like(head)], axis=0)

    owned = online_lengths.shape[0]
    length_row = lax.dynamic_update_slice(
        jnp.zeros((online_count,), jnp.float32), online_lengths.astype(jnp.float32), (z * owned,)
    )
    length_row = length_row[None]
    lanes = (offline_groups, 2 * step_count)
    offline_length = jnp.broadcast_to(offline_lengths[:, None], (offline_count, step_count))
    offline_terms = [
        x.reshape(lanes)
        for x in (
            offline_actions,
            offline_behaviour,
            offline_rewards,
            offline_done,
            offline_length,
        )
    ]

    got = [lax.ppermute(half, "mp", SWAP) for half in halves]
    early = halves + [back_head, forward_head, length_row] + offline_terms
    pre_online = own_half(place, online_obs, weight, early)
    pre_offline = own_half(place, offline_rows, weight, [pre_online])
    rests = [lax.ppermute(after(got[0], pre_offline), "section", SWAP)]
    online_slope, online_part = forward(
        place, pre_online, got[0], rests[0], weight, forward_head, []
    )
    rests.append(lax.ppermute(after(got[1], online_part), "section", SWAP))
    offline_slope, offline_part = forward(
        place, pre_offline, got[1], rests[1], weight, forward_head, [online_part]
    )
    offline_parts = chip_pair(offline_part, [])
    pack, spread = vmem_call(
        functools.partial(online_heads_body, action_count),
        place,
        chip_pair(online_part, [offline_part, offline_parts[2]])
        + [online_actions, online_behaviour, online_rewards, online_done, length_row],
        [
            ((4 * steps + 8, online_count), jnp.float32),
            ((steps, HEAD_ROWS, online_count), jnp.float32),
        ],
        "online_heads",
        [offline_part],
    )

    (dz_offline,) = vmem_call(
        functools.partial(offline_back_body, action_count, step_count, scale),
        place,
        offline_parts + offline_terms + [back_head, offline_slope],
        [(offline_slope.shape, jnp.bfloat16)],
        "offline_back",
        [pack],
    )

    blocks = [pack]
    for hop in range(1, dp):
        pairs = [(i, (i - hop) % dp) for i in range(dp)]
        blocks.append(lax.ppermute(pack, "dp", pairs))
    (dz_online,) = vmem_call(
        functools.partial(online_back_body, action_count, scale),
        place,
        blocks + [spread, back_head, online_slope],
        [(online_slope.shape, jnp.bfloat16)],
        "online_back",
        [dz_offline],
    )

    own_x = [(online_obs, 0, None), (offline_rows, 1, None)]
    other_x = []
    for which in range(2):
        other_x += [(got[which], which, 0), (rests[which], which, 1)]
    columns = 2 * features // GRAD_CHUNKS
    per_half = GRAD_CHUNKS // 2
    lane_blocks = hidden_count // LANES

    messages, inward, partial, across, total, outward = {}, {}, {}, {}, {}, {}
    result, last = None, dz_online
    for kind, k in pipeline_order(GRAD_CHUNKS, GRAD_LEAD):
        if kind == "grad":
            last = messages[k] = grad_chunk(
                place,
                own_x if k < per_half else other_x,
                [dz_online, dz_offline],
                k % per_half,
                columns,
                [last],
            )
            inward[k] = lax.ppermute(last, "dp", TO_CENTER)
        elif kind == "partial":
            last = partial[k] = add_chunk(place, messages[k], inward[k], lane_blocks, [last])
            across[k] = lax.ppermute(last, "dp", CENTER)
        elif kind == "total":
            last = total[k] = add_chunk(place, partial[k], across[k], lane_blocks, [last])
            outward[k] = lax.ppermute(last, "dp", FROM_CENTER)
        else:
            result, last = place_chunk(
                place,
                total[k],
                outward[k],
                result,
                k < per_half,
                k % per_half,
                columns,
                (2 * features, hidden_count),
                [last],
            )
    return result[None]


def solution(mesh):
    on_line = mesh.shape["dp"] == 4 and mesh.shape["mp"] == 2 and mesh.shape["section"] == 2
    in_specs = (
        P("dp", "groups", "mp"),
        P(("groups", "dp"), None, "mp"),
        P("dp", "groups"),
        P(("groups", "dp"), None),
        P("dp", "groups"),
        P(("groups", "dp"), None),
        P("dp", "groups"),
        P(("groups", "dp"), None),
        P("dp", "groups"),
        P(("groups", "dp"), None),
        P(("groups", "dp")),
        P(("groups", "dp")),
        P("section", None, "mp"),
        P("mp"),
        P("mp", None),
    )
    out_specs = P(("groups", "section"), None, "mp")
    per_device = line_plan if on_line else general_plan
    return jax.shard_map(
        per_device, mesh=mesh, in_specs=in_specs, out_specs=out_specs, check_vma=False
    )
```

```python
import functools
import math

import jax
import jax.numpy as jnp
from jax import lax
from jax.experimental import pallas as pl
from jax.experimental.pallas import tpu as pltpu
from jax.sharding import PartitionSpec as P

DISCOUNT_RATE = 0.99
TRACE_LAMBDA = 0.95


def silu_slope(pre):
    sigma = jax.nn.sigmoid(pre)
    return sigma * (1.0 + pre * (1.0 - sigma))


def importance_trace_terms(
    value_estimates,
    policy_logits,
    reward_rows,
    behaviour_probs,
    taken_actions,
    episode_finished,
    sequence_length,
    objective_scale,
):
    seq_count, step_count = value_estimates.shape
    action_count = policy_logits.shape[0]
    positions = jnp.arange(step_count, dtype=jnp.int32)
    valid_mask = (positions[None, :] < sequence_length[:, None]).astype(jnp.float32)
    zero_column = jnp.zeros((seq_count, 1), jnp.float32)
    valid_next = jnp.concatenate([valid_mask[:, 1:], zero_column], axis=1)
    log_probs = jax.nn.log_softmax(policy_logits, axis=0)
    one_hot = (
        jnp.arange(action_count, dtype=jnp.int32)[:, None, None] == taken_actions[None]
    ).astype(jnp.float32)
    chosen = jnp.sum(one_hot * log_probs, axis=0)
    clip_ratio = jnp.exp(jnp.minimum(chosen - behaviour_probs, 0.0))
    discount = DISCOUNT_RATE * (1.0 - episode_finished.astype(jnp.float32))
    next_value = jnp.concatenate([value_estimates[:, 1:], zero_column], axis=1) * valid_next
    td_error = valid_mask * clip_ratio * (reward_rows + discount * next_value - value_estimates)
    trace_coef = discount * TRACE_LAMBDA * clip_ratio * valid_next

    def backward_step(carried, inputs):
        error_now, coef_now = inputs
        updated = error_now + coef_now * carried
        return (updated, updated)

    final_state, stacked = lax.scan(
        backward_step,
        jnp.zeros((seq_count,), jnp.float32),
        (td_error.T, trace_coef.T),
        reverse=True,
    )
    correction = stacked.T
    targets = value_estimates + correction
    next_target = jnp.concatenate([targets[:, 1:], zero_column], axis=1) * valid_next
    policy_adv = clip_ratio * (reward_rows + discount * next_target - value_estimates)
    value_gradient = -objective_scale * valid_mask * correction
    logits_gradient = (
        objective_scale * (valid_mask * policy_adv)[None] * (jnp.exp(log_probs) - one_hot)
    )
    return (value_gradient, logits_gradient)


def head_terms(hidden, value_w, policy_w):
    logit_part = jnp.einsum("rh,ha->ar", hidden, policy_w, preferred_element_type=jnp.float32)
    value_part = jnp.dot(hidden, value_w, preferred_element_type=jnp.float32)
    return jnp.concatenate([logit_part, value_part[None]], axis=0)


def full_rows(online_part, offline_part):
    return (
        lax.all_gather(online_part, "mp", axis=2, tiled=True),
        lax.all_gather(offline_part, "mp", axis=2, tiled=True),
    )


def general_plan(
    online_obs,
    offline_obs,
    online_rewards,
    offline_rewards,
    online_behaviour,
    offline_behaviour,
    online_actions,
    offline_actions,
    online_done,
    offline_done,
    online_lengths,
    offline_lengths,
    torso_weights,
    value_head,
    policy_head,
):
    owned_online = online_lengths.shape[0]
    owned_offline = offline_obs.shape[0]
    step_count = offline_obs.shape[1]
    action_count = policy_head.shape[1]
    record_stack = jnp.stack(
        [
            online_rewards,
            online_behaviour,
            online_actions.astype(jnp.float32),
            online_done.astype(jnp.float32),
        ]
    )
    records = lax.all_to_all(record_stack, "dp", split_axis=2, concat_axis=1, tiled=True)
    slabs = lax.all_to_all(online_obs, "dp", split_axis=1, concat_axis=0, tiled=True)
    x_online, x_offline = full_rows(slabs, offline_obs)
    feature_count = x_online.shape[2]
    x_online = x_online.reshape(step_count * owned_online, feature_count)
    x_offline = x_offline.reshape(owned_offline * step_count, feature_count)
    weight = torso_weights[0]
    pre_online = jnp.dot(x_online, weight, preferred_element_type=jnp.float32)
    pre_offline = jnp.dot(x_offline, weight, preferred_element_type=jnp.float32)
    hidden_online = jax.nn.silu(pre_online).astype(jnp.bfloat16)
    hidden_offline = jax.nn.silu(pre_offline).astype(jnp.bfloat16)
    is_critic = (lax.axis_index("section") == 0).astype(jnp.float32)
    is_policy = 1.0 - is_critic
    row_keep = jnp.where(jnp.arange(action_count + 1) == action_count, is_critic, is_policy)
    partial_value = jnp.concatenate(
        [
            head_terms(hidden_online, value_head, policy_head),
            head_terms(hidden_offline, value_head, policy_head),
        ],
        axis=1,
    )
    partial_value = partial_value * row_keep[:, None]
    heads = lax.psum(partial_value, ("mp", "section"))
    online_count = step_count * owned_online
    logits_on = (
        heads[:action_count, :online_count]
        .reshape(action_count, step_count, owned_online)
        .transpose(0, 2, 1)
    )
    logits_off = heads[:action_count, online_count:].reshape(
        action_count, owned_offline, step_count
    )
    values_on = heads[action_count, :online_count].reshape(step_count, owned_online).T
    values_off = heads[action_count, online_count:].reshape(owned_offline, step_count)
    record_seq = records.transpose(0, 2, 1)
    value_estimates = jnp.concatenate([values_on, values_off], axis=0)
    policy_logits = jnp.concatenate([logits_on, logits_off], axis=1)
    reward_rows = jnp.concatenate([record_seq[0], offline_rewards], axis=0)
    behaviour_probs = jnp.concatenate([record_seq[1], offline_behaviour], axis=0)
    taken_actions = jnp.concatenate([record_seq[2].astype(jnp.int32), offline_actions], axis=0)
    episode_finished = jnp.concatenate([record_seq[3].astype(jnp.int32), offline_done], axis=0)
    sequence_length = jnp.concatenate([online_lengths, offline_lengths], axis=0)
    total_seqs = online_obs.shape[1] + owned_offline * lax.axis_size("dp")
    hidden_total = value_head.shape[0] * lax.axis_size("mp")
    objective_scale = math.sqrt(hidden_total / (total_seqs * step_count))
    value_gradient, logits_gradient = importance_trace_terms(
        value_estimates,
        policy_logits,
        reward_rows,
        behaviour_probs,
        taken_actions,
        episode_finished,
        sequence_length,
        objective_scale,
    )
    value_gradient = value_gradient * is_critic
    logits_gradient = logits_gradient * is_policy
    dv_on = value_gradient[:owned_online].T.reshape(online_count)
    dv_off = value_gradient[owned_online:].reshape(owned_offline * step_count)
    dl_on = logits_gradient[:, :owned_online].transpose(0, 2, 1).reshape(action_count, online_count)
    dl_off = logits_gradient[:, owned_online:].reshape(action_count, owned_offline * step_count)
    value_w = value_head.astype(jnp.float32)
    policy_w = policy_head.astype(jnp.float32)
    dh_on = dv_on[:, None] * value_w[None, :] + jnp.einsum(
        "ar,ha->rh", dl_on, policy_w, precision=lax.Precision.HIGHEST
    )
    dh_off = dv_off[:, None] * value_w[None, :] + jnp.einsum(
        "ar,ha->rh", dl_off, policy_w, precision=lax.Precision.HIGHEST
    )
    dz_online = (dh_on * silu_slope(pre_online)).astype(jnp.bfloat16)
    dz_offline = (dh_off * silu_slope(pre_offline)).astype(jnp.bfloat16)
    local_grad = jnp.einsum("rd,rh->dh", x_online, dz_online, preferred_element_type=jnp.float32)
    local_grad = local_grad + jnp.einsum(
        "rd,rh->dh", x_offline, dz_offline, preferred_element_type=jnp.float32
    )
    summed = lax.psum(local_grad, "dp")
    return summed[None]


HEAD_ROWS = 24
SPLIT_ROWS = 4 * HEAD_ROWS
COLUMN_BLOCK = 256
GRAD_BLOCK = 512
ADD_BLOCKS = 2
ROW_GROUPS = 4
GRAD_CHUNKS = 8
GRAD_LEAD = 5
SEND_LEAD = 3
LANES = 128
CODE_LIMIT = 32512.0
CODE_TAIL = 16
LOG_TWO = math.log(2.0)
SCRATCH_BYTES = 6 * 1024 * 1024
SWAP = ((0, 1), (1, 0))
TO_CENTER = ((0, 1), (3, 2))
CENTER = ((1, 2), (2, 1))
FROM_CENTER = ((1, 0), (2, 3))
VMEM = pl.BlockSpec(memory_space=pltpu.VMEM)
HBM = pl.BlockSpec(memory_space=pltpu.HBM)
SMEM = pl.BlockSpec(memory_space=pltpu.SMEM)
EXPONENTS = pltpu.VMEM((CODE_TAIL, LANES), jnp.float32)


SHORT = pl.CostEstimate(flops=1, bytes_accessed=1, transcendentals=0)


def params():
    return pltpu.CompilerParams(vmem_limit_bytes=SCRATCH_BYTES)


def resident(array):
    return pltpu.with_memory_space_constraint(array, pltpu.VMEM)


def vmem_call(body, place, arrays, outs, name, deps=(), scratch=()):
    operands = list(arrays) + list(deps)

    def run(place_ref, *refs):
        body(place_ref, *refs[: len(arrays)], *refs[len(operands) :])

    return pl.pallas_call(
        run,
        in_specs=[SMEM] + [VMEM] * len(operands),
        out_specs=[VMEM] * len(outs),
        out_shape=[pltpu.VMEM(shape, dtype) for shape, dtype in outs],
        scratch_shapes=list(scratch),
        compiler_params=params(),
        cost_estimate=SHORT,
        name=name,
    )(place, *[resident(x) for x in operands])


def in_hbm(array):
    return pltpu.with_memory_space_constraint(array, pltpu.HBM)


def share_body(place, source, *refs):
    out, sem = refs[-2:]
    count = out.shape[0]
    copy = pltpu.make_async_copy(source.at[pl.ds(place[3] * count, count)], out, sem)
    copy.start()
    copy.wait()


def section_share(place, source, deps):
    groups, width, features = source.shape
    return pl.pallas_call(
        share_body,
        in_specs=[SMEM, HBM] + [VMEM] * len(deps),
        out_specs=VMEM,
        out_shape=pltpu.VMEM((groups // 2, width, features), source.dtype),
        scratch_shapes=[pltpu.SemaphoreType.DMA(())],
        compiler_params=params(),
        cost_estimate=SHORT,
        name="section_share",
    )(place, in_hbm(source), *[resident(x) for x in deps])


def own_half_body(place, source, weight_ref, *refs):
    own_ref, out_ref, sem = refs[-3:]
    groups, width, features = own_ref.shape
    copy = pltpu.make_async_copy(source, own_ref, sem)
    copy.start()
    copy.wait()
    at = pl.multiple_of(place[0] * features, features)
    for first in range(0, groups, ROW_GROUPS):
        part = slice(first, first + ROW_GROUPS)
        own = own_ref[part].reshape(-1, features)
        for h in range(0, weight_ref.shape[1], COLUMN_BLOCK):
            block = slice(h, h + COLUMN_BLOCK)
            pre = jnp.dot(
                own, weight_ref[pl.ds(at, features), block], preferred_element_type=jnp.float32
            )
            out_ref[part, :, block] = pre.reshape(-1, width, COLUMN_BLOCK)


def own_half(place, source, weight, deps):
    groups, width, _ = source.shape
    operands = [weight] + deps
    return pl.pallas_call(
        own_half_body,
        in_specs=[SMEM, HBM] + [VMEM] * len(operands),
        out_specs=[VMEM, VMEM],
        out_shape=[
            pltpu.VMEM(source.shape, source.dtype),
            pltpu.VMEM((groups, width, weight.shape[1]), jnp.float32),
        ],
        scratch_shapes=[pltpu.SemaphoreType.DMA(())],
        compiler_params=params(),
        cost_estimate=SHORT,
        name="own_half",
    )(place, in_hbm(source), *[resident(x) for x in operands])


def forward_body(place, pre_ref, got_ref, rest_ref, weight_ref, head_ref, *refs):
    slope_ref, heads_ref, hidden_ref = refs[-3:]
    half, width, features = got_ref.shape
    hidden_count = weight_ref.shape[1]
    m, section = place[0], place[3]
    other_at = pl.multiple_of((1 - m) * features, features)
    count = min(half, ROW_GROUPS)
    for x_ref, start in ((got_ref, section * half), (rest_ref, (1 - section) * half)):
        for first in range(0, half, count):
            at = pl.ds(start + first, count)
            other = x_ref[first : first + count].reshape(-1, features)
            for h in range(0, hidden_count, COLUMN_BLOCK):
                block = slice(h, h + COLUMN_BLOCK)
                pre = jnp.dot(
                    other,
                    weight_ref[pl.ds(other_at, features), block],
                    preferred_element_type=jnp.float32,
                )
                pre = pre + pre_ref[at, :, block].reshape(-1, COLUMN_BLOCK)
                sigma = 0.5 * jnp.tanh(0.5 * pre) + 0.5
                hidden = pre * sigma
                slope = sigma + hidden * (1.0 - sigma)
                slope_ref[at, :, block] = slope.reshape(-1, width, COLUMN_BLOCK)
                hidden_ref[:, block] = hidden.astype(jnp.bfloat16)
            for g in range(count):
                heads = lax.dot_general(
                    head_ref[...],
                    hidden_ref[g * width : (g + 1) * width],
                    (((1,), (1,)), ((), ())),
                    preferred_element_type=jnp.float32,
                )
                heads_ref[start + first + g] = heads[:HEAD_ROWS]


def forward(place, pre, got, rest, weight, head, deps):
    groups, width, hidden_count = pre.shape
    operands = [pre, got, rest, weight, head] + deps
    return pl.pallas_call(
        forward_body,
        in_specs=[SMEM] + [VMEM] * len(operands),
        out_specs=[VMEM, VMEM],
        out_shape=[
            pltpu.VMEM(pre.shape, jnp.float32),
            pltpu.VMEM((groups, HEAD_ROWS, width), jnp.float32),
        ],
        scratch_shapes=[
            pltpu.VMEM((min(groups // 2, ROW_GROUPS) * width, hidden_count), jnp.bfloat16)
        ],
        input_output_aliases={1: 0},
        compiler_params=params(),
        cost_estimate=SHORT,
        name="forward_rows",
    )(place, *[resident(x) for x in operands])


def action_terms(parts, actions, behaviour, action_count):
    heads = parts[0] + parts[1] + (parts[2] + parts[3])
    row = lax.broadcasted_iota(jnp.int32, heads.shape, 0)
    is_logit = row < action_count
    logits = jnp.where(is_logit, heads, -1e30)
    shifted = logits - jnp.max(logits, axis=0, keepdims=True)
    log_sum = jnp.log(jnp.sum(jnp.exp(shifted), axis=0, keepdims=True))
    log_probs = shifted - log_sum
    taken = row == actions
    chosen = jnp.sum(jnp.where(taken, log_probs, 0.0), axis=0, keepdims=True)
    rho = jnp.exp(jnp.minimum(chosen - behaviour, 0.0))
    spread = jnp.where(is_logit, jnp.exp(log_probs) - taken.astype(jnp.float32), 0.0)
    return heads[action_count : action_count + 1], rho, spread


def trace_terms(value, rho, reward, discount, length, position, axis, reach, scale):
    size = value.shape[axis]
    valid = (position < length).astype(jnp.float32)
    valid_next = (position + 1 < length).astype(jnp.float32)
    next_value = pltpu.roll(value, size - 1, axis) * valid_next
    correction = valid * rho * (reward + discount * next_value - value)
    coef = discount * TRACE_LAMBDA * rho * valid_next
    shift = 1
    while shift < reach:
        correction = correction + coef * pltpu.roll(correction, size - shift, axis)
        coef = coef * pltpu.roll(coef, size - shift, axis)
        shift *= 2
    targets = value + correction
    next_target = pltpu.roll(targets, size - 1, axis) * valid_next
    advantage = rho * (reward + discount * next_target - value)
    return -scale * valid * correction, scale * (valid * advantage)


def split_terms(logit_weight, value_weight, spread, action_count):
    row = lax.broadcasted_iota(jnp.int32, spread.shape, 0)
    full = jnp.where(row == action_count, value_weight, logit_weight * spread)
    high = full.astype(jnp.bfloat16).astype(jnp.float32)
    rest = full - high
    middle = rest.astype(jnp.bfloat16).astype(jnp.float32)
    low = rest - middle
    return jnp.concatenate([high, middle, low, jnp.zeros_like(full)], axis=0).astype(jnp.bfloat16)


def write_back(terms, head_ref, slope, dz_ref, g):
    dh = lax.dot_general(
        terms, head_ref[...], (((0,), (0,)), ((), ())), preferred_element_type=jnp.float32
    )
    dz_ref[g] = (dh * slope).astype(jnp.bfloat16)


def online_heads_body(action_count, place, *refs):
    parts = refs[:4]
    actions, behaviour, reward, done, lengths, pack_ref, spread_ref = refs[4:]
    steps = actions.shape[0]
    for t in range(steps):
        value, rho, spread = action_terms(
            [p[t] for p in parts],
            actions[t : t + 1, :],
            behaviour[t : t + 1, :],
            action_count,
        )
        pack_ref[t : t + 1, :] = value
        pack_ref[steps + t : steps + t + 1, :] = rho
        spread_ref[t] = spread
    pack_ref[2 * steps : 3 * steps, :] = reward[...]
    pack_ref[3 * steps : 4 * steps, :] = DISCOUNT_RATE * (1.0 - done[...].astype(jnp.float32))
    pack_ref[4 * steps :, :] = jnp.broadcast_to(lengths[...], (8, lengths.shape[1]))


def online_back_body(action_count, scale, place, *refs):
    blocks, spread, head_ref, slope_ref, dz_ref = refs[:4], *refs[4:]
    steps = spread.shape[0]
    z = place[2]

    def field(i):
        parts = []
        for hop, b in enumerate(blocks):
            part = b[i * steps : (i + 1) * steps, :]
            parts.append(jnp.where(z + hop < len(blocks), part, 0.0) if hop else part)
        return jnp.concatenate(parts, axis=0)

    length = sum(b[4 * steps : 4 * steps + 1, :] for b in blocks).astype(jnp.int32)
    value = field(0)
    position = lax.broadcasted_iota(jnp.int32, value.shape, 0) + z * steps
    value_weight, logit_weight = trace_terms(
        value,
        field(1),
        field(2),
        field(3),
        length,
        position,
        0,
        value.shape[0],
        scale,
    )
    for t in range(steps):
        terms = split_terms(
            logit_weight[t : t + 1, :], value_weight[t : t + 1, :], spread[t], action_count
        )
        write_back(terms, head_ref, slope_ref[t], dz_ref, t)


def offline_back_body(action_count, step_count, scale, place, *refs):
    parts = refs[:4]
    actions, behaviour, reward, done, length, head_ref, slope_ref, dz_ref = refs[4:]
    groups = dz_ref.shape[0]
    values, rhos, spreads = [], [], []
    for g in range(groups):
        value, rho, spread = action_terms(
            [p[g] for p in parts],
            actions[g : g + 1, :],
            behaviour[g : g + 1, :],
            action_count,
        )
        values.append(value)
        rhos.append(rho)
        spreads.append(spread)
    value = jnp.concatenate(values, axis=0)
    rho = jnp.concatenate(rhos, axis=0)
    position = lax.rem(lax.broadcasted_iota(jnp.int32, value.shape, 1), step_count)
    discount = DISCOUNT_RATE * (1.0 - done[...].astype(jnp.float32))
    value_weight, logit_weight = trace_terms(
        value, rho, reward[...], discount, length[...], position, 1, step_count, scale
    )
    for g in range(groups):
        terms = split_terms(
            logit_weight[g : g + 1, :], value_weight[g : g + 1, :], spreads[g], action_count
        )
        write_back(terms, head_ref, slope_ref[g], dz_ref, g)


def encode(v, c, message_ref, exponents_ref):
    rows = v.shape[0]
    largest = jnp.max(jnp.abs(v), axis=0, keepdims=True)
    exponent = jnp.ceil(jnp.log(jnp.maximum(largest, 1e-30)) * (1.0 / LOG_TWO) + 0.01)
    scale = jnp.exp(exponent * -LOG_TWO) * CODE_LIMIT
    code = jnp.floor(v * scale + 0.5)
    at = pl.ds(pl.multiple_of(c * rows, rows), rows)
    message_ref[at, :] = code.astype(jnp.int32).astype(jnp.int16)
    exponents_ref[pl.ds(c, 1), :] = exponent


def encode_tail(message_ref, exponents_ref):
    tail = exponents_ref[...].astype(jnp.int32)
    message_ref[message_ref.shape[0] - CODE_TAIL :, :] = tail.astype(jnp.int16)


def decode_steps(message_ref, steps_ref):
    exponents = message_ref[message_ref.shape[0] - CODE_TAIL :, :]
    exponents = exponents.astype(jnp.int32).astype(jnp.float32)
    steps_ref[...] = jnp.exp(exponents * LOG_TWO) * (1.0 / CODE_LIMIT)


def decode(message_ref, steps_ref, c, rows):
    at = pl.ds(pl.multiple_of(c * rows, rows), rows)
    code = message_ref[at, :].astype(jnp.int32).astype(jnp.float32)
    return code * steps_ref[pl.ds(c, 1), :]


def message_of(rows, columns):
    return ((rows * (columns // LANES) + CODE_TAIL, LANES), jnp.int16)


def grad_body(pieces, column, columns, place, *refs):
    xs, dzs = refs[: len(pieces)], refs[len(pieces) : len(pieces) + 2]
    message_ref, exponents_ref = refs[-2:]
    hidden_count = dzs[0].shape[2]
    section = place[3]
    at = slice(column * columns, (column + 1) * columns)
    exponents_ref[...] = jnp.zeros_like(exponents_ref)

    def step(h, carry):
        block = pl.ds(pl.multiple_of(h * GRAD_BLOCK, GRAD_BLOCK), GRAD_BLOCK)
        total = None
        for x, (which, swapped) in zip(xs, pieces):
            groups, width, _ = x.shape
            first = 0
            if swapped is not None:
                first = (1 - section if swapped else section) * groups
            part = lax.dot_general(
                x[:, :, at].reshape(groups * width, columns),
                dzs[which][pl.ds(first, groups), :, block].reshape(groups * width, GRAD_BLOCK),
                (((0,), (0,)), ((), ())),
                preferred_element_type=jnp.float32,
            )
            total = part if total is None else total + part
        per_block = GRAD_BLOCK // LANES
        for c in range(per_block):
            lanes = total[:, c * LANES : (c + 1) * LANES]
            encode(lanes, h * per_block + c, message_ref, exponents_ref)
        return carry

    lax.fori_loop(0, hidden_count // GRAD_BLOCK, step, 0)
    encode_tail(message_ref, exponents_ref)


def grad_chunk(place, pieces, dzs, column, columns, deps):
    hidden_count = dzs[0].shape[2]
    return vmem_call(
        functools.partial(grad_body, [p[1:] for p in pieces], column, columns),
        place,
        [x for x, _, _ in pieces] + dzs,
        [message_of(columns, hidden_count)],
        "grad_chunk",
        deps,
        [EXPONENTS],
    )[0]


def add_body(count, place, a_ref, b_ref, out_ref, exponents_ref, a_steps, b_steps):
    rows = (out_ref.shape[0] - CODE_TAIL) // count
    decode_steps(a_ref, a_steps)
    decode_steps(b_ref, b_steps)
    exponents_ref[...] = jnp.zeros_like(exponents_ref)

    def step(i, carry):
        for j in range(ADD_BLOCKS):
            c = i * ADD_BLOCKS + j
            v = decode(a_ref, a_steps, c, rows) + decode(b_ref, b_steps, c, rows)
            encode(v, c, out_ref, exponents_ref)
        return carry

    lax.fori_loop(0, count // ADD_BLOCKS, step, 0)
    encode_tail(out_ref, exponents_ref)


def add_chunk(place, a, b, count, deps):
    return vmem_call(
        functools.partial(add_body, count),
        place,
        [a, b],
        [(a.shape, a.dtype)],
        "add_chunk",
        deps,
        [EXPONENTS] * 3,
    )[0]


def place_body(count, rows, of_own, index, place, total, received, *refs):
    out, token, held, steps, sem = refs[-5:]
    token[...] = jnp.zeros_like(token)
    half = place[0] if of_own else 1 - place[0]
    first = pl.multiple_of(half * (out.shape[0] // 2) + index * rows, rows)
    at_end = place[1] == 1

    def write(message):
        decode_steps(message, steps)
        for c in range(count):
            held[:, c * LANES : (c + 1) * LANES] = decode(message, steps, c, rows)

    @pl.when(at_end)
    def _():
        write(received)

    @pl.when(jnp.logical_not(at_end))
    def _():
        write(total)

    copy = pltpu.make_async_copy(held, out.at[pl.ds(first, rows)], sem)
    copy.start()
    copy.wait()


def place_chunk(place, total, received, result, of_own, index, rows, shape, deps):
    hidden_count = shape[1]
    earlier = [] if result is None else [result]
    operands = [total, received] + deps
    return pl.pallas_call(
        functools.partial(place_body, hidden_count // LANES, rows, of_own, index),
        in_specs=[SMEM]
        + [VMEM] * len(operands)
        + [pl.BlockSpec(memory_space=pl.ANY) for _ in earlier],
        out_specs=[pl.BlockSpec(memory_space=pl.ANY), VMEM],
        out_shape=[
            jax.ShapeDtypeStruct(shape, jnp.float32),
            pltpu.VMEM((8, LANES), jnp.float32),
        ],
        scratch_shapes=[
            pltpu.VMEM((rows, hidden_count), jnp.float32),
            EXPONENTS,
            pltpu.SemaphoreType.DMA(()),
        ],
        input_output_aliases={1 + len(operands): 0} if earlier else {},
        compiler_params=params(),
        cost_estimate=SHORT,
        name="place_chunk",
    )(place, *[resident(x) for x in operands], *earlier)


def pipeline_order(count, lead):
    order = [("grad", k) for k in range(min(lead, count))]
    ahead = len(order)
    for k in range(count + 2):
        if k < count:
            order.append(("partial", k))
            while ahead < min(count, lead + 2 * (k + 1)):
                order.append(("grad", ahead))
                ahead += 1
        if 0 <= k - 1 < count:
            order.append(("total", k - 1))
        if 0 <= k - 2 < count:
            order.append(("place", k - 2))
    return order


def after(array, *others):
    return lax.optimization_barrier((array,) + others)[0]


def chip_pair(part, gate=()):
    across = lax.ppermute(part, "mp", SWAP)
    return [
        part,
        lax.ppermute(part, "section", SWAP),
        across,
        lax.ppermute(after(across, *gate), "section", SWAP),
    ]


def line_plan(
    online_obs,
    offline_obs,
    online_rewards,
    offline_rewards,
    online_behaviour,
    offline_behaviour,
    online_actions,
    offline_actions,
    online_done,
    offline_done,
    online_lengths,
    offline_lengths,
    torso_weights,
    value_head,
    policy_head,
):
    section = lax.axis_index("section")
    m = lax.axis_index("mp")
    z = lax.axis_index("dp")
    dp = lax.axis_size("dp")
    steps, online_count, features = online_obs.shape
    offline_count, step_count, _ = offline_obs.shape
    action_count = policy_head.shape[1]
    hidden_count = value_head.shape[0]
    at_end = ((z == 0) | (z == dp - 1)).astype(jnp.int32)
    place = jnp.stack([m, at_end, z, section]).astype(jnp.int32)
    weight = torso_weights[0]
    scale = math.sqrt(
        hidden_count
        * lax.axis_size("mp")
        / ((online_count + offline_count * dp) * step_count)
    )

    offline_groups = offline_count // 2
    offline_rows = offline_obs.reshape(offline_groups, 2 * step_count, features)
    halves = [section_share(place, online_obs, [])]
    halves.append(section_share(place, offline_rows, [halves[0]]))

    policy_rows = jnp.where(section == 1, policy_head.T, 0)
    value_row = jnp.where(section == 0, value_head[None], 0)
    head = jnp.concatenate([policy_rows, value_row], axis=0).astype(jnp.bfloat16)
    head = jnp.pad(head, ((0, HEAD_ROWS - action_count - 1), (0, 0)))
    forward_head = jnp.pad(head, ((0, 32 - HEAD_ROWS), (0, 0)))
    back_head = jnp.concatenate([head, head, head, jnp.zeros_like(head)], axis=0)

    owned = online_lengths.shape[0]
    length_row = lax.dynamic_update_slice(
        jnp.zeros((online_count,), jnp.float32), online_lengths.astype(jnp.float32), (z * owned,)
    )
    length_row = length_row[None]
    lanes = (offline_groups, 2 * step_count)
    offline_length = jnp.broadcast_to(offline_lengths[:, None], (offline_count, step_count))
    offline_terms = [
        x.reshape(lanes)
        for x in (
            offline_actions,
            offline_behaviour,
            offline_rewards,
            offline_done,
            offline_length,
        )
    ]

    got = [lax.ppermute(half, "mp", SWAP) for half in halves]
    early = halves + [back_head, forward_head, length_row] + offline_terms
    own_online, pre_online = own_half(place, online_obs, weight, early)
    own_offline, pre_offline = own_half(place, offline_rows, weight, [pre_online])
    rests = [lax.ppermute(after(got[0], pre_offline), "section", SWAP)]
    online_slope, online_part = forward(
        place, pre_online, got[0], rests[0], weight, forward_head, []
    )
    rests.append(lax.ppermute(after(got[1], online_part), "section", SWAP))
    offline_slope, offline_part = forward(
        place, pre_offline, got[1], rests[1], weight, forward_head, [online_part]
    )
    offline_parts = chip_pair(offline_part, [])
    pack, spread = vmem_call(
        functools.partial(online_heads_body, action_count),
        place,
        chip_pair(online_part, [offline_part, offline_parts[2]])
        + [online_actions, online_behaviour, online_rewards, online_done, length_row],
        [
            ((4 * steps + 8, online_count), jnp.float32),
            ((steps, HEAD_ROWS, online_count), jnp.float32),
        ],
        "online_heads",
        [offline_part],
    )

    (dz_offline,) = vmem_call(
        functools.partial(offline_back_body, action_count, step_count, scale),
        place,
        offline_parts + offline_terms + [back_head, offline_slope],
        [(offline_slope.shape, jnp.bfloat16)],
        "offline_back",
        [pack],
    )

    blocks = [pack]
    for hop in range(1, dp):
        pairs = [(i, (i - hop) % dp) for i in range(dp)]
        blocks.append(lax.ppermute(pack, "dp", pairs))
    (dz_online,) = vmem_call(
        functools.partial(online_back_body, action_count, scale),
        place,
        blocks + [spread, back_head, online_slope],
        [(online_slope.shape, jnp.bfloat16)],
        "online_back",
        [dz_offline],
    )

    own_x = [(own_online, 0, None), (own_offline, 1, None)]
    other_x = []
    for which in range(2):
        other_x += [(got[which], which, 0), (rests[which], which, 1)]
    columns = 2 * features // GRAD_CHUNKS
    per_half = GRAD_CHUNKS // 2
    lane_blocks = hidden_count // LANES

    messages, inward, partial, across, total, outward = {}, {}, {}, {}, {}, {}
    result, last = None, dz_online
    for kind, k in pipeline_order(GRAD_CHUNKS, GRAD_LEAD):
        if kind == "grad":
            last = messages[k] = grad_chunk(
                place,
                own_x if k < per_half else other_x,
                [dz_online, dz_offline],
                k % per_half,
                columns,
                [last],
            )
            if k < SEND_LEAD:
                inward[k] = lax.ppermute(last, "dp", TO_CENTER)
        elif kind == "partial":
            last = partial[k] = add_chunk(place, messages[k], inward[k], lane_blocks, [last])
            across[k] = lax.ppermute(last, "dp", CENTER)
        elif kind == "total":
            last = total[k] = add_chunk(place, partial[k], across[k], lane_blocks, [last])
            outward[k] = lax.ppermute(last, "dp", FROM_CENTER)
            ahead = k + SEND_LEAD
            if ahead < GRAD_CHUNKS:
                inward[ahead] = lax.ppermute(after(messages[ahead], last), "dp", TO_CENTER)
        else:
            result, last = place_chunk(
                place,
                total[k],
                outward[k],
                result,
                k < per_half,
                k % per_half,
                columns,
                (2 * features, hidden_count),
                [last],
            )
    return result[None]


def solution(mesh):
    on_line = mesh.shape["dp"] == 4 and mesh.shape["mp"] == 2 and mesh.shape["section"] == 2
    in_specs = (
        P("dp", "groups", "mp"),
        P(("groups", "dp"), None, "mp"),
        P("dp", "groups"),
        P(("groups", "dp"), None),
        P("dp", "groups"),
        P(("groups", "dp"), None),
        P("dp", "groups"),
        P(("groups", "dp"), None),
        P("dp", "groups"),
        P(("groups", "dp"), None),
        P(("groups", "dp")),
        P(("groups", "dp")),
        P("section", None, "mp"),
        P("mp"),
        P("mp", None),
    )
    out_specs = P(("groups", "section"), None, "mp")
    per_device = line_plan if on_line else general_plan
    return jax.shard_map(
        per_device, mesh=mesh, in_specs=in_specs, out_specs=out_specs, check_vma=False
    )
```

```python
import functools
import math

import jax
import jax.numpy as jnp
from jax import lax
from jax.experimental import pallas as pl
from jax.experimental.pallas import tpu as pltpu
from jax.sharding import PartitionSpec as P

DISCOUNT_RATE = 0.99
TRACE_LAMBDA = 0.95


def silu_slope(pre):
    sigma = jax.nn.sigmoid(pre)
    return sigma * (1.0 + pre * (1.0 - sigma))


def importance_trace_terms(
    value_estimates,
    policy_logits,
    reward_rows,
    behaviour_probs,
    taken_actions,
    episode_finished,
    sequence_length,
    objective_scale,
):
    seq_count, step_count = value_estimates.shape
    action_count = policy_logits.shape[0]
    positions = jnp.arange(step_count, dtype=jnp.int32)
    valid_mask = (positions[None, :] < sequence_length[:, None]).astype(jnp.float32)
    zero_column = jnp.zeros((seq_count, 1), jnp.float32)
    valid_next = jnp.concatenate([valid_mask[:, 1:], zero_column], axis=1)
    log_probs = jax.nn.log_softmax(policy_logits, axis=0)
    one_hot = (
        jnp.arange(action_count, dtype=jnp.int32)[:, None, None] == taken_actions[None]
    ).astype(jnp.float32)
    chosen = jnp.sum(one_hot * log_probs, axis=0)
    clip_ratio = jnp.exp(jnp.minimum(chosen - behaviour_probs, 0.0))
    discount = DISCOUNT_RATE * (1.0 - episode_finished.astype(jnp.float32))
    next_value = jnp.concatenate([value_estimates[:, 1:], zero_column], axis=1) * valid_next
    td_error = valid_mask * clip_ratio * (reward_rows + discount * next_value - value_estimates)
    trace_coef = discount * TRACE_LAMBDA * clip_ratio * valid_next

    def backward_step(carried, inputs):
        error_now, coef_now = inputs
        updated = error_now + coef_now * carried
        return (updated, updated)

    final_state, stacked = lax.scan(
        backward_step,
        jnp.zeros((seq_count,), jnp.float32),
        (td_error.T, trace_coef.T),
        reverse=True,
    )
    correction = stacked.T
    targets = value_estimates + correction
    next_target = jnp.concatenate([targets[:, 1:], zero_column], axis=1) * valid_next
    policy_adv = clip_ratio * (reward_rows + discount * next_target - value_estimates)
    value_gradient = -objective_scale * valid_mask * correction
    logits_gradient = (
        objective_scale * (valid_mask * policy_adv)[None] * (jnp.exp(log_probs) - one_hot)
    )
    return (value_gradient, logits_gradient)


def head_terms(hidden, value_w, policy_w):
    logit_part = jnp.einsum("rh,ha->ar", hidden, policy_w, preferred_element_type=jnp.float32)
    value_part = jnp.dot(hidden, value_w, preferred_element_type=jnp.float32)
    return jnp.concatenate([logit_part, value_part[None]], axis=0)


def full_rows(online_part, offline_part):
    return (
        lax.all_gather(online_part, "mp", axis=2, tiled=True),
        lax.all_gather(offline_part, "mp", axis=2, tiled=True),
    )


def general_plan(
    online_obs,
    offline_obs,
    online_rewards,
    offline_rewards,
    online_behaviour,
    offline_behaviour,
    online_actions,
    offline_actions,
    online_done,
    offline_done,
    online_lengths,
    offline_lengths,
    torso_weights,
    value_head,
    policy_head,
):
    owned_online = online_lengths.shape[0]
    owned_offline = offline_obs.shape[0]
    step_count = offline_obs.shape[1]
    action_count = policy_head.shape[1]
    record_stack = jnp.stack(
        [
            online_rewards,
            online_behaviour,
            online_actions.astype(jnp.float32),
            online_done.astype(jnp.float32),
        ]
    )
    records = lax.all_to_all(record_stack, "dp", split_axis=2, concat_axis=1, tiled=True)
    slabs = lax.all_to_all(online_obs, "dp", split_axis=1, concat_axis=0, tiled=True)
    x_online, x_offline = full_rows(slabs, offline_obs)
    feature_count = x_online.shape[2]
    x_online = x_online.reshape(step_count * owned_online, feature_count)
    x_offline = x_offline.reshape(owned_offline * step_count, feature_count)
    weight = torso_weights[0]
    pre_online = jnp.dot(x_online, weight, preferred_element_type=jnp.float32)
    pre_offline = jnp.dot(x_offline, weight, preferred_element_type=jnp.float32)
    hidden_online = jax.nn.silu(pre_online).astype(jnp.bfloat16)
    hidden_offline = jax.nn.silu(pre_offline).astype(jnp.bfloat16)
    is_critic = (lax.axis_index("section") == 0).astype(jnp.float32)
    is_policy = 1.0 - is_critic
    row_keep = jnp.where(jnp.arange(action_count + 1) == action_count, is_critic, is_policy)
    partial_value = jnp.concatenate(
        [
            head_terms(hidden_online, value_head, policy_head),
            head_terms(hidden_offline, value_head, policy_head),
        ],
        axis=1,
    )
    partial_value = partial_value * row_keep[:, None]
    heads = lax.psum(partial_value, ("mp", "section"))
    online_count = step_count * owned_online
    logits_on = (
        heads[:action_count, :online_count]
        .reshape(action_count, step_count, owned_online)
        .transpose(0, 2, 1)
    )
    logits_off = heads[:action_count, online_count:].reshape(
        action_count, owned_offline, step_count
    )
    values_on = heads[action_count, :online_count].reshape(step_count, owned_online).T
    values_off = heads[action_count, online_count:].reshape(owned_offline, step_count)
    record_seq = records.transpose(0, 2, 1)
    value_estimates = jnp.concatenate([values_on, values_off], axis=0)
    policy_logits = jnp.concatenate([logits_on, logits_off], axis=1)
    reward_rows = jnp.concatenate([record_seq[0], offline_rewards], axis=0)
    behaviour_probs = jnp.concatenate([record_seq[1], offline_behaviour], axis=0)
    taken_actions = jnp.concatenate([record_seq[2].astype(jnp.int32), offline_actions], axis=0)
    episode_finished = jnp.concatenate([record_seq[3].astype(jnp.int32), offline_done], axis=0)
    sequence_length = jnp.concatenate([online_lengths, offline_lengths], axis=0)
    total_seqs = online_obs.shape[1] + owned_offline * lax.axis_size("dp")
    hidden_total = value_head.shape[0] * lax.axis_size("mp")
    objective_scale = math.sqrt(hidden_total / (total_seqs * step_count))
    value_gradient, logits_gradient = importance_trace_terms(
        value_estimates,
        policy_logits,
        reward_rows,
        behaviour_probs,
        taken_actions,
        episode_finished,
        sequence_length,
        objective_scale,
    )
    value_gradient = value_gradient * is_critic
    logits_gradient = logits_gradient * is_policy
    dv_on = value_gradient[:owned_online].T.reshape(online_count)
    dv_off = value_gradient[owned_online:].reshape(owned_offline * step_count)
    dl_on = logits_gradient[:, :owned_online].transpose(0, 2, 1).reshape(action_count, online_count)
    dl_off = logits_gradient[:, owned_online:].reshape(action_count, owned_offline * step_count)
    value_w = value_head.astype(jnp.float32)
    policy_w = policy_head.astype(jnp.float32)
    dh_on = dv_on[:, None] * value_w[None, :] + jnp.einsum(
        "ar,ha->rh", dl_on, policy_w, precision=lax.Precision.HIGHEST
    )
    dh_off = dv_off[:, None] * value_w[None, :] + jnp.einsum(
        "ar,ha->rh", dl_off, policy_w, precision=lax.Precision.HIGHEST
    )
    dz_online = (dh_on * silu_slope(pre_online)).astype(jnp.bfloat16)
    dz_offline = (dh_off * silu_slope(pre_offline)).astype(jnp.bfloat16)
    local_grad = jnp.einsum("rd,rh->dh", x_online, dz_online, preferred_element_type=jnp.float32)
    local_grad = local_grad + jnp.einsum(
        "rd,rh->dh", x_offline, dz_offline, preferred_element_type=jnp.float32
    )
    summed = lax.psum(local_grad, "dp")
    return summed[None]


HEAD_ROWS = 24
SPLIT_ROWS = 4 * HEAD_ROWS
COLUMN_BLOCK = 256
GRAD_BLOCK = 512
ADD_BLOCKS = 2
ROW_GROUPS = 4
GRAD_CHUNKS = 8
GRAD_LEAD = 5
SEND_LEAD = 3
LANES = 128
CODE_LIMIT = 32512.0
CODE_TAIL = 16
LOG_TWO = math.log(2.0)
SCRATCH_BYTES = 6 * 1024 * 1024
SWAP = ((0, 1), (1, 0))
TO_CENTER = ((0, 1), (3, 2))
CENTER = ((1, 2), (2, 1))
FROM_CENTER = ((1, 0), (2, 3))
VMEM = pl.BlockSpec(memory_space=pltpu.VMEM)
HBM = pl.BlockSpec(memory_space=pltpu.HBM)
SMEM = pl.BlockSpec(memory_space=pltpu.SMEM)
EXPONENTS = pltpu.VMEM((CODE_TAIL, LANES), jnp.float32)


SHORT = pl.CostEstimate(flops=1, bytes_accessed=1, transcendentals=0)


def params():
    return pltpu.CompilerParams(vmem_limit_bytes=SCRATCH_BYTES)


def resident(array):
    return pltpu.with_memory_space_constraint(array, pltpu.VMEM)


def vmem_call(body, place, arrays, outs, name, deps=(), scratch=()):
    operands = list(arrays) + list(deps)

    def run(place_ref, *refs):
        body(place_ref, *refs[: len(arrays)], *refs[len(operands) :])

    return pl.pallas_call(
        run,
        in_specs=[SMEM] + [VMEM] * len(operands),
        out_specs=[VMEM] * len(outs),
        out_shape=[pltpu.VMEM(shape, dtype) for shape, dtype in outs],
        scratch_shapes=list(scratch),
        compiler_params=params(),
        cost_estimate=SHORT,
        name=name,
    )(place, *[resident(x) for x in operands])


def in_hbm(array):
    return pltpu.with_memory_space_constraint(array, pltpu.HBM)


def share_body(place, source, *refs):
    out, sem = refs[-2:]
    count = out.shape[0]
    copy = pltpu.make_async_copy(source.at[pl.ds(place[3] * count, count)], out, sem)
    copy.start()
    copy.wait()


def section_share(place, source, deps):
    groups, width, features = source.shape
    return pl.pallas_call(
        share_body,
        in_specs=[SMEM, HBM] + [VMEM] * len(deps),
        out_specs=VMEM,
        out_shape=pltpu.VMEM((groups // 2, width, features), source.dtype),
        scratch_shapes=[pltpu.SemaphoreType.DMA(())],
        compiler_params=params(),
        cost_estimate=SHORT,
        name="section_share",
    )(place, in_hbm(source), *[resident(x) for x in deps])


def own_half_body(place, source, weight_ref, *refs):
    own_ref, out_ref, sem = refs[-3:]
    groups, width, features = own_ref.shape
    copy = pltpu.make_async_copy(source, own_ref, sem)
    copy.start()
    copy.wait()
    at = pl.multiple_of(place[0] * features, features)
    for first in range(0, groups, ROW_GROUPS):
        part = slice(first, first + ROW_GROUPS)

        def step(h, carry, part=part):
            block = pl.ds(pl.multiple_of(h * COLUMN_BLOCK, COLUMN_BLOCK), COLUMN_BLOCK)
            pre = jnp.dot(
                own_ref[part].reshape(-1, features),
                weight_ref[pl.ds(at, features), block],
                preferred_element_type=jnp.float32,
            )
            out_ref[part, :, block] = pre.reshape(-1, width, COLUMN_BLOCK)
            return carry

        lax.fori_loop(0, weight_ref.shape[1] // COLUMN_BLOCK, step, 0)


def own_half(place, source, weight, deps):
    groups, width, _ = source.shape
    operands = [weight] + deps
    return pl.pallas_call(
        own_half_body,
        in_specs=[SMEM, HBM] + [VMEM] * len(operands),
        out_specs=[VMEM, VMEM],
        out_shape=[
            pltpu.VMEM(source.shape, source.dtype),
            pltpu.VMEM((groups, width, weight.shape[1]), jnp.float32),
        ],
        scratch_shapes=[pltpu.SemaphoreType.DMA(())],
        compiler_params=params(),
        cost_estimate=SHORT,
        name="own_half",
    )(place, in_hbm(source), *[resident(x) for x in operands])


def forward_body(place, pre_ref, got_ref, rest_ref, weight_ref, head_ref, *refs):
    slope_ref, heads_ref, hidden_ref = refs[-3:]
    half, width, features = got_ref.shape
    hidden_count = weight_ref.shape[1]
    m, section = place[0], place[3]
    other_at = pl.multiple_of((1 - m) * features, features)
    count = min(half, ROW_GROUPS)
    for x_ref, start in ((got_ref, section * half), (rest_ref, (1 - section) * half)):
        for first in range(0, half, count):
            at = pl.ds(start + first, count)
            other = x_ref[first : first + count].reshape(-1, features)
            for h in range(0, hidden_count, COLUMN_BLOCK):
                block = slice(h, h + COLUMN_BLOCK)
                pre = jnp.dot(
                    other,
                    weight_ref[pl.ds(other_at, features), block],
                    preferred_element_type=jnp.float32,
                )
                pre = pre + pre_ref[at, :, block].reshape(-1, COLUMN_BLOCK)
                sigma = 0.5 * jnp.tanh(0.5 * pre) + 0.5
                hidden = pre * sigma
                slope = sigma + hidden * (1.0 - sigma)
                slope_ref[at, :, block] = slope.reshape(-1, width, COLUMN_BLOCK)
                hidden_ref[:, block] = hidden.astype(jnp.bfloat16)
            for g in range(count):
                heads = lax.dot_general(
                    head_ref[...],
                    hidden_ref[g * width : (g + 1) * width],
                    (((1,), (1,)), ((), ())),
                    preferred_element_type=jnp.float32,
                )
                heads_ref[start + first + g] = heads[:HEAD_ROWS]


def forward(place, pre, got, rest, weight, head, deps):
    groups, width, hidden_count = pre.shape
    operands = [pre, got, rest, weight, head] + deps
    return pl.pallas_call(
        forward_body,
        in_specs=[SMEM] + [VMEM] * len(operands),
        out_specs=[VMEM, VMEM],
        out_shape=[
            pltpu.VMEM(pre.shape, jnp.float32),
            pltpu.VMEM((groups, HEAD_ROWS, width), jnp.float32),
        ],
        scratch_shapes=[
            pltpu.VMEM((min(groups // 2, ROW_GROUPS) * width, hidden_count), jnp.bfloat16)
        ],
        input_output_aliases={1: 0},
        compiler_params=params(),
        cost_estimate=SHORT,
        name="forward_rows",
    )(place, *[resident(x) for x in operands])


def action_terms(parts, actions, behaviour, action_count):
    heads = sum(parts[1:], start=parts[0])
    row = lax.broadcasted_iota(jnp.int32, heads.shape, 0)
    is_logit = row < action_count
    logits = jnp.where(is_logit, heads, -1e30)
    shifted = logits - jnp.max(logits, axis=0, keepdims=True)
    log_sum = jnp.log(jnp.sum(jnp.exp(shifted), axis=0, keepdims=True))
    log_probs = shifted - log_sum
    taken = row == actions
    chosen = jnp.sum(jnp.where(taken, log_probs, 0.0), axis=0, keepdims=True)
    rho = jnp.exp(jnp.minimum(chosen - behaviour, 0.0))
    spread = jnp.where(is_logit, jnp.exp(log_probs) - taken.astype(jnp.float32), 0.0)
    return heads[action_count : action_count + 1], rho, spread


def trace_terms(value, rho, reward, discount, length, position, axis, reach, scale):
    size = value.shape[axis]
    valid = (position < length).astype(jnp.float32)
    valid_next = (position + 1 < length).astype(jnp.float32)
    next_value = pltpu.roll(value, size - 1, axis) * valid_next
    correction = valid * rho * (reward + discount * next_value - value)
    coef = discount * TRACE_LAMBDA * rho * valid_next
    shift = 1
    while shift < reach:
        correction = correction + coef * pltpu.roll(correction, size - shift, axis)
        coef = coef * pltpu.roll(coef, size - shift, axis)
        shift *= 2
    targets = value + correction
    next_target = pltpu.roll(targets, size - 1, axis) * valid_next
    advantage = rho * (reward + discount * next_target - value)
    return -scale * valid * correction, scale * (valid * advantage)


def split_terms(logit_weight, value_weight, spread, action_count):
    row = lax.broadcasted_iota(jnp.int32, spread.shape, 0)
    full = jnp.where(row == action_count, value_weight, logit_weight * spread)
    high = full.astype(jnp.bfloat16).astype(jnp.float32)
    rest = full - high
    middle = rest.astype(jnp.bfloat16).astype(jnp.float32)
    low = rest - middle
    return jnp.concatenate([high, middle, low, jnp.zeros_like(full)], axis=0).astype(jnp.bfloat16)


def write_back(terms, head_ref, slope, dz_ref, g):
    dh = lax.dot_general(
        terms, head_ref[...], (((0,), (0,)), ((), ())), preferred_element_type=jnp.float32
    )
    dz_ref[g] = (dh * slope).astype(jnp.bfloat16)


def chip_heads_body(place, own, other, both_ref, share_ref):
    both_ref[...] = own[...] + other[...]
    count = share_ref.shape[0]
    share_ref[...] = both_ref[pl.ds(place[3] * count, count)]


def online_heads_body(action_count, place, *refs):
    both, across, far, actions, behaviour, reward, done, lengths = refs[:8]
    pack_ref, spread_ref, other = refs[8:]
    steps = actions.shape[0]
    half, section = steps // 2, place[3]
    other[pl.ds(section * half, half)] = across[...]
    other[pl.ds((1 - section) * half, half)] = far[...]
    for t in range(steps):
        value, rho, spread = action_terms(
            [both[t], other[t]],
            actions[t : t + 1, :],
            behaviour[t : t + 1, :],
            action_count,
        )
        pack_ref[t : t + 1, :] = value
        pack_ref[steps + t : steps + t + 1, :] = rho
        spread_ref[t] = spread
    pack_ref[2 * steps : 3 * steps, :] = reward[...]
    pack_ref[3 * steps : 4 * steps, :] = DISCOUNT_RATE * (1.0 - done[...].astype(jnp.float32))
    pack_ref[4 * steps :, :] = jnp.broadcast_to(lengths[...], (8, lengths.shape[1]))


def online_back_body(action_count, scale, place, *refs):
    blocks, spread, head_ref, slope_ref, dz_ref = refs[:4], *refs[4:]
    steps = spread.shape[0]
    z = place[2]

    def field(i):
        parts = []
        for hop, b in enumerate(blocks):
            part = b[i * steps : (i + 1) * steps, :]
            parts.append(jnp.where(z + hop < len(blocks), part, 0.0) if hop else part)
        return jnp.concatenate(parts, axis=0)

    length = sum(b[4 * steps : 4 * steps + 1, :] for b in blocks).astype(jnp.int32)
    value = field(0)
    position = lax.broadcasted_iota(jnp.int32, value.shape, 0) + z * steps
    value_weight, logit_weight = trace_terms(
        value,
        field(1),
        field(2),
        field(3),
        length,
        position,
        0,
        value.shape[0],
        scale,
    )
    for t in range(steps):
        terms = split_terms(
            logit_weight[t : t + 1, :], value_weight[t : t + 1, :], spread[t], action_count
        )
        write_back(terms, head_ref, slope_ref[t], dz_ref, t)


def offline_back_body(action_count, step_count, scale, place, *refs):
    parts = refs[:4]
    actions, behaviour, reward, done, length, head_ref, slope_ref, dz_ref = refs[4:]
    groups = dz_ref.shape[0]
    values, rhos, spreads = [], [], []
    for g in range(groups):
        value, rho, spread = action_terms(
            [p[g] for p in parts],
            actions[g : g + 1, :],
            behaviour[g : g + 1, :],
            action_count,
        )
        values.append(value)
        rhos.append(rho)
        spreads.append(spread)
    value = jnp.concatenate(values, axis=0)
    rho = jnp.concatenate(rhos, axis=0)
    position = lax.rem(lax.broadcasted_iota(jnp.int32, value.shape, 1), step_count)
    discount = DISCOUNT_RATE * (1.0 - done[...].astype(jnp.float32))
    value_weight, logit_weight = trace_terms(
        value, rho, reward[...], discount, length[...], position, 1, step_count, scale
    )
    for g in range(groups):
        terms = split_terms(
            logit_weight[g : g + 1, :], value_weight[g : g + 1, :], spreads[g], action_count
        )
        write_back(terms, head_ref, slope_ref[g], dz_ref, g)


def encode(v, c, message_ref, exponents_ref):
    rows = v.shape[0]
    largest = jnp.max(jnp.abs(v), axis=0, keepdims=True)
    exponent = jnp.ceil(jnp.log(jnp.maximum(largest, 1e-30)) * (1.0 / LOG_TWO) + 0.01)
    scale = jnp.exp(exponent * -LOG_TWO) * CODE_LIMIT
    code = jnp.floor(v * scale + 0.5)
    at = pl.ds(pl.multiple_of(c * rows, rows), rows)
    message_ref[at, :] = code.astype(jnp.int32).astype(jnp.int16)
    exponents_ref[pl.ds(c, 1), :] = exponent


def encode_tail(message_ref, exponents_ref):
    tail = exponents_ref[...].astype(jnp.int32)
    message_ref[message_ref.shape[0] - CODE_TAIL :, :] = tail.astype(jnp.int16)


def decode_steps(message_ref, steps_ref):
    exponents = message_ref[message_ref.shape[0] - CODE_TAIL :, :]
    exponents = exponents.astype(jnp.int32).astype(jnp.float32)
    steps_ref[...] = jnp.exp(exponents * LOG_TWO) * (1.0 / CODE_LIMIT)


def decode(message_ref, steps_ref, c, rows):
    at = pl.ds(pl.multiple_of(c * rows, rows), rows)
    code = message_ref[at, :].astype(jnp.int32).astype(jnp.float32)
    return code * steps_ref[pl.ds(c, 1), :]


def message_of(rows, columns):
    return ((rows * (columns // LANES) + CODE_TAIL, LANES), jnp.int16)


def grad_body(pieces, column, columns, place, *refs):
    xs, dzs = refs[: len(pieces)], refs[len(pieces) : len(pieces) + 2]
    message_ref, exponents_ref = refs[-2:]
    hidden_count = dzs[0].shape[2]
    section = place[3]
    at = slice(column * columns, (column + 1) * columns)
    exponents_ref[...] = jnp.zeros_like(exponents_ref)

    def step(h, carry):
        block = pl.ds(pl.multiple_of(h * GRAD_BLOCK, GRAD_BLOCK), GRAD_BLOCK)
        total = None
        for x, (which, swapped) in zip(xs, pieces):
            groups, width, _ = x.shape
            first = 0
            if swapped is not None:
                first = (1 - section if swapped else section) * groups
            part = lax.dot_general(
                x[:, :, at].reshape(groups * width, columns),
                dzs[which][pl.ds(first, groups), :, block].reshape(groups * width, GRAD_BLOCK),
                (((0,), (0,)), ((), ())),
                preferred_element_type=jnp.float32,
            )
            total = part if total is None else total + part
        per_block = GRAD_BLOCK // LANES
        for c in range(per_block):
            lanes = total[:, c * LANES : (c + 1) * LANES]
            encode(lanes, h * per_block + c, message_ref, exponents_ref)
        return carry

    lax.fori_loop(0, hidden_count // GRAD_BLOCK, step, 0)
    encode_tail(message_ref, exponents_ref)


def grad_chunk(place, pieces, dzs, column, columns, deps):
    hidden_count = dzs[0].shape[2]
    return vmem_call(
        functools.partial(grad_body, [p[1:] for p in pieces], column, columns),
        place,
        [x for x, _, _ in pieces] + dzs,
        [message_of(columns, hidden_count)],
        "grad_chunk",
        deps,
        [EXPONENTS],
    )[0]


def add_body(count, place, a_ref, b_ref, out_ref, exponents_ref, a_steps, b_steps):
    rows = (out_ref.shape[0] - CODE_TAIL) // count
    decode_steps(a_ref, a_steps)
    decode_steps(b_ref, b_steps)
    exponents_ref[...] = jnp.zeros_like(exponents_ref)

    def step(i, carry):
        for j in range(ADD_BLOCKS):
            c = i * ADD_BLOCKS + j
            v = decode(a_ref, a_steps, c, rows) + decode(b_ref, b_steps, c, rows)
            encode(v, c, out_ref, exponents_ref)
        return carry

    lax.fori_loop(0, count // ADD_BLOCKS, step, 0)
    encode_tail(out_ref, exponents_ref)


def add_chunk(place, a, b, count, deps):
    return vmem_call(
        functools.partial(add_body, count),
        place,
        [a, b],
        [(a.shape, a.dtype)],
        "add_chunk",
        deps,
        [EXPONENTS] * 3,
    )[0]


def place_body(count, rows, of_own, index, place, total, received, *refs):
    out, token, held, steps, sem = refs[-5:]
    token[...] = jnp.zeros_like(token)
    half = place[0] if of_own else 1 - place[0]
    first = pl.multiple_of(half * (out.shape[0] // 2) + index * rows, rows)
    at_end = place[1] == 1

    def write(message):
        decode_steps(message, steps)
        for c in range(count):
            held[:, c * LANES : (c + 1) * LANES] = decode(message, steps, c, rows)

    @pl.when(at_end)
    def _():
        write(received)

    @pl.when(jnp.logical_not(at_end))
    def _():
        write(total)

    copy = pltpu.make_async_copy(held, out.at[pl.ds(first, rows)], sem)
    copy.start()
    copy.wait()


def place_chunk(place, total, received, result, of_own, index, rows, shape, deps):
    hidden_count = shape[1]
    earlier = [] if result is None else [result]
    operands = [total, received] + deps
    return pl.pallas_call(
        functools.partial(place_body, hidden_count // LANES, rows, of_own, index),
        in_specs=[SMEM]
        + [VMEM] * len(operands)
        + [pl.BlockSpec(memory_space=pl.ANY) for _ in earlier],
        out_specs=[pl.BlockSpec(memory_space=pl.ANY), VMEM],
        out_shape=[
            jax.ShapeDtypeStruct(shape, jnp.float32),
            pltpu.VMEM((8, LANES), jnp.float32),
        ],
        scratch_shapes=[
            pltpu.VMEM((rows, hidden_count), jnp.float32),
            EXPONENTS,
            pltpu.SemaphoreType.DMA(()),
        ],
        input_output_aliases={1 + len(operands): 0} if earlier else {},
        compiler_params=params(),
        cost_estimate=SHORT,
        name="place_chunk",
    )(place, *[resident(x) for x in operands], *earlier)


def pipeline_order(count, lead):
    order = [("grad", k) for k in range(min(lead, count))]
    ahead = len(order)
    for k in range(count + 2):
        if k < count:
            order.append(("partial", k))
            while ahead < min(count, lead + 2 * (k + 1)):
                order.append(("grad", ahead))
                ahead += 1
        if 0 <= k - 1 < count:
            order.append(("total", k - 1))
        if 0 <= k - 2 < count:
            order.append(("place", k - 2))
    return order


def after(array, *others):
    return lax.optimization_barrier((array,) + others)[0]


def line_plan(
    online_obs,
    offline_obs,
    online_rewards,
    offline_rewards,
    online_behaviour,
    offline_behaviour,
    online_actions,
    offline_actions,
    online_done,
    offline_done,
    online_lengths,
    offline_lengths,
    torso_weights,
    value_head,
    policy_head,
):
    section = lax.axis_index("section")
    m = lax.axis_index("mp")
    z = lax.axis_index("dp")
    dp = lax.axis_size("dp")
    steps, online_count, features = online_obs.shape
    offline_count, step_count, _ = offline_obs.shape
    action_count = policy_head.shape[1]
    hidden_count = value_head.shape[0]
    at_end = ((z == 0) | (z == dp - 1)).astype(jnp.int32)
    place = jnp.stack([m, at_end, z, section]).astype(jnp.int32)
    weight = torso_weights[0]
    scale = math.sqrt(
        hidden_count
        * lax.axis_size("mp")
        / ((online_count + offline_count * dp) * step_count)
    )

    offline_groups = offline_count // 2
    offline_rows = offline_obs.reshape(offline_groups, 2 * step_count, features)
    halves = [section_share(place, online_obs, [])]
    halves.append(section_share(place, offline_rows, [halves[0]]))

    policy_rows = jnp.where(section == 1, policy_head.T, 0)
    value_row = jnp.where(section == 0, value_head[None], 0)
    head = jnp.concatenate([policy_rows, value_row], axis=0).astype(jnp.bfloat16)
    head = jnp.pad(head, ((0, HEAD_ROWS - action_count - 1), (0, 0)))
    forward_head = jnp.pad(head, ((0, 32 - HEAD_ROWS), (0, 0)))
    back_head = jnp.concatenate([head, head, head, jnp.zeros_like(head)], axis=0)

    owned = online_lengths.shape[0]
    length_row = lax.dynamic_update_slice(
        jnp.zeros((online_count,), jnp.float32), online_lengths.astype(jnp.float32), (z * owned,)
    )
    length_row = length_row[None]
    lanes = (offline_groups, 2 * step_count)
    offline_length = jnp.broadcast_to(offline_lengths[:, None], (offline_count, step_count))
    offline_terms = [
        x.reshape(lanes)
        for x in (
            offline_actions,
            offline_behaviour,
            offline_rewards,
            offline_done,
            offline_length,
        )
    ]

    got = [lax.ppermute(half, "mp", SWAP) for half in halves]
    early = halves + [back_head, forward_head, length_row] + offline_terms
    own_online, pre_online = own_half(place, online_obs, weight, early)
    own_offline, pre_offline = own_half(place, offline_rows, weight, [pre_online])
    rests = [lax.ppermute(after(got[0], pre_offline), "section", SWAP)]
    online_slope, online_part = forward(
        place, pre_online, got[0], rests[0], weight, forward_head, []
    )
    both, share = vmem_call(
        chip_heads_body,
        place,
        [online_part, lax.ppermute(online_part, "section", SWAP)],
        [
            (online_part.shape, jnp.float32),
            ((steps // 2, HEAD_ROWS, online_count), jnp.float32),
        ],
        "chip_heads",
    )
    across_heads = lax.ppermute(share, "mp", SWAP)
    rests.append(lax.ppermute(after(got[1], both), "section", SWAP))
    offline_slope, offline_part = forward(
        place, pre_offline, got[1], rests[1], weight, forward_head, [both]
    )
    across_offline = lax.ppermute(offline_part, "mp", SWAP)
    offline_parts = [offline_part, lax.ppermute(offline_part, "section", SWAP), across_offline]
    far_heads = lax.ppermute(after(across_heads, offline_part), "section", SWAP)
    pack, spread = vmem_call(
        functools.partial(online_heads_body, action_count),
        place,
        [both, across_heads, far_heads]
        + [online_actions, online_behaviour, online_rewards, online_done, length_row],
        [
            ((4 * steps + 8, online_count), jnp.float32),
            ((steps, HEAD_ROWS, online_count), jnp.float32),
        ],
        "online_heads",
        [offline_part],
        [pltpu.VMEM((steps, HEAD_ROWS, online_count), jnp.float32)],
    )

    blocks = [pack]
    for hop in range(1, dp):
        pairs = [(i, (i - hop) % dp) for i in range(dp)]
        blocks.append(lax.ppermute(pack, "dp", pairs))
    offline_parts.append(lax.ppermute(after(across_offline, pack), "section", SWAP))
    (dz_offline,) = vmem_call(
        functools.partial(offline_back_body, action_count, step_count, scale),
        place,
        offline_parts + offline_terms + [back_head, offline_slope],
        [(offline_slope.shape, jnp.bfloat16)],
        "offline_back",
        [pack],
    )

    (dz_online,) = vmem_call(
        functools.partial(online_back_body, action_count, scale),
        place,
        blocks + [spread, back_head, online_slope],
        [(online_slope.shape, jnp.bfloat16)],
        "online_back",
        [dz_offline],
    )

    own_x = [(own_online, 0, None), (own_offline, 1, None)]
    other_x = []
    for which in range(2):
        other_x += [(got[which], which, 0), (rests[which], which, 1)]
    columns = 2 * features // GRAD_CHUNKS
    per_half = GRAD_CHUNKS // 2
    lane_blocks = hidden_count // LANES

    messages, inward, partial, across, total, outward = {}, {}, {}, {}, {}, {}
    result, last = None, dz_online
    for kind, k in pipeline_order(GRAD_CHUNKS, GRAD_LEAD):
        if kind == "grad":
            last = messages[k] = grad_chunk(
                place,
                own_x if k < per_half else other_x,
                [dz_online, dz_offline],
                k % per_half,
                columns,
                [last],
            )
            if k < SEND_LEAD:
                inward[k] = lax.ppermute(last, "dp", TO_CENTER)
        elif kind == "partial":
            last = partial[k] = add_chunk(place, messages[k], inward[k], lane_blocks, [last])
            across[k] = lax.ppermute(last, "dp", CENTER)
        elif kind == "total":
            last = total[k] = add_chunk(place, partial[k], across[k], lane_blocks, [last])
            outward[k] = lax.ppermute(last, "dp", FROM_CENTER)
            ahead = k + SEND_LEAD
            if ahead < GRAD_CHUNKS:
                inward[ahead] = lax.ppermute(after(messages[ahead], last), "dp", TO_CENTER)
        else:
            result, last = place_chunk(
                place,
                total[k],
                outward[k],
                result,
                k < per_half,
                k % per_half,
                columns,
                (2 * features, hidden_count),
                [last],
            )
    return result[None]


def solution(mesh):
    on_line = mesh.shape["dp"] == 4 and mesh.shape["mp"] == 2 and mesh.shape["section"] == 2
    in_specs = (
        P("dp", "groups", "mp"),
        P(("groups", "dp"), None, "mp"),
        P("dp", "groups"),
        P(("groups", "dp"), None),
        P("dp", "groups"),
        P(("groups", "dp"), None),
        P("dp", "groups"),
        P(("groups", "dp"), None),
        P("dp", "groups"),
        P(("groups", "dp"), None),
        P(("groups", "dp")),
        P(("groups", "dp")),
        P("section", None, "mp"),
        P("mp"),
        P("mp", None),
    )
    out_specs = P(("groups", "section"), None, "mp")
    per_device = line_plan if on_line else general_plan
    return jax.shard_map(
        per_device, mesh=mesh, in_specs=in_specs, out_specs=out_specs, check_vma=False
    )
```

```python
import functools
import math

import jax
import jax.numpy as jnp
from jax import lax
from jax.experimental import pallas as pl
from jax.experimental.pallas import tpu as pltpu
from jax.sharding import PartitionSpec as P

DISCOUNT_RATE = 0.99
TRACE_LAMBDA = 0.95


def silu_slope(pre):
    sigma = jax.nn.sigmoid(pre)
    return sigma * (1.0 + pre * (1.0 - sigma))


def importance_trace_terms(
    value_estimates,
    policy_logits,
    reward_rows,
    behaviour_probs,
    taken_actions,
    episode_finished,
    sequence_length,
    objective_scale,
):
    seq_count, step_count = value_estimates.shape
    action_count = policy_logits.shape[0]
    positions = jnp.arange(step_count, dtype=jnp.int32)
    valid_mask = (positions[None, :] < sequence_length[:, None]).astype(jnp.float32)
    zero_column = jnp.zeros((seq_count, 1), jnp.float32)
    valid_next = jnp.concatenate([valid_mask[:, 1:], zero_column], axis=1)
    log_probs = jax.nn.log_softmax(policy_logits, axis=0)
    one_hot = (
        jnp.arange(action_count, dtype=jnp.int32)[:, None, None] == taken_actions[None]
    ).astype(jnp.float32)
    chosen = jnp.sum(one_hot * log_probs, axis=0)
    clip_ratio = jnp.exp(jnp.minimum(chosen - behaviour_probs, 0.0))
    discount = DISCOUNT_RATE * (1.0 - episode_finished.astype(jnp.float32))
    next_value = jnp.concatenate([value_estimates[:, 1:], zero_column], axis=1) * valid_next
    td_error = valid_mask * clip_ratio * (reward_rows + discount * next_value - value_estimates)
    trace_coef = discount * TRACE_LAMBDA * clip_ratio * valid_next

    def backward_step(carried, inputs):
        error_now, coef_now = inputs
        updated = error_now + coef_now * carried
        return (updated, updated)

    final_state, stacked = lax.scan(
        backward_step,
        jnp.zeros((seq_count,), jnp.float32),
        (td_error.T, trace_coef.T),
        reverse=True,
    )
    correction = stacked.T
    targets = value_estimates + correction
    next_target = jnp.concatenate([targets[:, 1:], zero_column], axis=1) * valid_next
    policy_adv = clip_ratio * (reward_rows + discount * next_target - value_estimates)
    value_gradient = -objective_scale * valid_mask * correction
    logits_gradient = (
        objective_scale * (valid_mask * policy_adv)[None] * (jnp.exp(log_probs) - one_hot)
    )
    return (value_gradient, logits_gradient)


def head_terms(hidden, value_w, policy_w):
    logit_part = jnp.einsum("rh,ha->ar", hidden, policy_w, preferred_element_type=jnp.float32)
    value_part = jnp.dot(hidden, value_w, preferred_element_type=jnp.float32)
    return jnp.concatenate([logit_part, value_part[None]], axis=0)


def full_rows(online_part, offline_part):
    return (
        lax.all_gather(online_part, "mp", axis=2, tiled=True),
        lax.all_gather(offline_part, "mp", axis=2, tiled=True),
    )


def general_plan(
    online_obs,
    offline_obs,
    online_rewards,
    offline_rewards,
    online_behaviour,
    offline_behaviour,
    online_actions,
    offline_actions,
    online_done,
    offline_done,
    online_lengths,
    offline_lengths,
    torso_weights,
    value_head,
    policy_head,
):
    owned_online = online_lengths.shape[0]
    owned_offline = offline_obs.shape[0]
    step_count = offline_obs.shape[1]
    action_count = policy_head.shape[1]
    record_stack = jnp.stack(
        [
            online_rewards,
            online_behaviour,
            online_actions.astype(jnp.float32),
            online_done.astype(jnp.float32),
        ]
    )
    records = lax.all_to_all(record_stack, "dp", split_axis=2, concat_axis=1, tiled=True)
    slabs = lax.all_to_all(online_obs, "dp", split_axis=1, concat_axis=0, tiled=True)
    x_online, x_offline = full_rows(slabs, offline_obs)
    feature_count = x_online.shape[2]
    x_online = x_online.reshape(step_count * owned_online, feature_count)
    x_offline = x_offline.reshape(owned_offline * step_count, feature_count)
    weight = torso_weights[0]
    pre_online = jnp.dot(x_online, weight, preferred_element_type=jnp.float32)
    pre_offline = jnp.dot(x_offline, weight, preferred_element_type=jnp.float32)
    hidden_online = jax.nn.silu(pre_online).astype(jnp.bfloat16)
    hidden_offline = jax.nn.silu(pre_offline).astype(jnp.bfloat16)
    is_critic = (lax.axis_index("section") == 0).astype(jnp.float32)
    is_policy = 1.0 - is_critic
    row_keep = jnp.where(jnp.arange(action_count + 1) == action_count, is_critic, is_policy)
    partial_value = jnp.concatenate(
        [
            head_terms(hidden_online, value_head, policy_head),
            head_terms(hidden_offline, value_head, policy_head),
        ],
        axis=1,
    )
    partial_value = partial_value * row_keep[:, None]
    heads = lax.psum(partial_value, ("mp", "section"))
    online_count = step_count * owned_online
    logits_on = (
        heads[:action_count, :online_count]
        .reshape(action_count, step_count, owned_online)
        .transpose(0, 2, 1)
    )
    logits_off = heads[:action_count, online_count:].reshape(
        action_count, owned_offline, step_count
    )
    values_on = heads[action_count, :online_count].reshape(step_count, owned_online).T
    values_off = heads[action_count, online_count:].reshape(owned_offline, step_count)
    record_seq = records.transpose(0, 2, 1)
    value_estimates = jnp.concatenate([values_on, values_off], axis=0)
    policy_logits = jnp.concatenate([logits_on, logits_off], axis=1)
    reward_rows = jnp.concatenate([record_seq[0], offline_rewards], axis=0)
    behaviour_probs = jnp.concatenate([record_seq[1], offline_behaviour], axis=0)
    taken_actions = jnp.concatenate([record_seq[2].astype(jnp.int32), offline_actions], axis=0)
    episode_finished = jnp.concatenate([record_seq[3].astype(jnp.int32), offline_done], axis=0)
    sequence_length = jnp.concatenate([online_lengths, offline_lengths], axis=0)
    total_seqs = online_obs.shape[1] + owned_offline * lax.axis_size("dp")
    hidden_total = value_head.shape[0] * lax.axis_size("mp")
    objective_scale = math.sqrt(hidden_total / (total_seqs * step_count))
    value_gradient, logits_gradient = importance_trace_terms(
        value_estimates,
        policy_logits,
        reward_rows,
        behaviour_probs,
        taken_actions,
        episode_finished,
        sequence_length,
        objective_scale,
    )
    value_gradient = value_gradient * is_critic
    logits_gradient = logits_gradient * is_policy
    dv_on = value_gradient[:owned_online].T.reshape(online_count)
    dv_off = value_gradient[owned_online:].reshape(owned_offline * step_count)
    dl_on = logits_gradient[:, :owned_online].transpose(0, 2, 1).reshape(action_count, online_count)
    dl_off = logits_gradient[:, owned_online:].reshape(action_count, owned_offline * step_count)
    value_w = value_head.astype(jnp.float32)
    policy_w = policy_head.astype(jnp.float32)
    dh_on = dv_on[:, None] * value_w[None, :] + jnp.einsum(
        "ar,ha->rh", dl_on, policy_w, precision=lax.Precision.HIGHEST
    )
    dh_off = dv_off[:, None] * value_w[None, :] + jnp.einsum(
        "ar,ha->rh", dl_off, policy_w, precision=lax.Precision.HIGHEST
    )
    dz_online = (dh_on * silu_slope(pre_online)).astype(jnp.bfloat16)
    dz_offline = (dh_off * silu_slope(pre_offline)).astype(jnp.bfloat16)
    local_grad = jnp.einsum("rd,rh->dh", x_online, dz_online, preferred_element_type=jnp.float32)
    local_grad = local_grad + jnp.einsum(
        "rd,rh->dh", x_offline, dz_offline, preferred_element_type=jnp.float32
    )
    summed = lax.psum(local_grad, "dp")
    return summed[None]


HEAD_ROWS = 24
SPLIT_ROWS = 4 * HEAD_ROWS
COLUMN_BLOCK = 256
GRAD_BLOCK = 512
ADD_BLOCKS = 2
ROW_GROUPS = 4
GRAD_CHUNKS = 8
GRAD_LEAD = 6
SEND_LEAD = 3
LANES = 128
CODE_LIMIT = 32512.0
CODE_TAIL = 16
LOG_TWO = math.log(2.0)
SCRATCH_BYTES = 6 * 1024 * 1024
SWAP = ((0, 1), (1, 0))
TO_CENTER = ((0, 1), (3, 2))
CENTER = ((1, 2), (2, 1))
FROM_CENTER = ((1, 0), (2, 3))
VMEM = pl.BlockSpec(memory_space=pltpu.VMEM)
HBM = pl.BlockSpec(memory_space=pltpu.HBM)
SMEM = pl.BlockSpec(memory_space=pltpu.SMEM)
EXPONENTS = pltpu.VMEM((CODE_TAIL, LANES), jnp.float32)


SHORT = pl.CostEstimate(flops=1, bytes_accessed=1, transcendentals=0)


def params():
    return pltpu.CompilerParams(vmem_limit_bytes=SCRATCH_BYTES)


def resident(array):
    return pltpu.with_memory_space_constraint(array, pltpu.VMEM)


def vmem_call(body, place, arrays, outs, name, deps=(), scratch=()):
    operands = list(arrays) + list(deps)

    def run(place_ref, *refs):
        body(place_ref, *refs[: len(arrays)], *refs[len(operands) :])

    return pl.pallas_call(
        run,
        in_specs=[SMEM] + [VMEM] * len(operands),
        out_specs=[VMEM] * len(outs),
        out_shape=[pltpu.VMEM(shape, dtype) for shape, dtype in outs],
        scratch_shapes=list(scratch),
        compiler_params=params(),
        cost_estimate=SHORT,
        name=name,
    )(place, *[resident(x) for x in operands])


def in_hbm(array):
    return pltpu.with_memory_space_constraint(array, pltpu.HBM)


def share_body(place, source, *refs):
    out, sem = refs[-2:]
    count = out.shape[0]
    copy = pltpu.make_async_copy(source.at[pl.ds(place[3] * count, count)], out, sem)
    copy.start()
    copy.wait()


def section_share(place, source, deps):
    groups, width, features = source.shape
    return pl.pallas_call(
        share_body,
        in_specs=[SMEM, HBM] + [VMEM] * len(deps),
        out_specs=VMEM,
        out_shape=pltpu.VMEM((groups // 2, width, features), source.dtype),
        scratch_shapes=[pltpu.SemaphoreType.DMA(())],
        compiler_params=params(),
        cost_estimate=SHORT,
        name="section_share",
    )(place, in_hbm(source), *[resident(x) for x in deps])


def own_half_body(place, source, weight_ref, *refs):
    own_ref, out_ref, sem = refs[-3:]
    groups, width, features = own_ref.shape
    copy = pltpu.make_async_copy(source, own_ref, sem)
    copy.start()
    copy.wait()
    at = pl.multiple_of(place[0] * features, features)
    for first in range(0, groups, ROW_GROUPS):
        part = slice(first, first + ROW_GROUPS)

        def step(h, carry, part=part):
            block = pl.ds(pl.multiple_of(h * COLUMN_BLOCK, COLUMN_BLOCK), COLUMN_BLOCK)
            pre = jnp.dot(
                own_ref[part].reshape(-1, features),
                weight_ref[pl.ds(at, features), block],
                preferred_element_type=jnp.float32,
            )
            out_ref[part, :, block] = pre.reshape(-1, width, COLUMN_BLOCK)
            return carry

        lax.fori_loop(0, weight_ref.shape[1] // COLUMN_BLOCK, step, 0)


def own_half(place, source, weight, deps):
    groups, width, _ = source.shape
    operands = [weight] + deps
    return pl.pallas_call(
        own_half_body,
        in_specs=[SMEM, HBM] + [VMEM] * len(operands),
        out_specs=[VMEM, VMEM],
        out_shape=[
            pltpu.VMEM(source.shape, source.dtype),
            pltpu.VMEM((groups, width, weight.shape[1]), jnp.float32),
        ],
        scratch_shapes=[pltpu.SemaphoreType.DMA(())],
        compiler_params=params(),
        cost_estimate=SHORT,
        name="own_half",
    )(place, in_hbm(source), *[resident(x) for x in operands])


def forward_body(place, pre_ref, got_ref, rest_ref, weight_ref, head_ref, *refs):
    slope_ref, heads_ref, hidden_ref = refs[-3:]
    half, width, features = got_ref.shape
    hidden_count = weight_ref.shape[1]
    m, section = place[0], place[3]
    other_at = pl.multiple_of((1 - m) * features, features)
    count = min(half, ROW_GROUPS)
    for x_ref, start in ((got_ref, section * half), (rest_ref, (1 - section) * half)):
        for first in range(0, half, count):
            at = pl.ds(start + first, count)
            other = x_ref[first : first + count].reshape(-1, features)
            for h in range(0, hidden_count, COLUMN_BLOCK):
                block = slice(h, h + COLUMN_BLOCK)
                pre = jnp.dot(
                    other,
                    weight_ref[pl.ds(other_at, features), block],
                    preferred_element_type=jnp.float32,
                )
                pre = pre + pre_ref[at, :, block].reshape(-1, COLUMN_BLOCK)
                sigma = 0.5 * jnp.tanh(0.5 * pre) + 0.5
                hidden = pre * sigma
                slope = sigma + hidden * (1.0 - sigma)
                slope_ref[at, :, block] = slope.reshape(-1, width, COLUMN_BLOCK)
                hidden_ref[:, block] = hidden.astype(jnp.bfloat16)
            for g in range(count):
                heads = lax.dot_general(
                    head_ref[...],
                    hidden_ref[g * width : (g + 1) * width],
                    (((1,), (1,)), ((), ())),
                    preferred_element_type=jnp.float32,
                )
                heads_ref[start + first + g] = heads[:HEAD_ROWS]


def forward(place, pre, got, rest, weight, head, deps):
    groups, width, hidden_count = pre.shape
    operands = [pre, got, rest, weight, head] + deps
    return pl.pallas_call(
        forward_body,
        in_specs=[SMEM] + [VMEM] * len(operands),
        out_specs=[VMEM, VMEM],
        out_shape=[
            pltpu.VMEM(pre.shape, jnp.float32),
            pltpu.VMEM((groups, HEAD_ROWS, width), jnp.float32),
        ],
        scratch_shapes=[
            pltpu.VMEM((min(groups // 2, ROW_GROUPS) * width, hidden_count), jnp.bfloat16)
        ],
        input_output_aliases={1: 0},
        compiler_params=params(),
        cost_estimate=SHORT,
        name="forward_rows",
    )(place, *[resident(x) for x in operands])


def action_terms(parts, actions, behaviour, action_count):
    heads = sum(parts[1:], start=parts[0])
    row = lax.broadcasted_iota(jnp.int32, heads.shape, 0)
    is_logit = row < action_count
    logits = jnp.where(is_logit, heads, -1e30)
    shifted = logits - jnp.max(logits, axis=0, keepdims=True)
    log_sum = jnp.log(jnp.sum(jnp.exp(shifted), axis=0, keepdims=True))
    log_probs = shifted - log_sum
    taken = row == actions
    chosen = jnp.sum(jnp.where(taken, log_probs, 0.0), axis=0, keepdims=True)
    rho = jnp.exp(jnp.minimum(chosen - behaviour, 0.0))
    spread = jnp.where(is_logit, jnp.exp(log_probs) - taken.astype(jnp.float32), 0.0)
    return heads[action_count : action_count + 1], rho, spread


def trace_terms(value, rho, reward, discount, length, position, axis, reach, scale):
    size = value.shape[axis]
    valid = (position < length).astype(jnp.float32)
    valid_next = (position + 1 < length).astype(jnp.float32)
    next_value = pltpu.roll(value, size - 1, axis) * valid_next
    correction = valid * rho * (reward + discount * next_value - value)
    coef = discount * TRACE_LAMBDA * rho * valid_next
    shift = 1
    while shift < reach:
        correction = correction + coef * pltpu.roll(correction, size - shift, axis)
        coef = coef * pltpu.roll(coef, size - shift, axis)
        shift *= 2
    targets = value + correction
    next_target = pltpu.roll(targets, size - 1, axis) * valid_next
    advantage = rho * (reward + discount * next_target - value)
    return -scale * valid * correction, scale * (valid * advantage)


def split_terms(logit_weight, value_weight, spread, action_count):
    row = lax.broadcasted_iota(jnp.int32, spread.shape, 0)
    full = jnp.where(row == action_count, value_weight, logit_weight * spread)
    high = full.astype(jnp.bfloat16).astype(jnp.float32)
    rest = full - high
    middle = rest.astype(jnp.bfloat16).astype(jnp.float32)
    low = rest - middle
    return jnp.concatenate([high, middle, low, jnp.zeros_like(full)], axis=0).astype(jnp.bfloat16)


def write_back(terms, head_ref, slope, dz_ref, g):
    dh = lax.dot_general(
        terms, head_ref[...], (((0,), (0,)), ((), ())), preferred_element_type=jnp.float32
    )
    dz_ref[g] = (dh * slope).astype(jnp.bfloat16)


def chip_heads_body(place, own, other, both_ref, share_ref):
    both_ref[...] = own[...] + other[...]
    count = share_ref.shape[0]
    share_ref[...] = both_ref[pl.ds(place[3] * count, count)]


def online_heads_body(action_count, place, *refs):
    both, across, far, actions, behaviour, reward, done, lengths = refs[:8]
    pack_ref, spread_ref, other = refs[8:]
    steps = actions.shape[0]
    half, section = steps // 2, place[3]
    other[pl.ds(section * half, half)] = across[...]
    other[pl.ds((1 - section) * half, half)] = far[...]
    for t in range(steps):
        value, rho, spread = action_terms(
            [both[t], other[t]],
            actions[t : t + 1, :],
            behaviour[t : t + 1, :],
            action_count,
        )
        pack_ref[t : t + 1, :] = value
        pack_ref[steps + t : steps + t + 1, :] = rho
        spread_ref[t] = spread
    pack_ref[2 * steps : 3 * steps, :] = reward[...]
    pack_ref[3 * steps : 4 * steps, :] = DISCOUNT_RATE * (1.0 - done[...].astype(jnp.float32))
    pack_ref[4 * steps :, :] = jnp.broadcast_to(lengths[...], (8, lengths.shape[1]))


def online_back_body(action_count, scale, place, *refs):
    blocks, spread, head_ref, slope_ref, dz_ref = refs[:4], *refs[4:]
    steps = spread.shape[0]
    z = place[2]

    def field(i):
        parts = []
        for hop, b in enumerate(blocks):
            part = b[i * steps : (i + 1) * steps, :]
            parts.append(jnp.where(z + hop < len(blocks), part, 0.0) if hop else part)
        return jnp.concatenate(parts, axis=0)

    length = sum(b[4 * steps : 4 * steps + 1, :] for b in blocks).astype(jnp.int32)
    value = field(0)
    position = lax.broadcasted_iota(jnp.int32, value.shape, 0) + z * steps
    value_weight, logit_weight = trace_terms(
        value,
        field(1),
        field(2),
        field(3),
        length,
        position,
        0,
        value.shape[0],
        scale,
    )
    for t in range(steps):
        terms = split_terms(
            logit_weight[t : t + 1, :], value_weight[t : t + 1, :], spread[t], action_count
        )
        write_back(terms, head_ref, slope_ref[t], dz_ref, t)


def offline_back_body(action_count, step_count, scale, place, *refs):
    parts = refs[:4]
    actions, behaviour, reward, done, length, head_ref, slope_ref, dz_ref = refs[4:]
    groups = dz_ref.shape[0]
    values, rhos, spreads = [], [], []
    for g in range(groups):
        value, rho, spread = action_terms(
            [p[g] for p in parts],
            actions[g : g + 1, :],
            behaviour[g : g + 1, :],
            action_count,
        )
        values.append(value)
        rhos.append(rho)
        spreads.append(spread)
    value = jnp.concatenate(values, axis=0)
    rho = jnp.concatenate(rhos, axis=0)
    position = lax.rem(lax.broadcasted_iota(jnp.int32, value.shape, 1), step_count)
    discount = DISCOUNT_RATE * (1.0 - done[...].astype(jnp.float32))
    value_weight, logit_weight = trace_terms(
        value, rho, reward[...], discount, length[...], position, 1, step_count, scale
    )
    for g in range(groups):
        terms = split_terms(
            logit_weight[g : g + 1, :], value_weight[g : g + 1, :], spreads[g], action_count
        )
        write_back(terms, head_ref, slope_ref[g], dz_ref, g)


def encode(v, c, message_ref, exponents_ref):
    rows = v.shape[0]
    largest = jnp.max(jnp.abs(v), axis=0, keepdims=True)
    exponent = jnp.ceil(jnp.log(jnp.maximum(largest, 1e-30)) * (1.0 / LOG_TWO) + 0.01)
    scale = jnp.exp(exponent * -LOG_TWO) * CODE_LIMIT
    code = jnp.floor(v * scale + 0.5)
    at = pl.ds(pl.multiple_of(c * rows, rows), rows)
    message_ref[at, :] = code.astype(jnp.int32).astype(jnp.int16)
    exponents_ref[pl.ds(c, 1), :] = exponent


def encode_tail(message_ref, exponents_ref):
    tail = exponents_ref[...].astype(jnp.int32)
    message_ref[message_ref.shape[0] - CODE_TAIL :, :] = tail.astype(jnp.int16)


def decode_steps(message_ref, steps_ref):
    exponents = message_ref[message_ref.shape[0] - CODE_TAIL :, :]
    exponents = exponents.astype(jnp.int32).astype(jnp.float32)
    steps_ref[...] = jnp.exp(exponents * LOG_TWO) * (1.0 / CODE_LIMIT)


def decode(message_ref, steps_ref, c, rows):
    at = pl.ds(pl.multiple_of(c * rows, rows), rows)
    code = message_ref[at, :].astype(jnp.int32).astype(jnp.float32)
    return code * steps_ref[pl.ds(c, 1), :]


def message_of(rows, columns):
    return ((rows * (columns // LANES) + CODE_TAIL, LANES), jnp.int16)


def grad_body(pieces, column, columns, place, *refs):
    xs, dzs = refs[: len(pieces)], refs[len(pieces) : len(pieces) + 2]
    message_ref, exponents_ref = refs[-2:]
    hidden_count = dzs[0].shape[2]
    section = place[3]
    at = slice(column * columns, (column + 1) * columns)
    exponents_ref[...] = jnp.zeros_like(exponents_ref)

    def step(h, carry):
        block = pl.ds(pl.multiple_of(h * GRAD_BLOCK, GRAD_BLOCK), GRAD_BLOCK)
        total = None
        for x, (which, swapped) in zip(xs, pieces):
            groups, width, _ = x.shape
            first = 0
            if swapped is not None:
                first = (1 - section if swapped else section) * groups
            part = lax.dot_general(
                x[:, :, at].reshape(groups * width, columns),
                dzs[which][pl.ds(first, groups), :, block].reshape(groups * width, GRAD_BLOCK),
                (((0,), (0,)), ((), ())),
                preferred_element_type=jnp.float32,
            )
            total = part if total is None else total + part
        per_block = GRAD_BLOCK // LANES
        for c in range(per_block):
            lanes = total[:, c * LANES : (c + 1) * LANES]
            encode(lanes, h * per_block + c, message_ref, exponents_ref)
        return carry

    lax.fori_loop(0, hidden_count // GRAD_BLOCK, step, 0)
    encode_tail(message_ref, exponents_ref)


def grad_chunk(place, pieces, dzs, column, columns, deps):
    hidden_count = dzs[0].shape[2]
    return vmem_call(
        functools.partial(grad_body, [p[1:] for p in pieces], column, columns),
        place,
        [x for x, _, _ in pieces] + dzs,
        [message_of(columns, hidden_count)],
        "grad_chunk",
        deps,
        [EXPONENTS],
    )[0]


def add_body(count, place, a_ref, b_ref, out_ref, exponents_ref, a_steps, b_steps):
    rows = (out_ref.shape[0] - CODE_TAIL) // count
    decode_steps(a_ref, a_steps)
    decode_steps(b_ref, b_steps)
    exponents_ref[...] = jnp.zeros_like(exponents_ref)

    def step(i, carry):
        for j in range(ADD_BLOCKS):
            c = i * ADD_BLOCKS + j
            v = decode(a_ref, a_steps, c, rows) + decode(b_ref, b_steps, c, rows)
            encode(v, c, out_ref, exponents_ref)
        return carry

    lax.fori_loop(0, count // ADD_BLOCKS, step, 0)
    encode_tail(out_ref, exponents_ref)


def add_chunk(place, a, b, count, deps):
    return vmem_call(
        functools.partial(add_body, count),
        place,
        [a, b],
        [(a.shape, a.dtype)],
        "add_chunk",
        deps,
        [EXPONENTS] * 3,
    )[0]


def place_body(count, rows, of_own, index, place, total, received, *refs):
    out, token, held, steps, sem = refs[-5:]
    token[...] = jnp.zeros_like(token)
    half = place[0] if of_own else 1 - place[0]
    first = pl.multiple_of(half * (out.shape[0] // 2) + index * rows, rows)
    at_end = place[1] == 1

    def write(message):
        decode_steps(message, steps)
        for c in range(count):
            held[:, c * LANES : (c + 1) * LANES] = decode(message, steps, c, rows)

    @pl.when(at_end)
    def _():
        write(received)

    @pl.when(jnp.logical_not(at_end))
    def _():
        write(total)

    copy = pltpu.make_async_copy(held, out.at[pl.ds(first, rows)], sem)
    copy.start()
    copy.wait()


def place_chunk(place, total, received, result, of_own, index, rows, shape, deps):
    hidden_count = shape[1]
    earlier = [] if result is None else [result]
    operands = [total, received] + deps
    return pl.pallas_call(
        functools.partial(place_body, hidden_count // LANES, rows, of_own, index),
        in_specs=[SMEM]
        + [VMEM] * len(operands)
        + [pl.BlockSpec(memory_space=pl.ANY) for _ in earlier],
        out_specs=[pl.BlockSpec(memory_space=pl.ANY), VMEM],
        out_shape=[
            jax.ShapeDtypeStruct(shape, jnp.float32),
            pltpu.VMEM((8, LANES), jnp.float32),
        ],
        scratch_shapes=[
            pltpu.VMEM((rows, hidden_count), jnp.float32),
            EXPONENTS,
            pltpu.SemaphoreType.DMA(()),
        ],
        input_output_aliases={1 + len(operands): 0} if earlier else {},
        compiler_params=params(),
        cost_estimate=SHORT,
        name="place_chunk",
    )(place, *[resident(x) for x in operands], *earlier)


def pipeline_order(count, lead):
    order = [("grad", k) for k in range(min(lead, count))]
    ahead = len(order)
    for k in range(count + 2):
        if k < count:
            order.append(("partial", k))
            while ahead < min(count, lead + 2 * (k + 1)):
                order.append(("grad", ahead))
                ahead += 1
        if 0 <= k - 1 < count:
            order.append(("total", k - 1))
        if 0 <= k - 2 < count:
            order.append(("place", k - 2))
    return order


def after(array, *others):
    return lax.optimization_barrier((array,) + others)[0]


def line_plan(
    online_obs,
    offline_obs,
    online_rewards,
    offline_rewards,
    online_behaviour,
    offline_behaviour,
    online_actions,
    offline_actions,
    online_done,
    offline_done,
    online_lengths,
    offline_lengths,
    torso_weights,
    value_head,
    policy_head,
):
    section = lax.axis_index("section")
    m = lax.axis_index("mp")
    z = lax.axis_index("dp")
    dp = lax.axis_size("dp")
    steps, online_count, features = online_obs.shape
    offline_count, step_count, _ = offline_obs.shape
    action_count = policy_head.shape[1]
    hidden_count = value_head.shape[0]
    at_end = ((z == 0) | (z == dp - 1)).astype(jnp.int32)
    place = jnp.stack([m, at_end, z, section]).astype(jnp.int32)
    weight = torso_weights[0]
    scale = math.sqrt(
        hidden_count
        * lax.axis_size("mp")
        / ((online_count + offline_count * dp) * step_count)
    )

    offline_groups = offline_count // 2
    offline_rows = offline_obs.reshape(offline_groups, 2 * step_count, features)
    halves = [section_share(place, online_obs, [])]
    halves.append(section_share(place, offline_rows, [halves[0]]))

    policy_rows = jnp.where(section == 1, policy_head.T, 0)
    value_row = jnp.where(section == 0, value_head[None], 0)
    head = jnp.concatenate([policy_rows, value_row], axis=0).astype(jnp.bfloat16)
    head = jnp.pad(head, ((0, HEAD_ROWS - action_count - 1), (0, 0)))
    forward_head = jnp.pad(head, ((0, 32 - HEAD_ROWS), (0, 0)))
    back_head = jnp.concatenate([head, head, head, jnp.zeros_like(head)], axis=0)

    owned = online_lengths.shape[0]
    length_row = lax.dynamic_update_slice(
        jnp.zeros((online_count,), jnp.float32), online_lengths.astype(jnp.float32), (z * owned,)
    )
    length_row = length_row[None]
    lanes = (offline_groups, 2 * step_count)
    offline_length = jnp.broadcast_to(offline_lengths[:, None], (offline_count, step_count))
    offline_terms = [
        x.reshape(lanes)
        for x in (
            offline_actions,
            offline_behaviour,
            offline_rewards,
            offline_done,
            offline_length,
        )
    ]

    got = [lax.ppermute(half, "mp", SWAP) for half in halves]
    early = halves + [back_head, forward_head, length_row] + offline_terms
    own_online, pre_online = own_half(place, online_obs, weight, early)
    own_offline, pre_offline = own_half(place, offline_rows, weight, [pre_online])
    rests = [lax.ppermute(after(got[0], pre_offline), "section", SWAP)]
    online_slope, online_part = forward(
        place, pre_online, got[0], rests[0], weight, forward_head, []
    )
    both, share = vmem_call(
        chip_heads_body,
        place,
        [online_part, lax.ppermute(online_part, "section", SWAP)],
        [
            (online_part.shape, jnp.float32),
            ((steps // 2, HEAD_ROWS, online_count), jnp.float32),
        ],
        "chip_heads",
    )
    across_heads = lax.ppermute(share, "mp", SWAP)
    rests.append(lax.ppermute(after(got[1], both), "section", SWAP))
    offline_slope, offline_part = forward(
        place, pre_offline, got[1], rests[1], weight, forward_head, [both]
    )
    across_offline = lax.ppermute(offline_part, "mp", SWAP)
    offline_parts = [offline_part, lax.ppermute(offline_part, "section", SWAP), across_offline]
    far_heads = lax.ppermute(after(across_heads, offline_part), "section", SWAP)
    pack, spread = vmem_call(
        functools.partial(online_heads_body, action_count),
        place,
        [both, across_heads, far_heads]
        + [online_actions, online_behaviour, online_rewards, online_done, length_row],
        [
            ((4 * steps + 8, online_count), jnp.float32),
            ((steps, HEAD_ROWS, online_count), jnp.float32),
        ],
        "online_heads",
        [offline_part],
        [pltpu.VMEM((steps, HEAD_ROWS, online_count), jnp.float32)],
    )

    blocks = [pack]
    for hop in range(1, dp):
        pairs = [(i, (i - hop) % dp) for i in range(dp)]
        blocks.append(lax.ppermute(pack, "dp", pairs))
    offline_parts.append(lax.ppermute(after(across_offline, pack), "section", SWAP))
    (dz_offline,) = vmem_call(
        functools.partial(offline_back_body, action_count, step_count, scale),
        place,
        offline_parts + offline_terms + [back_head, offline_slope],
        [(offline_slope.shape, jnp.bfloat16)],
        "offline_back",
        [pack],
    )

    (dz_online,) = vmem_call(
        functools.partial(online_back_body, action_count, scale),
        place,
        blocks + [spread, back_head, online_slope],
        [(online_slope.shape, jnp.bfloat16)],
        "online_back",
        [dz_offline],
    )

    own_x = [(own_online, 0, None), (own_offline, 1, None)]
    other_x = []
    for which in range(2):
        other_x += [(got[which], which, 0), (rests[which], which, 1)]
    columns = 2 * features // GRAD_CHUNKS
    per_half = GRAD_CHUNKS // 2
    lane_blocks = hidden_count // LANES

    messages, inward, partial, across, total, outward = {}, {}, {}, {}, {}, {}
    result, last = None, dz_online
    for kind, k in pipeline_order(GRAD_CHUNKS, GRAD_LEAD):
        if kind == "grad":
            last = messages[k] = grad_chunk(
                place,
                own_x if k < per_half else other_x,
                [dz_online, dz_offline],
                k % per_half,
                columns,
                [last],
            )
            if k < SEND_LEAD:
                inward[k] = lax.ppermute(last, "dp", TO_CENTER)
        elif kind == "partial":
            last = partial[k] = add_chunk(place, messages[k], inward[k], lane_blocks, [last])
            across[k] = lax.ppermute(last, "dp", CENTER)
        elif kind == "total":
            last = total[k] = add_chunk(place, partial[k], across[k], lane_blocks, [last])
            outward[k] = lax.ppermute(last, "dp", FROM_CENTER)
            ahead = k + SEND_LEAD
            if ahead < GRAD_CHUNKS:
                inward[ahead] = lax.ppermute(after(messages[ahead], last), "dp", TO_CENTER)
        else:
            result, last = place_chunk(
                place,
                total[k],
                outward[k],
                result,
                k < per_half,
                k % per_half,
                columns,
                (2 * features, hidden_count),
                [last],
            )
    return result[None]


def solution(mesh):
    on_line = mesh.shape["dp"] == 4 and mesh.shape["mp"] == 2 and mesh.shape["section"] == 2
    in_specs = (
        P("dp", "groups", "mp"),
        P(("groups", "dp"), None, "mp"),
        P("dp", "groups"),
        P(("groups", "dp"), None),
        P("dp", "groups"),
        P(("groups", "dp"), None),
        P("dp", "groups"),
        P(("groups", "dp"), None),
        P("dp", "groups"),
        P(("groups", "dp"), None),
        P(("groups", "dp")),
        P(("groups", "dp")),
        P("section", None, "mp"),
        P("mp"),
        P("mp", None),
    )
    out_specs = P(("groups", "section"), None, "mp")
    per_device = line_plan if on_line else general_plan
    return jax.shard_map(
        per_device, mesh=mesh, in_specs=in_specs, out_specs=out_specs, check_vma=False
    )
```

```python
import functools
import math

import jax
import jax.numpy as jnp
from jax import lax
from jax.experimental import pallas as pl
from jax.experimental.pallas import tpu as pltpu
from jax.sharding import PartitionSpec as P

DISCOUNT_RATE = 0.99
TRACE_LAMBDA = 0.95


def silu_slope(pre):
    sigma = jax.nn.sigmoid(pre)
    return sigma * (1.0 + pre * (1.0 - sigma))


def importance_trace_terms(
    value_estimates,
    policy_logits,
    reward_rows,
    behaviour_probs,
    taken_actions,
    episode_finished,
    sequence_length,
    objective_scale,
):
    seq_count, step_count = value_estimates.shape
    action_count = policy_logits.shape[0]
    positions = jnp.arange(step_count, dtype=jnp.int32)
    valid_mask = (positions[None, :] < sequence_length[:, None]).astype(jnp.float32)
    zero_column = jnp.zeros((seq_count, 1), jnp.float32)
    valid_next = jnp.concatenate([valid_mask[:, 1:], zero_column], axis=1)
    log_probs = jax.nn.log_softmax(policy_logits, axis=0)
    one_hot = (
        jnp.arange(action_count, dtype=jnp.int32)[:, None, None] == taken_actions[None]
    ).astype(jnp.float32)
    chosen = jnp.sum(one_hot * log_probs, axis=0)
    clip_ratio = jnp.exp(jnp.minimum(chosen - behaviour_probs, 0.0))
    discount = DISCOUNT_RATE * (1.0 - episode_finished.astype(jnp.float32))
    next_value = jnp.concatenate([value_estimates[:, 1:], zero_column], axis=1) * valid_next
    td_error = valid_mask * clip_ratio * (reward_rows + discount * next_value - value_estimates)
    trace_coef = discount * TRACE_LAMBDA * clip_ratio * valid_next

    def backward_step(carried, inputs):
        error_now, coef_now = inputs
        updated = error_now + coef_now * carried
        return (updated, updated)

    final_state, stacked = lax.scan(
        backward_step,
        jnp.zeros((seq_count,), jnp.float32),
        (td_error.T, trace_coef.T),
        reverse=True,
    )
    correction = stacked.T
    targets = value_estimates + correction
    next_target = jnp.concatenate([targets[:, 1:], zero_column], axis=1) * valid_next
    policy_adv = clip_ratio * (reward_rows + discount * next_target - value_estimates)
    value_gradient = -objective_scale * valid_mask * correction
    logits_gradient = (
        objective_scale * (valid_mask * policy_adv)[None] * (jnp.exp(log_probs) - one_hot)
    )
    return (value_gradient, logits_gradient)


def head_terms(hidden, value_w, policy_w):
    logit_part = jnp.einsum("rh,ha->ar", hidden, policy_w, preferred_element_type=jnp.float32)
    value_part = jnp.dot(hidden, value_w, preferred_element_type=jnp.float32)
    return jnp.concatenate([logit_part, value_part[None]], axis=0)


def full_rows(online_part, offline_part):
    return (
        lax.all_gather(online_part, "mp", axis=2, tiled=True),
        lax.all_gather(offline_part, "mp", axis=2, tiled=True),
    )


def general_plan(
    online_obs,
    offline_obs,
    online_rewards,
    offline_rewards,
    online_behaviour,
    offline_behaviour,
    online_actions,
    offline_actions,
    online_done,
    offline_done,
    online_lengths,
    offline_lengths,
    torso_weights,
    value_head,
    policy_head,
):
    owned_online = online_lengths.shape[0]
    owned_offline = offline_obs.shape[0]
    step_count = offline_obs.shape[1]
    action_count = policy_head.shape[1]
    record_stack = jnp.stack(
        [
            online_rewards,
            online_behaviour,
            online_actions.astype(jnp.float32),
            online_done.astype(jnp.float32),
        ]
    )
    records = lax.all_to_all(record_stack, "dp", split_axis=2, concat_axis=1, tiled=True)
    slabs = lax.all_to_all(online_obs, "dp", split_axis=1, concat_axis=0, tiled=True)
    x_online, x_offline = full_rows(slabs, offline_obs)
    feature_count = x_online.shape[2]
    x_online = x_online.reshape(step_count * owned_online, feature_count)
    x_offline = x_offline.reshape(owned_offline * step_count, feature_count)
    weight = torso_weights[0]
    pre_online = jnp.dot(x_online, weight, preferred_element_type=jnp.float32)
    pre_offline = jnp.dot(x_offline, weight, preferred_element_type=jnp.float32)
    hidden_online = jax.nn.silu(pre_online).astype(jnp.bfloat16)
    hidden_offline = jax.nn.silu(pre_offline).astype(jnp.bfloat16)
    is_critic = (lax.axis_index("section") == 0).astype(jnp.float32)
    is_policy = 1.0 - is_critic
    row_keep = jnp.where(jnp.arange(action_count + 1) == action_count, is_critic, is_policy)
    partial_value = jnp.concatenate(
        [
            head_terms(hidden_online, value_head, policy_head),
            head_terms(hidden_offline, value_head, policy_head),
        ],
        axis=1,
    )
    partial_value = partial_value * row_keep[:, None]
    heads = lax.psum(partial_value, ("mp", "section"))
    online_count = step_count * owned_online
    logits_on = (
        heads[:action_count, :online_count]
        .reshape(action_count, step_count, owned_online)
        .transpose(0, 2, 1)
    )
    logits_off = heads[:action_count, online_count:].reshape(
        action_count, owned_offline, step_count
    )
    values_on = heads[action_count, :online_count].reshape(step_count, owned_online).T
    values_off = heads[action_count, online_count:].reshape(owned_offline, step_count)
    record_seq = records.transpose(0, 2, 1)
    value_estimates = jnp.concatenate([values_on, values_off], axis=0)
    policy_logits = jnp.concatenate([logits_on, logits_off], axis=1)
    reward_rows = jnp.concatenate([record_seq[0], offline_rewards], axis=0)
    behaviour_probs = jnp.concatenate([record_seq[1], offline_behaviour], axis=0)
    taken_actions = jnp.concatenate([record_seq[2].astype(jnp.int32), offline_actions], axis=0)
    episode_finished = jnp.concatenate([record_seq[3].astype(jnp.int32), offline_done], axis=0)
    sequence_length = jnp.concatenate([online_lengths, offline_lengths], axis=0)
    total_seqs = online_obs.shape[1] + owned_offline * lax.axis_size("dp")
    hidden_total = value_head.shape[0] * lax.axis_size("mp")
    objective_scale = math.sqrt(hidden_total / (total_seqs * step_count))
    value_gradient, logits_gradient = importance_trace_terms(
        value_estimates,
        policy_logits,
        reward_rows,
        behaviour_probs,
        taken_actions,
        episode_finished,
        sequence_length,
        objective_scale,
    )
    value_gradient = value_gradient * is_critic
    logits_gradient = logits_gradient * is_policy
    dv_on = value_gradient[:owned_online].T.reshape(online_count)
    dv_off = value_gradient[owned_online:].reshape(owned_offline * step_count)
    dl_on = logits_gradient[:, :owned_online].transpose(0, 2, 1).reshape(action_count, online_count)
    dl_off = logits_gradient[:, owned_online:].reshape(action_count, owned_offline * step_count)
    value_w = value_head.astype(jnp.float32)
    policy_w = policy_head.astype(jnp.float32)
    dh_on = dv_on[:, None] * value_w[None, :] + jnp.einsum(
        "ar,ha->rh", dl_on, policy_w, precision=lax.Precision.HIGHEST
    )
    dh_off = dv_off[:, None] * value_w[None, :] + jnp.einsum(
        "ar,ha->rh", dl_off, policy_w, precision=lax.Precision.HIGHEST
    )
    dz_online = (dh_on * silu_slope(pre_online)).astype(jnp.bfloat16)
    dz_offline = (dh_off * silu_slope(pre_offline)).astype(jnp.bfloat16)
    local_grad = jnp.einsum("rd,rh->dh", x_online, dz_online, preferred_element_type=jnp.float32)
    local_grad = local_grad + jnp.einsum(
        "rd,rh->dh", x_offline, dz_offline, preferred_element_type=jnp.float32
    )
    summed = lax.psum(local_grad, "dp")
    return summed[None]


HEAD_ROWS = 24
SPLIT_ROWS = 4 * HEAD_ROWS
COLUMN_BLOCK = 256
GRAD_BLOCK = 512
ADD_BLOCKS = 2
ROW_GROUPS = 4
GRAD_CHUNKS = 8
GRAD_LEAD = 7
SEND_LEAD = 3
LANES = 128
CODE_LIMIT = 32512.0
CODE_TAIL = 16
LOG_TWO = math.log(2.0)
SCRATCH_BYTES = 6 * 1024 * 1024
SWAP = ((0, 1), (1, 0))
TO_CENTER = ((0, 1), (3, 2))
CENTER = ((1, 2), (2, 1))
FROM_CENTER = ((1, 0), (2, 3))
VMEM = pl.BlockSpec(memory_space=pltpu.VMEM)
HBM = pl.BlockSpec(memory_space=pltpu.HBM)
SMEM = pl.BlockSpec(memory_space=pltpu.SMEM)
EXPONENTS = pltpu.VMEM((CODE_TAIL, LANES), jnp.float32)


SHORT = pl.CostEstimate(flops=1, bytes_accessed=1, transcendentals=0)


def params():
    return pltpu.CompilerParams(vmem_limit_bytes=SCRATCH_BYTES)


def resident(array):
    return pltpu.with_memory_space_constraint(array, pltpu.VMEM)


def vmem_call(body, place, arrays, outs, name, deps=(), scratch=()):
    operands = list(arrays) + list(deps)

    def run(place_ref, *refs):
        body(place_ref, *refs[: len(arrays)], *refs[len(operands) :])

    return pl.pallas_call(
        run,
        in_specs=[SMEM] + [VMEM] * len(operands),
        out_specs=[VMEM] * len(outs),
        out_shape=[pltpu.VMEM(shape, dtype) for shape, dtype in outs],
        scratch_shapes=list(scratch),
        compiler_params=params(),
        cost_estimate=SHORT,
        name=name,
    )(place, *[resident(x) for x in operands])


def in_hbm(array):
    return pltpu.with_memory_space_constraint(array, pltpu.HBM)


def share_body(place, source, *refs):
    out, sem = refs[-2:]
    count = out.shape[0]
    copy = pltpu.make_async_copy(source.at[pl.ds(place[3] * count, count)], out, sem)
    copy.start()
    copy.wait()


def section_share(place, source, deps):
    groups, width, features = source.shape
    return pl.pallas_call(
        share_body,
        in_specs=[SMEM, HBM] + [VMEM] * len(deps),
        out_specs=VMEM,
        out_shape=pltpu.VMEM((groups // 2, width, features), source.dtype),
        scratch_shapes=[pltpu.SemaphoreType.DMA(())],
        compiler_params=params(),
        cost_estimate=SHORT,
        name="section_share",
    )(place, in_hbm(source), *[resident(x) for x in deps])


def own_half_body(place, source, weight_ref, *refs):
    own_ref, out_ref, sem = refs[-3:]
    groups, width, features = own_ref.shape
    copy = pltpu.make_async_copy(source, own_ref, sem)
    copy.start()
    copy.wait()
    at = pl.multiple_of(place[0] * features, features)
    for first in range(0, groups, ROW_GROUPS):
        part = slice(first, first + ROW_GROUPS)

        def step(h, carry, part=part):
            block = pl.ds(pl.multiple_of(h * COLUMN_BLOCK, COLUMN_BLOCK), COLUMN_BLOCK)
            pre = jnp.dot(
                own_ref[part].reshape(-1, features),
                weight_ref[pl.ds(at, features), block],
                preferred_element_type=jnp.float32,
            )
            out_ref[part, :, block] = pre.reshape(-1, width, COLUMN_BLOCK)
            return carry

        lax.fori_loop(0, weight_ref.shape[1] // COLUMN_BLOCK, step, 0)


def own_half(place, source, weight, deps):
    groups, width, _ = source.shape
    operands = [weight] + deps
    return pl.pallas_call(
        own_half_body,
        in_specs=[SMEM, HBM] + [VMEM] * len(operands),
        out_specs=[VMEM, VMEM],
        out_shape=[
            pltpu.VMEM(source.shape, source.dtype),
            pltpu.VMEM((groups, width, weight.shape[1]), jnp.float32),
        ],
        scratch_shapes=[pltpu.SemaphoreType.DMA(())],
        compiler_params=params(),
        cost_estimate=SHORT,
        name="own_half",
    )(place, in_hbm(source), *[resident(x) for x in operands])


def forward_body(place, pre_ref, got_ref, rest_ref, weight_ref, head_ref, *refs):
    slope_ref, heads_ref, hidden_ref = refs[-3:]
    half, width, features = got_ref.shape
    hidden_count = weight_ref.shape[1]
    m, section = place[0], place[3]
    other_at = pl.multiple_of((1 - m) * features, features)
    count = min(half, ROW_GROUPS)
    for x_ref, start in ((got_ref, section * half), (rest_ref, (1 - section) * half)):
        for first in range(0, half, count):
            at = pl.ds(start + first, count)
            other = x_ref[first : first + count].reshape(-1, features)
            for h in range(0, hidden_count, COLUMN_BLOCK):
                block = slice(h, h + COLUMN_BLOCK)
                pre = jnp.dot(
                    other,
                    weight_ref[pl.ds(other_at, features), block],
                    preferred_element_type=jnp.float32,
                )
                pre = pre + pre_ref[at, :, block].reshape(-1, COLUMN_BLOCK)
                sigma = 0.5 * jnp.tanh(0.5 * pre) + 0.5
                hidden = pre * sigma
                slope = sigma + hidden * (1.0 - sigma)
                slope_ref[at, :, block] = slope.reshape(-1, width, COLUMN_BLOCK)
                hidden_ref[:, block] = hidden.astype(jnp.bfloat16)
            for g in range(count):
                heads = lax.dot_general(
                    head_ref[...],
                    hidden_ref[g * width : (g + 1) * width],
                    (((1,), (1,)), ((), ())),
                    preferred_element_type=jnp.float32,
                )
                heads_ref[start + first + g] = heads[:HEAD_ROWS]


def forward(place, pre, got, rest, weight, head, deps):
    groups, width, hidden_count = pre.shape
    operands = [pre, got, rest, weight, head] + deps
    return pl.pallas_call(
        forward_body,
        in_specs=[SMEM] + [VMEM] * len(operands),
        out_specs=[VMEM, VMEM],
        out_shape=[
            pltpu.VMEM(pre.shape, jnp.float32),
            pltpu.VMEM((groups, HEAD_ROWS, width), jnp.float32),
        ],
        scratch_shapes=[
            pltpu.VMEM((min(groups // 2, ROW_GROUPS) * width, hidden_count), jnp.bfloat16)
        ],
        input_output_aliases={1: 0},
        compiler_params=params(),
        cost_estimate=SHORT,
        name="forward_rows",
    )(place, *[resident(x) for x in operands])


def action_terms(parts, actions, behaviour, action_count):
    heads = sum(parts[1:], start=parts[0])
    row = lax.broadcasted_iota(jnp.int32, heads.shape, 0)
    is_logit = row < action_count
    logits = jnp.where(is_logit, heads, -1e30)
    shifted = logits - jnp.max(logits, axis=0, keepdims=True)
    log_sum = jnp.log(jnp.sum(jnp.exp(shifted), axis=0, keepdims=True))
    log_probs = shifted - log_sum
    taken = row == actions
    chosen = jnp.sum(jnp.where(taken, log_probs, 0.0), axis=0, keepdims=True)
    rho = jnp.exp(jnp.minimum(chosen - behaviour, 0.0))
    spread = jnp.where(is_logit, jnp.exp(log_probs) - taken.astype(jnp.float32), 0.0)
    return heads[action_count : action_count + 1], rho, spread


def trace_terms(value, rho, reward, discount, length, position, axis, reach, scale):
    size = value.shape[axis]
    valid = (position < length).astype(jnp.float32)
    valid_next = (position + 1 < length).astype(jnp.float32)
    next_value = pltpu.roll(value, size - 1, axis) * valid_next
    correction = valid * rho * (reward + discount * next_value - value)
    coef = discount * TRACE_LAMBDA * rho * valid_next
    shift = 1
    while shift < reach:
        correction = correction + coef * pltpu.roll(correction, size - shift, axis)
        coef = coef * pltpu.roll(coef, size - shift, axis)
        shift *= 2
    targets = value + correction
    next_target = pltpu.roll(targets, size - 1, axis) * valid_next
    advantage = rho * (reward + discount * next_target - value)
    return -scale * valid * correction, scale * (valid * advantage)


def split_terms(logit_weight, value_weight, spread, action_count):
    row = lax.broadcasted_iota(jnp.int32, spread.shape, 0)
    full = jnp.where(row == action_count, value_weight, logit_weight * spread)
    high = full.astype(jnp.bfloat16).astype(jnp.float32)
    rest = full - high
    middle = rest.astype(jnp.bfloat16).astype(jnp.float32)
    low = rest - middle
    return jnp.concatenate([high, middle, low, jnp.zeros_like(full)], axis=0).astype(jnp.bfloat16)


def write_back(terms, head_ref, slope, dz_ref, g):
    dh = lax.dot_general(
        terms, head_ref[...], (((0,), (0,)), ((), ())), preferred_element_type=jnp.float32
    )
    dz_ref[g] = (dh * slope).astype(jnp.bfloat16)


def chip_heads_body(place, own, other, both_ref, share_ref):
    both_ref[...] = own[...] + other[...]
    count = share_ref.shape[0]
    share_ref[...] = both_ref[pl.ds(place[3] * count, count)]


def online_heads_body(action_count, place, *refs):
    both, across, far, actions, behaviour, reward, done, lengths = refs[:8]
    pack_ref, spread_ref, other = refs[8:]
    steps = actions.shape[0]
    half, section = steps // 2, place[3]
    other[pl.ds(section * half, half)] = across[...]
    other[pl.ds((1 - section) * half, half)] = far[...]
    for t in range(steps):
        value, rho, spread = action_terms(
            [both[t], other[t]],
            actions[t : t + 1, :],
            behaviour[t : t + 1, :],
            action_count,
        )
        pack_ref[t : t + 1, :] = value
        pack_ref[steps + t : steps + t + 1, :] = rho
        spread_ref[t] = spread
    pack_ref[2 * steps : 3 * steps, :] = reward[...]
    pack_ref[3 * steps : 4 * steps, :] = DISCOUNT_RATE * (1.0 - done[...].astype(jnp.float32))
    pack_ref[4 * steps :, :] = jnp.broadcast_to(lengths[...], (8, lengths.shape[1]))


def online_back_body(action_count, scale, place, *refs):
    blocks, spread, head_ref, slope_ref, dz_ref = refs[:4], *refs[4:]
    steps = spread.shape[0]
    z = place[2]

    def field(i):
        parts = []
        for hop, b in enumerate(blocks):
            part = b[i * steps : (i + 1) * steps, :]
            parts.append(jnp.where(z + hop < len(blocks), part, 0.0) if hop else part)
        return jnp.concatenate(parts, axis=0)

    length = sum(b[4 * steps : 4 * steps + 1, :] for b in blocks).astype(jnp.int32)
    value = field(0)
    position = lax.broadcasted_iota(jnp.int32, value.shape, 0) + z * steps
    value_weight, logit_weight = trace_terms(
        value,
        field(1),
        field(2),
        field(3),
        length,
        position,
        0,
        value.shape[0],
        scale,
    )
    for t in range(steps):
        terms = split_terms(
            logit_weight[t : t + 1, :], value_weight[t : t + 1, :], spread[t], action_count
        )
        write_back(terms, head_ref, slope_ref[t], dz_ref, t)


def offline_back_body(action_count, step_count, scale, place, *refs):
    parts = refs[:4]
    actions, behaviour, reward, done, length, head_ref, slope_ref, dz_ref = refs[4:]
    groups = dz_ref.shape[0]
    values, rhos, spreads = [], [], []
    for g in range(groups):
        value, rho, spread = action_terms(
            [p[g] for p in parts],
            actions[g : g + 1, :],
            behaviour[g : g + 1, :],
            action_count,
        )
        values.append(value)
        rhos.append(rho)
        spreads.append(spread)
    value = jnp.concatenate(values, axis=0)
    rho = jnp.concatenate(rhos, axis=0)
    position = lax.rem(lax.broadcasted_iota(jnp.int32, value.shape, 1), step_count)
    discount = DISCOUNT_RATE * (1.0 - done[...].astype(jnp.float32))
    value_weight, logit_weight = trace_terms(
        value, rho, reward[...], discount, length[...], position, 1, step_count, scale
    )
    for g in range(groups):
        terms = split_terms(
            logit_weight[g : g + 1, :], value_weight[g : g + 1, :], spreads[g], action_count
        )
        write_back(terms, head_ref, slope_ref[g], dz_ref, g)


def encode(v, c, message_ref, exponents_ref):
    rows = v.shape[0]
    largest = jnp.max(jnp.abs(v), axis=0, keepdims=True)
    exponent = jnp.ceil(jnp.log(jnp.maximum(largest, 1e-30)) * (1.0 / LOG_TWO) + 0.01)
    scale = jnp.exp(exponent * -LOG_TWO) * CODE_LIMIT
    code = jnp.floor(v * scale + 0.5)
    at = pl.ds(pl.multiple_of(c * rows, rows), rows)
    message_ref[at, :] = code.astype(jnp.int32).astype(jnp.int16)
    exponents_ref[pl.ds(c, 1), :] = exponent


def encode_tail(message_ref, exponents_ref):
    tail = exponents_ref[...].astype(jnp.int32)
    message_ref[message_ref.shape[0] - CODE_TAIL :, :] = tail.astype(jnp.int16)


def decode_steps(message_ref, steps_ref):
    exponents = message_ref[message_ref.shape[0] - CODE_TAIL :, :]
    exponents = exponents.astype(jnp.int32).astype(jnp.float32)
    steps_ref[...] = jnp.exp(exponents * LOG_TWO) * (1.0 / CODE_LIMIT)


def decode(message_ref, steps_ref, c, rows):
    at = pl.ds(pl.multiple_of(c * rows, rows), rows)
    code = message_ref[at, :].astype(jnp.int32).astype(jnp.float32)
    return code * steps_ref[pl.ds(c, 1), :]


def message_of(rows, columns):
    return ((rows * (columns // LANES) + CODE_TAIL, LANES), jnp.int16)


def grad_body(pieces, column, columns, place, *refs):
    xs, dzs = refs[: len(pieces)], refs[len(pieces) : len(pieces) + 2]
    message_ref, exponents_ref = refs[-2:]
    hidden_count = dzs[0].shape[2]
    section = place[3]
    at = slice(column * columns, (column + 1) * columns)
    exponents_ref[...] = jnp.zeros_like(exponents_ref)

    def step(h, carry):
        block = pl.ds(pl.multiple_of(h * GRAD_BLOCK, GRAD_BLOCK), GRAD_BLOCK)
        total = None
        for x, (which, swapped) in zip(xs, pieces):
            groups, width, _ = x.shape
            first = 0
            if swapped is not None:
                first = (1 - section if swapped else section) * groups
            part = lax.dot_general(
                x[:, :, at].reshape(groups * width, columns),
                dzs[which][pl.ds(first, groups), :, block].reshape(groups * width, GRAD_BLOCK),
                (((0,), (0,)), ((), ())),
                preferred_element_type=jnp.float32,
            )
            total = part if total is None else total + part
        per_block = GRAD_BLOCK // LANES
        for c in range(per_block):
            lanes = total[:, c * LANES : (c + 1) * LANES]
            encode(lanes, h * per_block + c, message_ref, exponents_ref)
        return carry

    lax.fori_loop(0, hidden_count // GRAD_BLOCK, step, 0)
    encode_tail(message_ref, exponents_ref)


def grad_chunk(place, pieces, dzs, column, columns, deps):
    hidden_count = dzs[0].shape[2]
    return vmem_call(
        functools.partial(grad_body, [p[1:] for p in pieces], column, columns),
        place,
        [x for x, _, _ in pieces] + dzs,
        [message_of(columns, hidden_count)],
        "grad_chunk",
        deps,
        [EXPONENTS],
    )[0]


def add_body(count, place, a_ref, b_ref, out_ref, exponents_ref, a_steps, b_steps):
    rows = (out_ref.shape[0] - CODE_TAIL) // count
    decode_steps(a_ref, a_steps)
    decode_steps(b_ref, b_steps)
    exponents_ref[...] = jnp.zeros_like(exponents_ref)

    def step(i, carry):
        for j in range(ADD_BLOCKS):
            c = i * ADD_BLOCKS + j
            v = decode(a_ref, a_steps, c, rows) + decode(b_ref, b_steps, c, rows)
            encode(v, c, out_ref, exponents_ref)
        return carry

    lax.fori_loop(0, count // ADD_BLOCKS, step, 0)
    encode_tail(out_ref, exponents_ref)


def add_chunk(place, a, b, count, deps):
    return vmem_call(
        functools.partial(add_body, count),
        place,
        [a, b],
        [(a.shape, a.dtype)],
        "add_chunk",
        deps,
        [EXPONENTS] * 3,
    )[0]


def place_body(count, rows, of_own, index, place, total, received, *refs):
    out, token, held, steps, sem = refs[-5:]
    token[...] = jnp.zeros_like(token)
    half = place[0] if of_own else 1 - place[0]
    first = pl.multiple_of(half * (out.shape[0] // 2) + index * rows, rows)
    at_end = place[1] == 1

    def write(message):
        decode_steps(message, steps)
        for c in range(count):
            held[:, c * LANES : (c + 1) * LANES] = decode(message, steps, c, rows)

    @pl.when(at_end)
    def _():
        write(received)

    @pl.when(jnp.logical_not(at_end))
    def _():
        write(total)

    copy = pltpu.make_async_copy(held, out.at[pl.ds(first, rows)], sem)
    copy.start()
    copy.wait()


def place_chunk(place, total, received, result, of_own, index, rows, shape, deps):
    hidden_count = shape[1]
    earlier = [] if result is None else [result]
    operands = [total, received] + deps
    return pl.pallas_call(
        functools.partial(place_body, hidden_count // LANES, rows, of_own, index),
        in_specs=[SMEM]
        + [VMEM] * len(operands)
        + [pl.BlockSpec(memory_space=pl.ANY) for _ in earlier],
        out_specs=[pl.BlockSpec(memory_space=pl.ANY), VMEM],
        out_shape=[
            jax.ShapeDtypeStruct(shape, jnp.float32),
            pltpu.VMEM((8, LANES), jnp.float32),
        ],
        scratch_shapes=[
            pltpu.VMEM((rows, hidden_count), jnp.float32),
            EXPONENTS,
            pltpu.SemaphoreType.DMA(()),
        ],
        input_output_aliases={1 + len(operands): 0} if earlier else {},
        compiler_params=params(),
        cost_estimate=SHORT,
        name="place_chunk",
    )(place, *[resident(x) for x in operands], *earlier)


def pipeline_order(count, lead):
    order = [("grad", k) for k in range(min(lead, count))]
    ahead = len(order)
    for k in range(count + 2):
        if k < count:
            order.append(("partial", k))
            while ahead < min(count, lead + 2 * (k + 1)):
                order.append(("grad", ahead))
                ahead += 1
        if 0 <= k - 1 < count:
            order.append(("total", k - 1))
        if 0 <= k - 2 < count:
            order.append(("place", k - 2))
    return order


def after(array, *others):
    return lax.optimization_barrier((array,) + others)[0]


def line_plan(
    online_obs,
    offline_obs,
    online_rewards,
    offline_rewards,
    online_behaviour,
    offline_behaviour,
    online_actions,
    offline_actions,
    online_done,
    offline_done,
    online_lengths,
    offline_lengths,
    torso_weights,
    value_head,
    policy_head,
):
    section = lax.axis_index("section")
    m = lax.axis_index("mp")
    z = lax.axis_index("dp")
    dp = lax.axis_size("dp")
    steps, online_count, features = online_obs.shape
    offline_count, step_count, _ = offline_obs.shape
    action_count = policy_head.shape[1]
    hidden_count = value_head.shape[0]
    at_end = ((z == 0) | (z == dp - 1)).astype(jnp.int32)
    place = jnp.stack([m, at_end, z, section]).astype(jnp.int32)
    weight = torso_weights[0]
    scale = math.sqrt(
        hidden_count
        * lax.axis_size("mp")
        / ((online_count + offline_count * dp) * step_count)
    )

    offline_groups = offline_count // 2
    offline_rows = offline_obs.reshape(offline_groups, 2 * step_count, features)
    halves = [section_share(place, online_obs, [])]
    halves.append(section_share(place, offline_rows, [halves[0]]))

    policy_rows = jnp.where(section == 1, policy_head.T, 0)
    value_row = jnp.where(section == 0, value_head[None], 0)
    head = jnp.concatenate([policy_rows, value_row], axis=0).astype(jnp.bfloat16)
    head = jnp.pad(head, ((0, HEAD_ROWS - action_count - 1), (0, 0)))
    forward_head = jnp.pad(head, ((0, 32 - HEAD_ROWS), (0, 0)))
    back_head = jnp.concatenate([head, head, head, jnp.zeros_like(head)], axis=0)

    owned = online_lengths.shape[0]
    length_row = lax.dynamic_update_slice(
        jnp.zeros((online_count,), jnp.float32), online_lengths.astype(jnp.float32), (z * owned,)
    )
    length_row = length_row[None]
    lanes = (offline_groups, 2 * step_count)
    offline_length = jnp.broadcast_to(offline_lengths[:, None], (offline_count, step_count))
    offline_terms = [
        x.reshape(lanes)
        for x in (
            offline_actions,
            offline_behaviour,
            offline_rewards,
            offline_done,
            offline_length,
        )
    ]

    got = [lax.ppermute(half, "mp", SWAP) for half in halves]
    early = halves + [back_head, forward_head, length_row] + offline_terms
    own_online, pre_online = own_half(place, online_obs, weight, early)
    own_offline, pre_offline = own_half(place, offline_rows, weight, [pre_online])
    rests = [lax.ppermute(after(got[0], pre_offline), "section", SWAP)]
    online_slope, online_part = forward(
        place, pre_online, got[0], rests[0], weight, forward_head, []
    )
    both, share = vmem_call(
        chip_heads_body,
        place,
        [online_part, lax.ppermute(online_part, "section", SWAP)],
        [
            (online_part.shape, jnp.float32),
            ((steps // 2, HEAD_ROWS, online_count), jnp.float32),
        ],
        "chip_heads",
    )
    across_heads = lax.ppermute(share, "mp", SWAP)
    rests.append(lax.ppermute(after(got[1], both), "section", SWAP))
    offline_slope, offline_part = forward(
        place, pre_offline, got[1], rests[1], weight, forward_head, [both]
    )
    across_offline = lax.ppermute(offline_part, "mp", SWAP)
    offline_parts = [offline_part, lax.ppermute(offline_part, "section", SWAP), across_offline]
    far_heads = lax.ppermute(after(across_heads, offline_part), "section", SWAP)
    pack, spread = vmem_call(
        functools.partial(online_heads_body, action_count),
        place,
        [both, across_heads, far_heads]
        + [online_actions, online_behaviour, online_rewards, online_done, length_row],
        [
            ((4 * steps + 8, online_count), jnp.float32),
            ((steps, HEAD_ROWS, online_count), jnp.float32),
        ],
        "online_heads",
        [offline_part],
        [pltpu.VMEM((steps, HEAD_ROWS, online_count), jnp.float32)],
    )

    blocks = [pack]
    for hop in range(1, dp):
        pairs = [(i, (i - hop) % dp) for i in range(dp)]
        blocks.append(lax.ppermute(pack, "dp", pairs))
    offline_parts.append(lax.ppermute(after(across_offline, pack), "section", SWAP))
    (dz_offline,) = vmem_call(
        functools.partial(offline_back_body, action_count, step_count, scale),
        place,
        offline_parts + offline_terms + [back_head, offline_slope],
        [(offline_slope.shape, jnp.bfloat16)],
        "offline_back",
        [pack],
    )

    (dz_online,) = vmem_call(
        functools.partial(online_back_body, action_count, scale),
        place,
        blocks + [spread, back_head, online_slope],
        [(online_slope.shape, jnp.bfloat16)],
        "online_back",
        [dz_offline],
    )

    own_x = [(own_online, 0, None), (own_offline, 1, None)]
    other_x = []
    for which in range(2):
        other_x += [(got[which], which, 0), (rests[which], which, 1)]
    columns = 2 * features // GRAD_CHUNKS
    per_half = GRAD_CHUNKS // 2
    lane_blocks = hidden_count // LANES

    messages, inward, partial, across, total, outward = {}, {}, {}, {}, {}, {}
    result, last = None, dz_online
    for kind, k in pipeline_order(GRAD_CHUNKS, GRAD_LEAD):
        if kind == "grad":
            last = messages[k] = grad_chunk(
                place,
                own_x if k < per_half else other_x,
                [dz_online, dz_offline],
                k % per_half,
                columns,
                [last],
            )
            if k < SEND_LEAD:
                inward[k] = lax.ppermute(last, "dp", TO_CENTER)
        elif kind == "partial":
            last = partial[k] = add_chunk(place, messages[k], inward[k], lane_blocks, [last])
            across[k] = lax.ppermute(last, "dp", CENTER)
        elif kind == "total":
            last = total[k] = add_chunk(place, partial[k], across[k], lane_blocks, [last])
            outward[k] = lax.ppermute(last, "dp", FROM_CENTER)
            ahead = k + SEND_LEAD
            if ahead < GRAD_CHUNKS:
                inward[ahead] = lax.ppermute(after(messages[ahead], last), "dp", TO_CENTER)
        else:
            result, last = place_chunk(
                place,
                total[k],
                outward[k],
                result,
                k < per_half,
                k % per_half,
                columns,
                (2 * features, hidden_count),
                [last],
            )
    return result[None]


def solution(mesh):
    on_line = mesh.shape["dp"] == 4 and mesh.shape["mp"] == 2 and mesh.shape["section"] == 2
    in_specs = (
        P("dp", "groups", "mp"),
        P(("groups", "dp"), None, "mp"),
        P("dp", "groups"),
        P(("groups", "dp"), None),
        P("dp", "groups"),
        P(("groups", "dp"), None),
        P("dp", "groups"),
        P(("groups", "dp"), None),
        P("dp", "groups"),
        P(("groups", "dp"), None),
        P(("groups", "dp")),
        P(("groups", "dp")),
        P("section", None, "mp"),
        P("mp"),
        P("mp", None),
    )
    out_specs = P(("groups", "section"), None, "mp")
    per_device = line_plan if on_line else general_plan
    return jax.shard_map(
        per_device, mesh=mesh, in_specs=in_specs, out_specs=out_specs, check_vma=False
    )
```
